32 devices in a mesh: replica: 4 (over y, x), fsdp: 8 (over z, core).
Axes of the slice: x: 2, y: 2, z: 4, core: 2. Of those that a mesh axis runs over, the one named last changes fastest.
Arguments:
- tokens: bfloat16 [32768, 1280], P(('replica', 'fsdp')), may hold values from -6 to 6
- lengths: int32 [32], P(('replica', 'fsdp')), may hold values from 256 to 1024, as said below
- cotangent: bfloat16 [32768, 1280], P(('replica', 'fsdp')), may hold values from -6 to 6
- query_weight: bfloat16 [1280, 1280], P('fsdp'), may hold values from -0.15625 to 0.15625
- key_weight: bfloat16 [1280, 1280], P('fsdp'), may hold values from -0.15625 to 0.15625
- value_weight: bfloat16 [1280, 1280], P('fsdp'), may hold values from -0.15625 to 0.15625
- output_weight: bfloat16 [1280, 1280], P('fsdp'), may hold values from -1.25 to 1.25
- up_weight: bfloat16 [1280, 1280], P('fsdp'), may hold values from -0.15625 to 0.15625
- down_weight: bfloat16 [1280, 1280], P('fsdp'), may hold values from -0.15625 to 0.15625
- attn_gain: bfloat16 [1280], P('fsdp'), may hold values from 0.099609375 to 1.8984375
- mlp_gain: bfloat16 [1280], P('fsdp'), may hold values from 0.099609375 to 1.8984375
- up_bias: bfloat16 [1280], P('fsdp'), may hold values from -3 to 3
- down_bias: bfloat16 [1280], P('fsdp'), may hold values from -1.796875 to 1.796875
- query_scale: bfloat16 [80], replicated, may hold values from 0.5 to 2
Outputs:
- output: bfloat16 [32768, 1280], P(('replica', 'fsdp'))
- input_grad: bfloat16 [32768, 1280], P(('replica', 'fsdp'))
- query_grad: float32 [1280, 1280], P('fsdp')
- key_grad: float32 [1280, 1280], P('fsdp')
- value_grad: float32 [1280, 1280], P('fsdp')
- output_grad: float32 [1280, 1280], P('fsdp')
- up_grad: float32 [1280, 1280], P('fsdp')
- down_grad: float32 [1280, 1280], P('fsdp')
- attn_gain_grad: float32 [1280], P('fsdp')
- mlp_gain_grad: float32 [1280], P('fsdp')
- up_bias_grad: float32 [1280], P('fsdp')
- down_bias_grad: float32 [1280], P('fsdp')
- scale_grad: float32 [80], replicated
The draws below stay inside these ranges and needn't reach their ends.
Inputs may be any that keep to these rules, and one draw needn't show every extreme that they name: `lengths`: valid tokens of each slot; some slot has exactly 1024 and some exactly 256.
All inputs are finite; a program needn't handle non-finite values.
Results may differ from the reference program's by a relative error of at most 0.017.
Values may be sent and summed in bfloat16 or wider, within the bound.
No kernel may reach another device: no remote copies, remote signals or barrier semaphores. Data moves between devices by JAX's collectives and lax.ppermute only.
A program may use at most 384 MiB of HBM per device.

```python
import math
import jax
import jax.numpy as jnp
from jax import lax

D = 1280
HEADS = 16
HD = 80
FF = 1280
SEQ = 1024
SLOTS = 32
TOKENS = 32768


def draw_lengths(key, part):
    base = jax.random.randint(key, (SLOTS,), SEQ // 4, SEQ + 1)
    picks = jax.random.permutation(jax.random.fold_in(key, 7), SLOTS)
    places = jnp.arange(SLOTS, dtype=jnp.int32)
    base = jnp.where(places == picks[0], SEQ, base)
    base = jnp.where(places == picks[1], SEQ // 4, base)
    return base.astype(jnp.int32)


def block_scale(own_key, shape, pieces, low, top_value):
    level, own = 1.0, jax.random.fold_in(own_key, 6)
    for dim, blocks in pieces:
        draws = jnp.exp(jax.random.uniform(jax.random.fold_in(own, dim), (blocks,), jnp.float32, low / len(pieces), top_value / len(pieces)))
        level = level * jnp.repeat(draws, shape[dim] // blocks).reshape([-1 if axis == dim else 1 for axis in range(len(shape))])
    return level


def gaussian(rng, shape, spread, limit, shards=(), kind=jnp.bfloat16):
    loudness = block_scale(rng, shape, shards, -0.22, 0.18) if shards else 1.0
    array = jax.random.normal(rng, shape, jnp.float32) * spread * loudness
    return jnp.minimum(jnp.maximum(array, -limit), limit).astype(kind)


def setup_inputs(seed: int = 0) -> dict:
    streams_of = jax.random.split(jax.random.key(seed), 15)
    return {
        "tokens": gaussian(streams_of[0], (TOKENS, D), 1.0, 6.0, ((0, 32),)),
        "lengths": draw_lengths(jax.random.fold_in(streams_of[14], 71), 0),
        "cotangent": gaussian(streams_of[2], (TOKENS, D), 1.0, 6.0, ((0, 32),)),
        "query_weight": gaussian(streams_of[3], (D, D), D ** -0.5, 0.15625, ((0, 8),)),
        "key_weight": gaussian(streams_of[4], (D, D), D ** -0.5, 0.15625, ((0, 8),)),
        "value_weight": gaussian(streams_of[5], (D, D), D ** -0.5, 0.15625, ((0, 8),)),
        "output_weight": gaussian(streams_of[6], (D, D), (max(D // 64, 4)) ** -0.5, 1.25, ((0, 8),)),
        "up_weight": gaussian(streams_of[7], (D, FF), D ** -0.5, 0.15625, ((0, 8),)),
        "down_weight": gaussian(streams_of[8], (FF, D), FF ** -0.5, 0.15625, ((0, 8),)),
        "attn_gain": jnp.clip(1.0 + 0.18 * jax.random.normal(streams_of[9], (D,), jnp.float32), 0.099609375, 1.8984375).astype(jnp.bfloat16),
        "mlp_gain": jnp.clip(1.0 + 0.18 * jax.random.normal(streams_of[10], (D,), jnp.float32), 0.099609375, 1.8984375).astype(jnp.bfloat16),
        "up_bias": gaussian(streams_of[11], (FF,), 0.5, 3.0, ((0, 8),)),
        "down_bias": gaussian(streams_of[12], (D,), 0.3, 1.796875, ((0, 8),)),
        "query_scale": jnp.clip(jnp.exp(jax.random.uniform(streams_of[13], (HD,), jnp.float32, math.log(0.5), math.log(2.0))), 0.5, 2.0).astype(jnp.bfloat16),
    }


@jax.custom_vjp
def low(v):
    return lax.optimization_barrier(v.astype(jnp.bfloat16)).astype(jnp.float32)

@jax.custom_vjp
def low_back(v):
    return v

def low_keep(v):
    return (low(v), None)

def low_pass(kept, grad):
    return (grad,)

def back_keep(v):
    return (v, None)

def back_low(kept, grad):
    return (low(grad),)
low.defvjp(low_keep, low_pass)
low_back.defvjp(back_keep, back_low)
EPS = 1e-06
HIGH = lax.Precision.HIGHEST

def matmul(left, right):
    return jnp.dot(left, right, precision=HIGH, preferred_element_type=jnp.float32)

def rms_norm(v, gain):
    return v * lax.rsqrt(lax.optimization_barrier(jnp.mean(v * v, axis=-1, keepdims=True)) + EPS) * gain

def attend_slot(scaled, keys, values, length):
    positions = jnp.arange(SEQ, dtype=jnp.int32)
    allowed = (positions[None, :] <= positions[:, None]) & (positions[None, :] < length)
    query_r = scaled.reshape(SEQ, HEADS, HD)
    key_r = keys.reshape(SEQ, HEADS, HD)
    value_r = values.reshape(SEQ, HEADS, HD)
    scores = low_back(jnp.einsum('qhd,khd->hqk', query_r, key_r, precision=HIGH))
    probs = jax.nn.softmax(jnp.where(allowed[None], scores, -1e+30), axis=-1)
    attended = jnp.einsum('hqk,khd->qhd', low(probs), value_r, precision=HIGH)
    return attended.reshape(SEQ, D)

def layer(xin, weights, lengths):
    wq, wk, wv, wo, w_up, w_down, gain_a, gain_m, bias_up, bias_down, qscale = weights
    attn_in = low(rms_norm(xin, gain_a))
    query_raw = low_back(matmul(attn_in, wq))
    factor = qscale * (1.0 / jnp.sqrt(jnp.float32(HD)))
    scaled = low(low_back((query_raw.reshape(-1, HEADS, HD) * factor).reshape(-1, D)))
    keys = low(low_back(matmul(attn_in, wk)))
    values = low(low_back(matmul(attn_in, wv)))
    slot_fn = jax.checkpoint(lambda pack: attend_slot(pack[0], pack[1], pack[2], pack[3]))
    attended = lax.map(slot_fn, (scaled.reshape(-1, SEQ, D), keys.reshape(-1, SEQ, D), values.reshape(-1, SEQ, D), lengths))
    attended = low(low_back(attended.reshape(-1, D)))
    hidden1 = xin + low_back(matmul(attended, wo))
    mlp_in = low(rms_norm(hidden1, gain_m))
    pre = low_back(matmul(mlp_in, w_up) + bias_up)
    act = low(jax.nn.silu(pre))
    return hidden1 + low_back(matmul(act, w_down) + bias_down)

def reference(tokens, lengths, cotangent, query_weight, key_weight, value_weight, output_weight, up_weight, down_weight, attn_gain, mlp_gain, up_bias, down_bias, query_scale):
    weights = [w.astype(jnp.float32) for w in (query_weight, key_weight, value_weight, output_weight, up_weight, down_weight, attn_gain, mlp_gain, up_bias, down_bias, query_scale)]
    xin = tokens.astype(jnp.float32)
    out_f, pull = jax.vjp(lambda xx, *ws: layer(xx, ws, lengths), xin, *weights)
    positions = jnp.arange(SEQ, dtype=jnp.int32)
    valid = (positions[None, :] < lengths[:, None]).reshape(-1, 1).astype(jnp.float32)
    grads = pull(cotangent.astype(jnp.float32) * valid)
    return (out_f.astype(jnp.bfloat16), grads[0].astype(jnp.bfloat16), grads[1], grads[2], grads[3], grads[4], grads[5], grads[6], grads[7], grads[8], grads[9], grads[10], grads[11])
```

```python
import functools
import math

import jax
import jax.numpy as jnp
from jax import lax
from jax.experimental import pallas as pl
from jax.experimental.pallas import tpu as pltpu
from jax.sharding import PartitionSpec as P

D = 1280
HEADS = 16
HD = 80
FF = 1280
SEQ = 1024
EPS = 1e-06
LOG2E = math.log2(math.e)
NEG = -1e30
LANES = 128
BLOCK = 256
GROUP = 8

bf16 = jnp.bfloat16
f32 = jnp.float32


def rms_parts(v):
    inverse = lax.rsqrt(jnp.mean(v * v, axis=-1, keepdims=True) + EPS)
    return (v * inverse, inverse)


def rms_back(grad_n, normed, inverse):
    return inverse * (grad_n - normed * jnp.mean(grad_n * normed, axis=-1, keepdims=True))


def nt(a, b):
    return lax.dot_general(a, b, (((1,), (1,)), ((), ())), preferred_element_type=f32)


def nn(a, b):
    return lax.dot_general(a, b, (((1,), (0,)), ((), ())), preferred_element_type=f32)


def tn(a, b):
    return lax.dot_general(a, b, (((0,), (0,)), ((), ())), preferred_element_type=f32)


def widen(v):
    return jnp.pad(v, ((0, 0), (0, LANES - HD)))


def split3(v):
    a = v.astype(bf16).astype(f32)
    b = (v - a).astype(bf16).astype(f32)
    c = (v - a - b).astype(bf16).astype(f32)
    return a, b, c


def extra_lanes(lane, base, extra):
    out = jnp.zeros_like(base)
    for place, value in reversed(list(enumerate(extra))):
        out = jnp.where(lane == HD + place, value, out)
    return jnp.where(lane < HD, base, out)


def forward_kernel(heads, len_ref, q_ref, k_ref, v_ref, o_ref, qa_ref, ka_ref, va_ref):
    length = len_ref[0]
    lane = lax.broadcasted_iota(jnp.int32, (SEQ, LANES), 1)
    row = lax.broadcasted_iota(jnp.int32, (SEQ, LANES), 0)
    mask = jnp.where(row < length, 0.0, NEG)
    k_pad = jnp.where(lane == HD, mask, jnp.where((lane > HD) & (lane < HD + 4), 1.0, 0.0)).astype(bf16)
    v_pad = jnp.where((lane >= HD) & (lane < HD + 3), 1.0, 0.0).astype(bf16)
    q_pad = jnp.where(lane == HD, 1.0, 0.0).astype(bf16)
    in_head = lane < HD
    block_lane = lane[:BLOCK]
    block_row = lax.broadcasted_iota(jnp.int32, (LANES, BLOCK), 0)
    causal = lax.broadcasted_iota(jnp.int32, (BLOCK, BLOCK), 0) <= lax.broadcasted_iota(
        jnp.int32, (BLOCK, BLOCK), 1
    )
    blocks = SEQ // BLOCK

    def prepare(h):
        own = slice(h * HD, (h + 1) * HD)
        ka_ref[h] = jnp.where(in_head, widen(k_ref[:, own]), k_pad)
        va_ref[h] = jnp.where(in_head, widen(v_ref[:, own]), v_pad)
        qa_ref[h] = jnp.where(in_head, widen(q_ref[:, own]), q_pad)

    def scores(h, i):
        return nt(ka_ref[h, : (i + 1) * BLOCK, :], qa_ref[h, i * BLOCK : (i + 1) * BLOCK, :])

    def attend(h, i, st):
        before = i * BLOCK
        diagonal = jnp.where(causal, st[before:], NEG)
        top = jnp.max(diagonal, axis=0, keepdims=True)
        if i:
            top = jnp.maximum(top, jnp.max(st[:before], axis=0, keepdims=True))
        p = jnp.exp2(diagonal - top).astype(bf16)
        if i:
            p = jnp.concatenate([jnp.exp2(st[:before] - top).astype(bf16), p], axis=0)
        return tn(va_ref[h, : before + BLOCK, :], p), top

    def finish(h, i, ot, top):
        rows = slice(i * BLOCK, (i + 1) * BLOCK)
        total = ot[HD : HD + 1]
        a, b, c = split3(-(top + jnp.log2(total)))
        scaled = jnp.where(block_row < HD, ot / total, 0.0)
        for place, value in ((1, a), (2, b), (3, c)):
            scaled = jnp.where(block_row == HD + place, value, scaled)
        o = scaled.T
        o_ref[rows, h * HD : (h + 1) * HD] = o[:, :HD].astype(bf16)
        qa_ref[h, rows, :] = jnp.where(block_lane <= HD, qa_ref[h, rows, :].astype(f32), o).astype(bf16)

    for h in range(heads):
        prepare(h)
    scored, done = [], []
    for h, i in [(h, i) for h in range(heads) for i in range(blocks)] + [(None, None)] * 2:
        if h is not None:
            scored.append((h, i, scores(h, i)))
        if len(scored) > 1 or (h is None and scored):
            hh, ii, st = scored.pop(0)
            done.append((hh, ii, *attend(hh, ii, st)))
        if len(done) > 1 or (h is None and not scored and done):
            finish(*done.pop(0))
    while done:
        finish(*done.pop(0))


def attend_forward(lengths, q, k, v):
    heads = GROUP
    part = pl.BlockSpec((SEQ, heads * HD), lambda g: (0, g))
    wide = pl.BlockSpec((heads, SEQ, LANES), lambda g: (g, 0, 0))
    return pl.pallas_call(
        functools.partial(forward_kernel, heads),
        grid=(HEADS // heads,),
        in_specs=[pl.BlockSpec(memory_space=pltpu.SMEM), part, part, part],
        out_specs=[part, wide, wide, wide],
        out_shape=[jax.ShapeDtypeStruct((SEQ, D), bf16)]
        + [jax.ShapeDtypeStruct((HEADS, SEQ, LANES), bf16)] * 3,
        compiler_params=pltpu.CompilerParams(vmem_limit_bytes=56 << 20),
        cost_estimate=pl.CostEstimate(
            flops=HEADS * SEQ * SEQ * 1200, bytes_accessed=20 << 20, transcendentals=HEADS * SEQ * SEQ
        ),
        name="attend_forward",
    )(lengths, q, k, v)


def backward_kernel(
    heads, fac_ref, qa_ref, ka_ref, va_ref, o_ref, g_ref, dq_ref, dk_ref, dv_ref, sg_ref, dqs, gs
):
    lane = lax.broadcasted_iota(jnp.int32, (SEQ, LANES), 1)
    causal = lax.broadcasted_iota(jnp.int32, (BLOCK, BLOCK), 0) <= lax.broadcasted_iota(
        jnp.int32, (BLOCK, BLOCK), 1
    )
    fac = fac_ref[0:1, :]
    blocks = SEQ // BLOCK

    @pl.when(pl.program_id(0) == 0)
    def _():
        sg_ref[...] = jnp.zeros_like(sg_ref)

    sums = []

    def prepare(h):
        own = slice(h * HD, (h + 1) * HD)
        g = widen(g_ref[:, own]).astype(f32)
        o = widen(o_ref[:, own]).astype(f32)
        delta = jnp.sum(g * o, axis=1, keepdims=True)
        gs[h] = extra_lanes(lane, g, split3(-delta)).astype(bf16)

    def products(h, j):
        js = slice(j * BLOCK, (j + 1) * BLOCK)
        return nt(ka_ref[h, js, :], qa_ref[h, j * BLOCK :, :]), nt(va_ref[h, js, :], gs[h, j * BLOCK :, :])

    def middle(j, st, dpt):
        p = jnp.exp2(st)
        diagonal = jnp.where(causal, p[:, :BLOCK], 0.0)
        p = jnp.concatenate([diagonal, p[:, BLOCK:]], axis=1) if j < blocks - 1 else diagonal
        return (p * dpt).astype(bf16), p.astype(bf16)

    def finish(h, j, ds, p):
        own = slice(h * HD, (h + 1) * HD)
        js = slice(j * BLOCK, (j + 1) * BLOCK)
        dv_ref[js, own] = nn(p, gs[h, j * BLOCK :, :])[:, :HD].astype(bf16)
        dk_ref[js, own] = (nn(ds, qa_ref[h, j * BLOCK :, :])[:, :HD] * (1.0 / LOG2E)).astype(bf16)
        dqt = tn(ka_ref[h, js, :], ds)
        if j == 0:
            dqs[h % 2] = dqt
        else:
            dqs[h % 2, :, j * BLOCK :] += dqt
        if j == blocks - 1:
            dq = dqs[h % 2].T.astype(bf16).astype(f32)
            sums.append(jnp.sum(dq * qa_ref[h].astype(f32), axis=0, keepdims=True))
            dq_ref[:, own] = (dq * fac)[:, :HD].astype(bf16)

    for h in range(heads):
        prepare(h)
    waiting = []
    for h, j in [(h, j) for h in range(heads) for j in range(blocks)]:
        waiting.append((h, j, *products(h, j)))
        if len(waiting) > 1:
            hh, jj, st, dpt = waiting.pop(0)
            finish(hh, jj, *middle(jj, st, dpt))
    hh, jj, st, dpt = waiting.pop(0)
    finish(hh, jj, *middle(jj, st, dpt))
    sg_ref[0:1, :] += sum(sums)


def attend_backward(fac, qa, ka, va, o, g):
    heads = GROUP
    part = pl.BlockSpec((SEQ, heads * HD), lambda g: (0, g))
    wide = pl.BlockSpec((heads, SEQ, LANES), lambda g: (g, 0, 0))
    full = pl.BlockSpec((8, LANES), lambda g: (0, 0))
    return pl.pallas_call(
        functools.partial(backward_kernel, heads),
        grid=(HEADS // heads,),
        in_specs=[full, wide, wide, wide, part, part],
        out_specs=[part, part, part, full],
        out_shape=[jax.ShapeDtypeStruct((SEQ, D), bf16)] * 3 + [jax.ShapeDtypeStruct((8, LANES), f32)],
        scratch_shapes=[pltpu.VMEM((2, LANES, SEQ), f32), pltpu.VMEM((heads, SEQ, LANES), bf16)],
        compiler_params=pltpu.CompilerParams(vmem_limit_bytes=56 << 20),
        cost_estimate=pl.CostEstimate(
            flops=HEADS * SEQ * SEQ * 2400, bytes_accessed=20 << 20, transcendentals=HEADS * SEQ * SEQ
        ),
        name="attend_backward",
    )(fac, qa, ka, va, o, g)


class Grid:
    def __init__(self, mesh_shape):
        self.copies, self.owners = mesh_shape["replica"], mesh_shape["fsdp"]
        self.planes = self.owners // 2
        self.rows = D // self.owners

    @property
    def pieced(self):
        return self.copies == 4 and self.owners % 2 == 0 and self.rows % 32 == 0 and self.planes <= 4

    def place(self):
        me, copy = lax.axis_index("fsdp"), lax.axis_index("replica")
        return copy // 2, copy % 2, me // 2, me % 2

    def along_z(self, v, step):
        n = self.planes
        pairs = [(i, (i // 2 + step) % n * 2 + i % 2) for i in range(self.owners)]
        return lax.ppermute(v, "fsdp", pairs)

    def other_core(self, v):
        return lax.ppermute(v, "fsdp", [(i, i ^ 1) for i in range(self.owners)])

    def across(self, v, code):
        return lax.ppermute(v, "replica", [(i, i ^ code) for i in range(self.copies)])


def assemble_kernel(count, planes, place_ref, *refs):
    own, other = refs[:5], refs[5:10]
    outs = refs[10 : 10 + count]
    sem = refs[10 + count]
    y, x, z, core = (place_ref[i] for i in range(4))
    rows = D // (2 * planes)
    half = rows // 2
    copies = []
    for source, c in ((own, core), (other, 1 - core)):
        block, along, *crossed = source
        for w in range(count):
            at = pl.multiple_of((2 * z + c) * rows, 16)
            copies.append((block.at[w], outs[w].at[pl.ds(at, rows), :]))
            for d in range(1, planes):
                plane = lax.rem(z - d + planes, planes)
                for code, piece in enumerate((along, *crossed)):
                    py = y if code < 2 else 1 - y
                    px = x if code % 2 == 0 else 1 - x
                    at = pl.multiple_of((2 * plane + c) * rows + py * half, 16)
                    across = pl.multiple_of(px * (D // 2), LANES)
                    copies.append(
                        (piece.at[d - 1, w], outs[w].at[pl.ds(at, half), pl.ds(across, D // 2)])
                    )
    started = []
    for n, (source, target) in enumerate(copies):
        copy = pltpu.make_async_copy(source, target, sem.at[n])
        copy.start()
        started.append(copy)
    for copy in started:
        copy.wait()


def gather_weights(grid, shards, extra=None):
    count = shards.shape[0]
    y, x, z, core = grid.place()
    half = grid.rows // 2
    piece = lax.dynamic_slice(shards, (0, y * half, x * (D // 2)), (count, half, D // 2))
    sent = piece.reshape(count * half, D // 2)
    if extra is not None:
        sent = jnp.concatenate([sent, extra], axis=0)
    arrived = [grid.along_z(sent, d) for d in range(1, grid.planes)]
    along = jnp.stack([a[: count * half] for a in arrived]).reshape(-1, count, half, D // 2)
    crossed = [grid.across(along, code) for code in (1, 2, 3)]
    own = [shards, along, *crossed]
    other = [grid.other_core(v) for v in own]
    place = jnp.stack([y, x, z, core]).astype(jnp.int32)
    total = 2 * count * (1 + 4 * (grid.planes - 1))
    whole = pl.pallas_call(
        functools.partial(assemble_kernel, count, grid.planes),
        in_specs=[pl.BlockSpec(memory_space=pltpu.SMEM)] + [pl.BlockSpec(memory_space=pl.ANY)] * 10,
        out_specs=[pl.BlockSpec(memory_space=pl.ANY)] * count,
        out_shape=[jax.ShapeDtypeStruct((D, D), bf16)] * count,
        scratch_shapes=[pltpu.SemaphoreType.DMA((total,))],
        cost_estimate=pl.CostEstimate(flops=0, bytes_accessed=count * D * D * 4, transcendentals=0),
        name="assemble",
    )(place, *own, *other)
    if extra is None:
        return whole, None
    mine = jnp.stack([extra] + [a[count * half :] for a in arrived])[:, :1]
    theirs = grid.other_core(mine)
    both = jnp.stack([jnp.where(core == 0, mine, theirs), jnp.where(core == 0, theirs, mine)], axis=1)
    planes = jnp.arange(grid.planes)
    ordered = sum(
        jnp.where((planes == (z - d) % grid.planes)[:, None, None, None], both[d][None], 0)
        for d in range(grid.planes)
    )
    return whole, ordered.reshape(grid.owners, D // 2)


def low_sum(*parts):
    total = parts[0].astype(f32)
    for part in parts[1:]:
        total = total + part.astype(f32)
    return total.astype(bf16)


def pick(v, index, axis):
    return lax.dynamic_index_in_dim(v, index, axis, keepdims=False)


def reduce_unit(grid, grads, vectors):
    y, x, z, core = grid.place()
    n, rows, half = grid.planes, grid.rows, grid.rows // 2
    extra = jnp.stack(vectors + [jnp.zeros_like(vectors[0])] * (4 - len(vectors)), axis=1)
    extra = extra.reshape(n, 2, 1, 1, 1, D // 2)
    extra = jnp.broadcast_to(
        jnp.pad(extra, ((0, 0),) * 4 + ((0, 15), (0, 0))), (n, 2, 2, 2, 16, D // 2)
    ).astype(bf16)

    def of_core(c):
        parts = [
            pick(g.reshape(n, 2, 2, half, 2, D // 2), c, 1).transpose(0, 1, 3, 2, 4).astype(bf16)
            for g in grads
        ]
        return jnp.concatenate(parts + [pick(extra, c, 1)], axis=3)

    a = low_sum(of_core(core), grid.other_core(of_core(1 - core)))
    low, high = a[..., :128, :], a[..., 128:, :]
    b1 = low_sum(pick(low, x, 2), grid.across(pick(low, 1 - x, 2), 1))
    b2 = low_sum(pick(high, y, 1), grid.across(pick(high, 1 - y, 1), 2))
    c1 = low_sum(pick(b1, y, 1), grid.across(pick(b1, 1 - y, 1), 2))
    c2 = low_sum(pick(b2, x, 1), grid.across(pick(b2, 1 - x, 1), 1))
    c = jnp.concatenate([c1, c2], axis=1)
    d = low_sum(
        pick(c, z, 0), *[grid.along_z(pick(c, (z + s) % n, 0), s) for s in range(1, n)]
    )
    crossed = [d] + [grid.across(d, code) for code in (1, 2, 3)]

    def at(py, px):
        code = (y != py) * 2 + (x != px)
        out = crossed[0]
        for k in (1, 2, 3):
            out = jnp.where(code == k, crossed[k], out)
        return out

    whole = jnp.concatenate(
        [jnp.concatenate([at(py, 0), at(py, 1)], axis=1)[None] for py in (0, 1)], axis=0
    ).astype(f32)
    out = [whole[:, w * half : (w + 1) * half].reshape(rows, D) for w in range(3)]
    tail = whole[0, 3 * half, : D // 2].reshape(4, rows)
    return out, tail


def shards(
    grid,
    tokens,
    lengths,
    cotangent,
    query_weight,
    key_weight,
    value_weight,
    output_weight,
    up_weight,
    down_weight,
    attn_gain,
    mlp_gain,
    up_bias,
    down_bias,
    query_scale,
):
    vectors = jnp.concatenate([attn_gain, mlp_gain, up_bias, down_bias])
    if grid.pieced:
        extra = jnp.pad(vectors[None], ((0, 15), (0, 0)))
        (wq, wk, wv), vecs = gather_weights(
            grid, jnp.stack([query_weight, key_weight, value_weight]), extra
        )
        (wo, w_up, w_down), _ = gather_weights(grid, jnp.stack([output_weight, up_weight, down_weight]))
        vecs = vecs.reshape(grid.owners, 4, grid.rows)
    else:
        wq, wk, wv, wo, w_up, w_down = (
            lax.all_gather(w, "fsdp", axis=0, tiled=True)
            for w in (query_weight, key_weight, value_weight, output_weight, up_weight, down_weight)
        )
        vecs = lax.all_gather(vectors, "fsdp", axis=0).reshape(grid.owners, 4, grid.rows)
    gain_a, gain_m, bias_up, bias_down = (vecs[:, i].reshape(D).astype(f32) for i in range(4))

    slots = lengths.shape[0]
    xin = tokens.astype(f32)
    normed1, inverse1 = rms_parts(xin)
    attn_in = (normed1 * gain_a).astype(bf16)
    factor = query_scale.astype(f32) * (1.0 / jnp.sqrt(f32(HD)))
    q2 = (nn(attn_in, wq) * jnp.tile(factor * LOG2E, HEADS)).astype(bf16)
    keys = nn(attn_in, wk).astype(bf16)
    values = nn(attn_in, wv).astype(bf16)

    def slot(v, s):
        return v[s * SEQ : (s + 1) * SEQ] if slots > 1 else v

    def joined(parts):
        return jnp.concatenate(parts, axis=0) if slots > 1 else parts[0]

    kept = [
        attend_forward(lengths[s : s + 1], slot(q2, s), slot(keys, s), slot(values, s)) for s in range(slots)
    ]
    attended = joined([k[0] for k in kept])
    hidden1 = xin + nn(attended, wo)
    normed2, inverse2 = rms_parts(hidden1)
    mlp_in = (normed2 * gain_m).astype(bf16)
    pre = nn(mlp_in, w_up) + bias_up
    sigma = jax.nn.sigmoid(pre)
    act = (pre * sigma).astype(bf16)
    out_f = hidden1 + nn(act, w_down) + bias_down

    positions = jnp.arange(SEQ, dtype=jnp.int32)
    valid = (positions[None, :] < lengths[:, None]).reshape(-1, 1).astype(f32)
    grad_out = cotangent.astype(f32) * valid
    grad_out_low = grad_out.astype(bf16)
    down_bias_grad = jnp.sum(grad_out, axis=0)
    grad_pre = (nt(grad_out_low, w_down) * (sigma * (1.0 + pre * (1.0 - sigma)))).astype(bf16)
    up_bias_grad = jnp.sum(grad_pre.astype(f32), axis=0)
    grad_mlp_in = nt(grad_pre, w_up)
    mlp_gain_grad = jnp.sum(grad_mlp_in * normed2, axis=0)
    grad_hidden = grad_out + rms_back(grad_mlp_in * gain_m, normed2, inverse2)
    grad_proj = grad_hidden.astype(bf16)
    grad_att = nt(grad_proj, wo).astype(bf16)

    fac_row = jnp.broadcast_to(jnp.pad(factor, (0, LANES - HD))[None], (8, LANES))
    backs = [
        attend_backward(fac_row, *kept[s][1:], kept[s][0], slot(grad_att, s)) for s in range(slots)
    ]
    grad_query, grad_keys, grad_values = (joined([b[i] for b in backs]) for i in range(3))
    scale_part = sum(b[3][0, :HD] for b in backs) / (query_scale.astype(f32) * LOG2E)
    grad_attn_in = nt(grad_query, wq) + nt(grad_keys, wk) + nt(grad_values, wv)
    attn_gain_grad = jnp.sum(grad_attn_in * normed1, axis=0)
    input_grad = grad_hidden + rms_back(grad_attn_in * gain_a, normed1, inverse1)

    mlp_grads = [tn(attended, grad_proj), tn(mlp_in, grad_pre), tn(act, grad_out_low)]
    attn_grads = [tn(attn_in, g) for g in (grad_query, grad_keys, grad_values)]
    if grid.pieced:
        owned = (grid.owners, grid.rows)
        (g_o, g_up, g_down), tail_m = reduce_unit(
            grid, mlp_grads, [v.reshape(owned) for v in (mlp_gain_grad, up_bias_grad, down_bias_grad)]
        )
        scale_rows = jnp.broadcast_to(jnp.pad(scale_part, (0, grid.rows - HD))[None], owned)
        (g_q, g_k, g_v), tail_a = reduce_unit(grid, attn_grads, [attn_gain_grad.reshape(owned), scale_rows])
        sums = (g_q, g_k, g_v, g_o, g_up, g_down, tail_a[0], tail_m[0], tail_m[1], tail_m[2])
        scale_grad = tail_a[1, :HD]
    else:
        sums = tuple(
            lax.psum(lax.psum_scatter(g, "fsdp", scatter_dimension=0, tiled=True), "replica")
            for g in (*attn_grads, *mlp_grads, attn_gain_grad, mlp_gain_grad, up_bias_grad, down_bias_grad)
        )
        scale_grad = lax.psum(scale_part, ("replica", "fsdp"))
    return (out_f.astype(bf16), input_grad.astype(bf16), *sums, scale_grad)


def solution(mesh):
    split = P(("replica", "fsdp"), None)
    rows = P("fsdp", None)
    part = P("fsdp")
    return jax.shard_map(
        functools.partial(shards, Grid(mesh.shape)),
        mesh=mesh,
        in_specs=(split, P(("replica", "fsdp")), split, *[rows] * 6, *[part] * 4, P()),
        out_specs=(split, split, *[rows] * 6, *[part] * 4, P()),
        check_vma=False,
    )
```

```python
import functools
import math

import jax
import jax.numpy as jnp
from jax import lax
from jax.experimental import pallas as pl
from jax.experimental.pallas import tpu as pltpu
from jax.sharding import PartitionSpec as P

D = 1280
HEADS = 16
HD = 80
FF = 1280
SEQ = 1024
EPS = 1e-06
LOG2E = math.log2(math.e)
NEG = -1e30
LANES = 128
BLOCK = 256
GROUP = 8
HALF = GROUP * HD
TRIPLE = 3 * HALF
VMEM_LIMIT = 58 << 20

bf16 = jnp.bfloat16
f32 = jnp.float32


def rms_parts(v):
    inverse = lax.rsqrt(jnp.mean(v * v, axis=-1, keepdims=True) + EPS)
    return (v * inverse, inverse)


def rms_back(grad_n, normed, inverse):
    return inverse * (grad_n - normed * jnp.mean(grad_n * normed, axis=-1, keepdims=True))


def nt(a, b):
    return lax.dot_general(a, b, (((1,), (1,)), ((), ())), preferred_element_type=f32)


def nn(a, b):
    return lax.dot_general(a, b, (((1,), (0,)), ((), ())), preferred_element_type=f32)


def tn(a, b):
    return lax.dot_general(a, b, (((0,), (0,)), ((), ())), preferred_element_type=f32)


def widen(v):
    return jnp.pad(v, ((0, 0), (0, LANES - HD)))


def split3(v):
    a = v.astype(bf16).astype(f32)
    b = (v - a).astype(bf16).astype(f32)
    c = (v - a - b).astype(bf16).astype(f32)
    return a, b, c


def extra_lanes(lane, base, extra):
    out = jnp.zeros_like(base)
    for place, value in reversed(list(enumerate(extra))):
        out = jnp.where(lane == HD + place, value, out)
    return jnp.where(lane < HD, base, out)


def forward_kernel(heads, len_ref, qkv_ref, o_ref, qa_ref, ka_ref, va_ref):
    length = len_ref[0]
    lane = lax.broadcasted_iota(jnp.int32, (SEQ, LANES), 1)
    row = lax.broadcasted_iota(jnp.int32, (SEQ, LANES), 0)
    mask = jnp.where(row < length, 0.0, NEG)
    k_pad = jnp.where(lane == HD, mask, jnp.where((lane > HD) & (lane < HD + 4), 1.0, 0.0)).astype(bf16)
    v_pad = jnp.where((lane >= HD) & (lane < HD + 3), 1.0, 0.0).astype(bf16)
    q_pad = jnp.where(lane == HD, 1.0, 0.0).astype(bf16)
    in_head = lane < HD
    block_lane = lane[:BLOCK]
    block_row = lax.broadcasted_iota(jnp.int32, (LANES, BLOCK), 0)
    causal = lax.broadcasted_iota(jnp.int32, (BLOCK, BLOCK), 0) <= lax.broadcasted_iota(
        jnp.int32, (BLOCK, BLOCK), 1
    )
    blocks = SEQ // BLOCK

    def prepare(h):
        for n, (ref, pad) in enumerate(((qa_ref, q_pad), (ka_ref, k_pad), (va_ref, v_pad))):
            at = n * HALF + h * HD
            ref[h] = jnp.where(in_head, widen(qkv_ref[:, at : at + HD]), pad)

    def scores(h, i):
        return nt(ka_ref[h, : (i + 1) * BLOCK, :], qa_ref[h, i * BLOCK : (i + 1) * BLOCK, :])

    def attend(h, i, st):
        before = i * BLOCK
        diagonal = jnp.where(causal, st[before:], NEG)
        top = jnp.max(diagonal, axis=0, keepdims=True)
        if i:
            top = jnp.maximum(top, jnp.max(st[:before], axis=0, keepdims=True))
        p = jnp.exp2(diagonal - top).astype(bf16)
        if i:
            p = jnp.concatenate([jnp.exp2(st[:before] - top).astype(bf16), p], axis=0)
        return tn(va_ref[h, : before + BLOCK, :], p), top

    def finish(h, i, ot, top):
        rows = slice(i * BLOCK, (i + 1) * BLOCK)
        total = ot[HD : HD + 1]
        a, b, c = split3(-(top + jnp.log2(total)))
        scaled = jnp.where(block_row < HD, ot / total, 0.0)
        for place, value in ((1, a), (2, b), (3, c)):
            scaled = jnp.where(block_row == HD + place, value, scaled)
        o = scaled.T
        o_ref[rows, h * HD : (h + 1) * HD] = o[:, :HD].astype(bf16)
        qa_ref[h, rows, :] = jnp.where(block_lane <= HD, qa_ref[h, rows, :].astype(f32), o).astype(bf16)

    for h in range(heads):
        prepare(h)
    scored, done = [], []
    for h, i in [(h, i) for h in range(heads) for i in range(blocks)] + [(None, None)] * 2:
        if h is not None:
            scored.append((h, i, scores(h, i)))
        if len(scored) > 1 or (h is None and scored):
            hh, ii, st = scored.pop(0)
            done.append((hh, ii, *attend(hh, ii, st)))
        if len(done) > 1 or (h is None and not scored and done):
            finish(*done.pop(0))
    while done:
        finish(*done.pop(0))


def attend_forward(half, lengths, qkv, before=None):
    wide = pl.BlockSpec((GROUP, SEQ, LANES), lambda g: (0, 0, 0))
    kept = [] if before is None else [before]

    def kernel(len_ref, qkv_ref, *refs):
        forward_kernel(GROUP, len_ref, qkv_ref, *refs[len(kept) :])

    return pl.pallas_call(
        kernel,
        grid=(1,),
        in_specs=[pl.BlockSpec(memory_space=pltpu.SMEM), pl.BlockSpec((SEQ, TRIPLE), lambda g: (0, 0))]
        + [pl.BlockSpec(memory_space=pl.ANY)] * len(kept),
        out_specs=[pl.BlockSpec((SEQ, HALF), lambda g: (0, half)), wide, wide, wide],
        out_shape=[jax.ShapeDtypeStruct((SEQ, D), bf16)]
        + [jax.ShapeDtypeStruct((GROUP, SEQ, LANES), bf16)] * 3,
        input_output_aliases={2: 0} if kept else {},
        compiler_params=pltpu.CompilerParams(vmem_limit_bytes=VMEM_LIMIT),
        cost_estimate=pl.CostEstimate(
            flops=GROUP * SEQ * SEQ * 1200, bytes_accessed=10 << 20, transcendentals=GROUP * SEQ * SEQ
        ),
        name="attend_forward",
    )(lengths, qkv, *kept)


def backward_kernel(
    heads, fac_ref, qa_ref, ka_ref, va_ref, o_ref, g_ref, d_ref, sg_ref, dqs, gs
):
    lane = lax.broadcasted_iota(jnp.int32, (SEQ, LANES), 1)
    causal = lax.broadcasted_iota(jnp.int32, (BLOCK, BLOCK), 0) <= lax.broadcasted_iota(
        jnp.int32, (BLOCK, BLOCK), 1
    )
    fac = fac_ref[0:1, :]
    blocks = SEQ // BLOCK

    @pl.when(pl.program_id(0) == 0)
    def _():
        sg_ref[...] = jnp.zeros_like(sg_ref)

    sums = []

    def prepare(h):
        own = slice(h * HD, (h + 1) * HD)
        g = widen(g_ref[:, own]).astype(f32)
        o = widen(o_ref[:, own]).astype(f32)
        delta = jnp.sum(g * o, axis=1, keepdims=True)
        gs[h] = extra_lanes(lane, g, split3(-delta)).astype(bf16)

    def products(h, j):
        js = slice(j * BLOCK, (j + 1) * BLOCK)
        return nt(ka_ref[h, js, :], qa_ref[h, j * BLOCK :, :]), nt(va_ref[h, js, :], gs[h, j * BLOCK :, :])

    def middle(j, st, dpt):
        p = jnp.exp2(st)
        diagonal = jnp.where(causal, p[:, :BLOCK], 0.0)
        p = jnp.concatenate([diagonal, p[:, BLOCK:]], axis=1) if j < blocks - 1 else diagonal
        return (p * dpt).astype(bf16), p.astype(bf16)

    def finish(h, j, ds, p):
        own, dk, dv = (slice(n * HALF + h * HD, n * HALF + (h + 1) * HD) for n in range(3))
        js = slice(j * BLOCK, (j + 1) * BLOCK)
        d_ref[js, dv] = nn(p, gs[h, j * BLOCK :, :])[:, :HD].astype(bf16)
        d_ref[js, dk] = (nn(ds, qa_ref[h, j * BLOCK :, :])[:, :HD] * (1.0 / LOG2E)).astype(bf16)
        dqt = tn(ka_ref[h, js, :], ds)
        if j == 0:
            dqs[h % 2] = dqt
        else:
            dqs[h % 2, :, j * BLOCK :] += dqt
        if j == blocks - 1:
            dq = dqs[h % 2].T.astype(bf16).astype(f32)
            sums.append(jnp.sum(dq * qa_ref[h].astype(f32), axis=0, keepdims=True))
            d_ref[:, own] = (dq * fac)[:, :HD].astype(bf16)

    for h in range(heads):
        prepare(h)
    waiting = []
    for h, j in [(h, j) for h in range(heads) for j in range(blocks)]:
        waiting.append((h, j, *products(h, j)))
        if len(waiting) > 1:
            hh, jj, st, dpt = waiting.pop(0)
            finish(hh, jj, *middle(jj, st, dpt))
    hh, jj, st, dpt = waiting.pop(0)
    finish(hh, jj, *middle(jj, st, dpt))
    sg_ref[0:1, :] += sum(sums)


def attend_backward(half, fac, qa, ka, va, o, g):
    part = pl.BlockSpec((SEQ, HALF), lambda g: (0, half))
    wide = pl.BlockSpec((GROUP, SEQ, LANES), lambda g: (0, 0, 0))
    full = pl.BlockSpec((8, LANES), lambda g: (0, 0))
    return pl.pallas_call(
        functools.partial(backward_kernel, GROUP),
        grid=(1,),
        in_specs=[full, wide, wide, wide, part, part],
        out_specs=[pl.BlockSpec((SEQ, TRIPLE), lambda g: (0, 0)), full],
        out_shape=[jax.ShapeDtypeStruct((SEQ, TRIPLE), bf16), jax.ShapeDtypeStruct((8, LANES), f32)],
        scratch_shapes=[pltpu.VMEM((2, LANES, SEQ), f32), pltpu.VMEM((GROUP, SEQ, LANES), bf16)],
        compiler_params=pltpu.CompilerParams(vmem_limit_bytes=VMEM_LIMIT),
        cost_estimate=pl.CostEstimate(
            flops=GROUP * SEQ * SEQ * 2400, bytes_accessed=10 << 20, transcendentals=GROUP * SEQ * SEQ
        ),
        name="attend_backward",
    )(fac, qa, ka, va, o, g)


class Grid:
    def __init__(self, mesh_shape):
        self.copies, self.owners = mesh_shape["replica"], mesh_shape["fsdp"]
        self.planes = self.owners // 2
        self.rows = D // self.owners

    @property
    def pieced(self):
        return self.copies == 4 and self.owners == 8

    def place(self):
        me, copy = lax.axis_index("fsdp"), lax.axis_index("replica")
        return copy // 2, copy % 2, me // 2, me % 2

    def along_z(self, v, step):
        n = self.planes
        pairs = [(i, (i // 2 + step) % n * 2 + i % 2) for i in range(self.owners)]
        return lax.ppermute(v, "fsdp", pairs)

    def other_core(self, v):
        return lax.ppermute(v, "fsdp", [(i, i ^ 1) for i in range(self.owners)])

    def across(self, v, code):
        return lax.ppermute(v, "replica", [(i, i ^ code) for i in range(self.copies)])


def kernel_call(kernel, name, operands, outs, scratch=(), flops=0, nbytes=0, **more):
    return pl.pallas_call(
        kernel,
        out_shape=outs,
        scratch_shapes=scratch,
        compiler_params=pltpu.CompilerParams(vmem_limit_bytes=VMEM_LIMIT),
        cost_estimate=pl.CostEstimate(flops=flops, bytes_accessed=nbytes, transcendentals=0),
        name=name,
        **more,
    )(*operands)


def piece_copies(planes, quarter, place_ref, refs, buf, sem):
    y, x, z, core = (place_ref[i] for i in range(4))
    groups = []
    for s, (source, c) in enumerate(((refs[:5], core), (refs[5:10], 1 - core))):
        block, *pieces = source
        home = 2 * z + c
        groups.append((home, [pltpu.make_async_copy(block, buf.at[home], sem.at[s, 0, 0])]))
        for d in range(1, planes):
            owner = 2 * lax.rem(z - d + planes, planes) + c
            copies = []
            for code, piece in enumerate(pieces):
                py = 1 - y if code >= 2 else y
                px = 1 - x if code % 2 else x
                at = pl.multiple_of((2 * py + px) * quarter, 16)
                copies.append(
                    pltpu.make_async_copy(piece.at[d - 1], buf.at[owner, pl.ds(at, quarter), :], sem.at[s, d, code])
                )
            groups.append((owner, copies))
    return groups


def assemble_kernel(tiles, planes, rows, quarter, place_ref, *refs):
    outs, (buf, sem_in, sem_out) = refs[10:-3], refs[-3:]
    groups = piece_copies(planes, quarter, place_ref, refs, buf, sem_in)
    for _, copies in groups:
        for copy in copies:
            copy.start()
    written = []
    for g, (owner, copies) in enumerate(groups):
        for copy in copies:
            copy.wait()
        at = pl.multiple_of(owner * rows, 16)
        for t, (w, h) in enumerate(tiles):
            copy = pltpu.make_async_copy(
                buf.at[owner, pl.ds(t * rows, rows), :],
                outs[w].at[pl.ds(at, rows), pl.ds(h * HALF, HALF)],
                sem_out.at[g, t],
            )
            copy.start()
            written.append(copy)
    for copy in written:
        copy.wait()


def project_kernel(planes, rows, quarter, first, place_ref, scale_ref, x_ref, *refs):
    outs, scratch = refs[10 : 10 + (5 if first else 2)], refs[10 + (5 if first else 2) :]
    qkv_ref, whole_ref = outs[:2]
    buf, sem_in, sem_out = scratch[:3]
    groups = piece_copies(planes, quarter, place_ref, refs, buf, sem_in)
    for _, copies in groups:
        for copy in copies:
            copy.start()
    if first:
        held = scratch[3]
        for at in range(0, SEQ, BLOCK):
            held[at : at + BLOCK, :] = rms_parts(x_ref[at : at + BLOCK, :].astype(f32))[0]
    written = []
    for g, (owner, copies) in enumerate(groups):
        for copy in copies:
            copy.wait()
        at = pl.multiple_of(owner * rows, 16)
        for t in range(3):
            copy = pltpu.make_async_copy(
                buf.at[owner, pl.ds(t * rows, rows), :],
                whole_ref.at[pl.ds(at, rows), pl.ds(t * HALF, HALF)],
                sem_out.at[g, t],
            )
            copy.start()
            written.append(copy)
    if first:
        vec_ref, attn_in, left_ref = outs[2:5]
        vec_ref[...] = buf[:, 3 * rows : 3 * rows + 16, :]
        gain = jnp.concatenate([buf[b, 3 * rows : 3 * rows + 16, :rows][0:1] for b in range(2 * planes)], axis=1)
        gain = gain.astype(f32)
        for at in range(0, SEQ, BLOCK):
            attn_in[at : at + BLOCK, :] = (held[at : at + BLOCK, :] * gain).astype(bf16)
    else:
        attn_in = x_ref
    for t in range(3):
        weight = buf[:, t * rows : (t + 1) * rows, :].reshape(D, HALF)
        result = nn(attn_in[...], weight)
        qkv_ref[:, t * HALF : (t + 1) * HALF] = (result * scale_ref[0:1, :] if t == 0 else result).astype(bf16)
    if first:
        left_ref[...] = attn_in[...].T
    for copy in written:
        copy.wait()


def project(grid, place, scale, x, pieces, first):
    total = pieces[0].shape[0]
    vmem, hbm = pl.BlockSpec(memory_space=pltpu.VMEM), pl.BlockSpec(memory_space=pl.ANY)
    outs = [jax.ShapeDtypeStruct((SEQ, TRIPLE), bf16), jax.ShapeDtypeStruct((D, TRIPLE), bf16)]
    scratch = [
        pltpu.VMEM((grid.owners, total, HALF), bf16),
        pltpu.SemaphoreType.DMA((2, grid.planes, 4)),
        pltpu.SemaphoreType.DMA((grid.owners, 3)),
    ]
    if first:
        outs += [
            jax.ShapeDtypeStruct((grid.owners, 16, HALF), bf16),
            jax.ShapeDtypeStruct((SEQ, D), bf16),
            jax.ShapeDtypeStruct((D, SEQ), bf16),
        ]
        scratch.append(pltpu.VMEM((SEQ, D), f32))
    return kernel_call(
        functools.partial(project_kernel, grid.planes, grid.rows, total // 4, first),
        "project",
        (place, scale, x, *pieces),
        outs,
        scratch=scratch,
        flops=2 * SEQ * D * TRIPLE,
        nbytes=4 * D * TRIPLE + 2 * SEQ * (D + TRIPLE),
        in_specs=[pl.BlockSpec(memory_space=pltpu.SMEM), vmem, vmem] + [hbm] * 10,
        out_specs=[vmem, hbm] + [vmem] * 3 * first,
    )


def cut_kernel(rows, place_ref, *refs):
    weights, vec_ref = refs[:6], refs[6]
    chunks, pieces = refs[7:10], refs[10:13]
    for half in range(2):
        for t in range(3):
            chunks[half][t * rows : (t + 1) * rows, :] = weights[t][:, half * HALF : (half + 1) * HALF]
        chunks[half][3 * rows :, :] = vec_ref[...]
    for t in range(6):
        w, half = 3 + t // 2, t % 2
        chunks[2][t * rows : (t + 1) * rows, :] = weights[w][:, half * HALF : (half + 1) * HALF]
    copy = 2 * place_ref[0] + place_ref[1]
    for chunk, piece in zip(chunks, pieces, strict=True):
        quarter = piece.shape[0]
        piece[...] = chunk[pl.ds(pl.multiple_of(copy * quarter, 16), quarter), :]


def cut(grid, place, weights, vectors):
    rows = [512, 512, 6 * grid.rows]
    vec = jnp.pad(vectors.reshape(1, HALF), ((0, 512 - 3 * grid.rows - 1), (0, 0)))
    out = kernel_call(
        functools.partial(cut_kernel, grid.rows),
        "cut",
        (place, *weights, vec),
        [jax.ShapeDtypeStruct((n, HALF), bf16) for n in rows]
        + [jax.ShapeDtypeStruct((n // 4, HALF), bf16) for n in rows],
        nbytes=12 * grid.rows * D * 2,
        in_specs=[pl.BlockSpec(memory_space=pltpu.SMEM)] + [pl.BlockSpec(memory_space=pltpu.VMEM)] * 7,
    )
    return out[:3], out[3:]


def chunk_across(grid, along):
    return [along] + [grid.across(along, code) for code in (1, 2, 3)]


def both_cores(grid, own):
    return own + [grid.other_core(v) for v in own]


def assemble(grid, place, tiles, pieces):
    total = pieces[0].shape[0]
    count = 1 + max(w for w, _ in tiles)
    return kernel_call(
        functools.partial(assemble_kernel, tiles, grid.planes, grid.rows, total // 4),
        "assemble",
        (place, *pieces),
        [jax.ShapeDtypeStruct((D, D), bf16)] * count,
        scratch=[
            pltpu.VMEM((grid.owners, total, HALF), bf16),
            pltpu.SemaphoreType.DMA((2, grid.planes, 4)),
            pltpu.SemaphoreType.DMA((grid.owners, len(tiles))),
        ],
        nbytes=count * D * D * 4,
        in_specs=[pl.BlockSpec(memory_space=pltpu.SMEM)] + [pl.BlockSpec(memory_space=pl.ANY)] * 10,
        out_specs=[pl.BlockSpec(memory_space=pl.ANY)] * count,
    )


def weight_grad_kernel(planes, rows, place_ref, left_ref, right_ref, vec_ref, mine, theirs, left, right, stage, sem_in, sem_out):
    core = place_ref[3]
    loads = [pltpu.make_async_copy(left_ref, left, sem_in.at[3])]
    for w in range(3):
        part = pl.ds(w * HALF, HALF)
        loads.append(pltpu.make_async_copy(right_ref.at[:, part], right.at[:, part], sem_in.at[w]))
    for load in loads:
        load.start()
    written = []

    def send(w, source, size, c, whole, z):
        copy = pltpu.make_async_copy(source, whole.at[z, pl.ds(w * rows, size), :], sem_out.at[w, c, z])
        copy.start()
        written.append(copy)

    sides = ((1, theirs), (0, mine))
    owner = {(c, z): 2 * z + (1 - core if c else core) for c in range(2) for z in range(planes)}
    for c, whole in sides:
        for z in range(planes):
            send(3, vec_ref.at[owner[c, z]], 32, c, whole, z)
    loads[0].wait()
    for w in range(3):
        loads[1 + w].wait()
        stage[w] = nn(left[...], right[:, w * HALF : (w + 1) * HALF]).astype(bf16)
        for c, whole in sides:
            for z in range(planes):
                at = pl.multiple_of(owner[c, z] * rows, 16)
                send(w, stage.at[w, pl.ds(at, rows), :], rows, c, whole, z)
    for copy in written:
        copy.wait()


def weight_grads(grid, place, left, right, vectors):
    rows = jnp.stack(vectors, axis=1).astype(bf16)
    rows = jnp.pad(rows, ((0, 0), (0, 32 - len(vectors)), (0, HALF - grid.rows)))
    shape = jax.ShapeDtypeStruct((grid.planes, 512, HALF), bf16)
    hbm = pl.BlockSpec(memory_space=pl.ANY)
    return kernel_call(
        functools.partial(weight_grad_kernel, grid.planes, grid.rows),
        "weight_grads",
        (place, left, right, rows),
        [shape, shape],
        scratch=[
            pltpu.VMEM((D, SEQ), bf16),
            pltpu.VMEM((SEQ, TRIPLE), bf16),
            pltpu.VMEM((3, D, HALF), bf16),
            pltpu.SemaphoreType.DMA((4,)),
            pltpu.SemaphoreType.DMA((4, 2, grid.planes)),
        ],
        flops=2 * SEQ * D * TRIPLE,
        nbytes=(SEQ * D + (SEQ + D) * TRIPLE) * 2,
        in_specs=[pl.BlockSpec(memory_space=pltpu.SMEM), hbm, hbm, pl.BlockSpec(memory_space=pltpu.VMEM)],
        out_specs=[hbm, hbm],
    )


def added(a, b):
    return (a.astype(f32) + b.astype(f32)).astype(bf16)


def fold_cores_kernel(place_ref, a_ref, b_ref, send_low, keep_low, send_high, keep_high):
    y, x = place_ref[0], place_ref[1]
    for p in range(2):
        send_low[0, p] = added(a_ref[0, p, 1 - x, 0], b_ref[0, p, 1 - x, 0])
        keep_low[0, p] = added(a_ref[0, p, x, 0], b_ref[0, p, x, 0])
        send_high[0, p] = added(a_ref[0, 1 - y, p, 1], b_ref[0, 1 - y, p, 1])
        keep_high[0, p] = added(a_ref[0, y, p, 1], b_ref[0, y, p, 1])


def fold_cores(grid, place, a, b):
    n, columns = grid.planes, a.shape[2]
    split = (n, 2, 2, 2, 64, columns)
    block = pl.BlockSpec((1, *split[1:]), lambda i: (i, 0, 0, 0, 0, 0))
    out = pl.BlockSpec((1, 2, 64, columns), lambda i: (i, 0, 0, 0))
    return kernel_call(
        fold_cores_kernel,
        "fold_cores",
        (place, a.reshape(split), b.reshape(split)),
        [jax.ShapeDtypeStruct((n, 2, 64, columns), bf16)] * 4,
        nbytes=a.size * 6,
        grid=(n,),
        in_specs=[pl.BlockSpec(memory_space=pltpu.SMEM), block, block],
        out_specs=[out] * 4,
    )


def fold_first_kernel(place_ref, low_a, low_b, high_a, high_b, send_low, keep_low, send_high, keep_high):
    y, x = place_ref[0], place_ref[1]
    send_low[0] = added(low_a[0, 1 - y], low_b[0, 1 - y])
    keep_low[0] = added(low_a[0, y], low_b[0, y])
    send_high[0] = added(high_a[0, 1 - x], high_b[0, 1 - x])
    keep_high[0] = added(high_a[0, x], high_b[0, x])


def fold_first(grid, place, *parts):
    n, columns = grid.planes, parts[0].shape[3]
    block = pl.BlockSpec((1, 2, 64, columns), lambda i: (i, 0, 0, 0))
    out = pl.BlockSpec((1, 64, columns), lambda i: (i, 0, 0))
    return kernel_call(
        fold_first_kernel,
        "fold_first",
        (place, *parts),
        [jax.ShapeDtypeStruct((n, 64, columns), bf16)] * 4,
        nbytes=parts[0].size * 12,
        grid=(n,),
        in_specs=[pl.BlockSpec(memory_space=pltpu.SMEM)] + [block] * 4,
        out_specs=[out] * 4,
    )


def fold_second_kernel(planes, place_ref, low_a, low_b, high_a, high_b, *outs):
    z = place_ref[2]
    for s in range(planes):
        at = lax.rem(z + s, planes)
        outs[s][0] = added(low_a[at], low_b[at])
        outs[s][1] = added(high_a[at], high_b[at])


def fold_second(grid, place, *parts):
    n, columns = grid.planes, parts[0].shape[2]
    return kernel_call(
        functools.partial(fold_second_kernel, n),
        "fold_second",
        (place, *parts),
        [jax.ShapeDtypeStruct((2, 64, columns), bf16)] * n,
        nbytes=parts[0].size * 12,
        in_specs=[pl.BlockSpec(memory_space=pltpu.SMEM)] + [pl.BlockSpec(memory_space=pltpu.VMEM)] * 4,
    )


def fold_planes_kernel(*refs):
    *parts, out = refs
    total = parts[0][...].astype(f32)
    for part in parts[1:]:
        total = total + part[...].astype(f32)
    out[...] = total.astype(bf16)


def fold_planes(grid, *parts):
    return kernel_call(
        fold_planes_kernel,
        "fold_planes",
        parts,
        jax.ShapeDtypeStruct(parts[0].shape, bf16),
        nbytes=parts[0].size * 10,
    )


def finish_kernel(units, rows, place_ref, *refs):
    me = 2 * place_ref[0] + place_ref[1]
    parts, outs, stage = refs[: 4 * units], refs[4 * units : -1], refs[-1]
    columns = parts[0].shape[2]
    for u in range(units):
        across = slice(u * columns, (u + 1) * columns)
        for r in range(4):
            for code in range(4):

                @pl.when(me == r ^ code)
                def _(r=r, code=code, u=u, across=across):
                    for h in range(2):
                        at = 128 * r + 64 * h
                        stage[at : at + 64, across] = parts[4 * u + code][h].astype(f32)

    for w in range(3):
        outs[w][...] = stage[w * rows : (w + 1) * rows, :]
    outs[3][...] = stage[3 * rows :, :]


def finish(grid, place, units):
    columns = units[0][0].shape[2] * len(units)
    parts = [part for unit in units for part in unit]
    return kernel_call(
        functools.partial(finish_kernel, len(units), grid.rows),
        "finish",
        (place, *parts),
        [jax.ShapeDtypeStruct((grid.rows, columns), f32)] * 3
        + [jax.ShapeDtypeStruct((512 - 3 * grid.rows, columns), f32)],
        scratch=[pltpu.VMEM((512, columns), f32)],
        nbytes=512 * columns * 6,
        in_specs=[pl.BlockSpec(memory_space=pltpu.SMEM)]
        + [pl.BlockSpec(memory_space=pltpu.VMEM)] * len(parts),
    )


def input_grad_kernel(x_ref, gain_ref, hidden_ref, grad_a, grad_b, weight_a, weight_b, out):
    total = nt(grad_a[...], weight_a[...]) + nt(grad_b[...], weight_b[...])
    normed, inverse = rms_parts(x_ref[...].astype(f32))
    out[...] = (hidden_ref[...] + rms_back(total * gain_ref[0:1, :], normed, inverse)).astype(bf16)


def input_grad_of(tokens, gain, grad_hidden, grads, weights):
    count, block = tokens.shape[0], BLOCK
    rows = pl.BlockSpec((block, D), lambda i: (i, 0))
    return kernel_call(
        input_grad_kernel,
        "input_grad",
        (tokens, jnp.broadcast_to(gain[None], (8, D)), grad_hidden, *grads, *weights),
        jax.ShapeDtypeStruct((count, D), bf16),
        flops=6 * count * D * D,
        nbytes=6 * D * D + 14 * count * D,
        grid=(count // block,),
        in_specs=[rows, pl.BlockSpec((8, D), lambda i: (0, 0)), rows]
        + [pl.BlockSpec((block, TRIPLE), lambda i: (i, 0))] * 2
        + [pl.BlockSpec((D, TRIPLE), lambda i: (0, 0))] * 2,
        out_specs=rows,
    )


def after(value, *first):
    return lax.optimization_barrier((value, first))[0]


def shards(
    grid,
    tokens,
    lengths,
    cotangent,
    query_weight,
    key_weight,
    value_weight,
    output_weight,
    up_weight,
    down_weight,
    attn_gain,
    mlp_gain,
    up_bias,
    down_bias,
    query_scale,
):
    assert lengths.shape[0] == 1 and tokens.shape[0] == SEQ
    vectors = jnp.concatenate([attn_gain, mlp_gain, up_bias, down_bias])
    y, x, z, core = grid.place()
    place = jnp.stack([y, x, z, core]).astype(jnp.int32)
    xin = tokens.astype(f32)
    factor = query_scale.astype(f32) * (1.0 / jnp.sqrt(f32(HD)))
    scale_half = jnp.broadcast_to(jnp.tile(factor * LOG2E, GROUP)[None], (8, HALF))
    if grid.pieced:
        weights = (query_weight, key_weight, value_weight, output_weight, up_weight, down_weight)
        chunks, cuts = cut(grid, place, weights, vectors)
        planes = range(1, grid.planes)
        z1 = [grid.along_z(cuts[0], d) for d in planes]
        z2 = [grid.along_z(after(cuts[1], *z1), d) for d in planes]
        across1 = chunk_across(grid, jnp.stack(z1))
        across2 = chunk_across(grid, jnp.stack(after(z2, *z1)))
        z3 = [grid.along_z(after(cuts[2], *z2), d) for d in planes]
        qkv_a, wa, vecs, attn_in, left = project(
            grid, place, scale_half, after(tokens, *z3), both_cores(grid, [chunks[0], *across1]), True
        )
        vecs = vecs[:, 0].reshape(grid.owners, 4, grid.rows)
        attended, *kept_a = attend_forward(0, lengths, qkv_a)
        across3 = chunk_across(grid, jnp.stack(after(z3, qkv_a)))
        pieces2 = both_cores(grid, [chunks[1], *after(across2, qkv_a)])
        qkv_b, wb = project(grid, place, scale_half, attn_in, pieces2, False)
        attended, *kept_b = attend_forward(1, lengths, qkv_b, attended)
        pieces3 = both_cores(grid, [chunks[2], *after(across3, qkv_b)])
        tiles = ((0, 0), (0, 1), (1, 0), (1, 1), (2, 0), (2, 1))
        wo, w_up, w_down = assemble(grid, place, tiles, pieces3)
    else:
        wq, wk, wv, wo, w_up, w_down = (
            lax.all_gather(w, "fsdp", axis=0, tiled=True)
            for w in (query_weight, key_weight, value_weight, output_weight, up_weight, down_weight)
        )
        wa = jnp.concatenate([w[:, :HALF] for w in (wq, wk, wv)], axis=1)
        wb = jnp.concatenate([w[:, HALF:] for w in (wq, wk, wv)], axis=1)
        vecs = lax.all_gather(vectors, "fsdp", axis=0).reshape(grid.owners, 4, grid.rows)
        attn_in = (rms_parts(xin)[0] * vecs[:, 0].reshape(D).astype(f32)).astype(bf16)
        left = attn_in.T
        scale_row = jnp.concatenate([scale_half[0], jnp.ones((2 * HALF,), f32)])
        attended, *kept_a = attend_forward(0, lengths, (nn(attn_in, wa) * scale_row).astype(bf16))
        attended, *kept_b = attend_forward(1, lengths, (nn(attn_in, wb) * scale_row).astype(bf16), attended)
    kept = (kept_a, kept_b)
    gain_a, gain_m, bias_up, bias_down = (vecs[:, i].reshape(D).astype(f32) for i in range(4))

    hidden1 = xin + nn(attended, wo)
    normed2, inverse2 = rms_parts(hidden1)
    mlp_in = (normed2 * gain_m).astype(bf16)
    pre = nn(mlp_in, w_up) + bias_up
    sigma = jax.nn.sigmoid(pre)
    act = (pre * sigma).astype(bf16)

    valid = (jnp.arange(SEQ, dtype=jnp.int32) < lengths[0]).reshape(-1, 1).astype(f32)
    grad_out = cotangent.astype(f32) * valid
    grad_out_low = grad_out.astype(bf16)
    down_bias_grad = jnp.sum(grad_out, axis=0)
    grad_pre = (nt(grad_out_low, w_down) * (sigma * (1.0 + pre * (1.0 - sigma)))).astype(bf16)
    up_bias_grad = jnp.sum(grad_pre.astype(f32), axis=0)
    grad_mlp_in = nt(grad_pre, w_up)
    grad_hidden = grad_out + rms_back(grad_mlp_in * gain_m, normed2, inverse2)
    grad_proj = grad_hidden.astype(bf16)
    grad_att = nt(grad_proj, wo).astype(bf16)

    fac_row = jnp.broadcast_to(jnp.pad(factor, (0, LANES - HD))[None], (8, LANES))
    owned = (grid.owners, grid.rows)

    def scattered(grad):
        return lax.psum_scatter(grad, "fsdp", scatter_dimension=0, tiled=True)

    down_grad = tn(act, grad_out_low).astype(bf16)
    part_down = scattered(down_grad)
    up_grad = tn(mlp_in, grad_pre).astype(bf16)
    part_up = scattered(up_grad)
    grad_att = after(grad_att, up_grad, down_grad)
    part_o = tn(attended, grad_proj).astype(bf16)
    back_a, scale_a = attend_backward(0, fac_row, *kept[0], attended, grad_att)
    if grid.pieced:
        mine_a, theirs_a = weight_grads(
            grid, place, left, back_a, [up_bias_grad.reshape(owned), down_bias_grad.reshape(owned)]
        )
        recv_a = grid.other_core(theirs_a)
        part_o = tn(attended, after(grad_proj, mine_a)).astype(bf16)
        a1 = fold_cores(grid, place, mine_a, after(recv_a, part_o))
        ra1 = (grid.across(a1[0], 1), grid.across(a1[2], 2))
        grad_att = after(grad_att, a1[0])
    part_o = scattered(part_o)
    back_b, scale_b = attend_backward(1, fac_row, *kept[1], attended, grad_att)
    scale_part = (scale_a + scale_b)[0, :HD] / (query_scale.astype(f32) * LOG2E)

    if grid.pieced:
        scale_rows = jnp.broadcast_to(jnp.pad(scale_part, (0, grid.rows - HD))[None], owned)
        mine_b, theirs_b = weight_grads(grid, place, left, after(back_b, *ra1), [scale_rows])
        recv_b = grid.other_core(theirs_b)
        a2 = fold_first(grid, place, a1[1], after(ra1[0], mine_b), a1[3], ra1[1])
        ra2 = (grid.across(a2[0], 2), grid.across(a2[2], 1))
        b1 = fold_cores(grid, place, mine_b, after(recv_b, a2[0]))
        rb1 = (grid.across(b1[0], 1), grid.across(b1[2], 2))
        late = jnp.concatenate(after([part_o, part_up, part_down], b1[0]))
        summed = lax.psum(late, "replica").astype(f32)
        input_grad = input_grad_of(tokens, gain_a, after(grad_hidden, b1[0], late), (back_a, back_b), (wa, wb))
        a3 = fold_second(grid, place, a2[1], after(ra2[0], input_grad), a2[3], ra2[1])
        ra3 = [grid.along_z(a3[s], s) for s in range(1, grid.planes)]
        b2 = fold_first(grid, place, b1[1], after(rb1[0], a3[0]), b1[3], rb1[1])
        rb2 = (grid.across(b2[0], 2), grid.across(b2[2], 1))
        act = after(act, b2[0])
        out_f = (hidden1 + nn(act, w_down) + bias_down).astype(bf16)
        a4 = fold_planes(grid, a3[0], *after(ra3, out_f))
        a5 = [a4] + [grid.across(a4, code) for code in (1, 2, 3)]
        b3 = fold_second(grid, place, b2[1], after(rb2[0], a4), b2[3], rb2[1])
        rb3 = [grid.along_z(b3[s], s) for s in range(1, grid.planes)]
        b4 = fold_planes(grid, b3[0], *after(rb3, summed))
        b5 = [b4] + [grid.across(b4, code) for code in (1, 2, 3)]
        g_q, g_k, g_v, tail = finish(grid, place, [a5, b5])
        g_o, g_up, g_down = (summed[i * grid.rows : (i + 1) * grid.rows] for i in range(3))
        g_up_bias, g_down_bias = tail[0, : grid.rows], tail[1, : grid.rows]
        scale_grad = tail[0, HALF : HALF + HD]
    else:
        out_f = (hidden1 + nn(act, w_down) + bias_down).astype(bf16)
        input_grad = input_grad_of(tokens, gain_a, grad_hidden, (back_a, back_b), (wa, wb))
        joined = [
            jnp.concatenate([g[:, w * HALF : (w + 1) * HALF] for g in (back_a, back_b)], axis=1) for w in range(3)
        ]
        g_o, g_up, g_down, g_q, g_k, g_v, g_up_bias, g_down_bias = (
            lax.psum(g.astype(f32), "replica")
            for g in (
                part_o,
                part_up,
                part_down,
                *[scattered(tn(attn_in, g).astype(bf16)) for g in joined],
                scattered(up_bias_grad),
                scattered(down_bias_grad),
            )
        )
        scale_grad = lax.psum(scale_part, ("replica", "fsdp"))

    def weighed(*pairs):
        return sum(jnp.sum(w.astype(f32) * g, axis=1) for w, g in pairs)

    g_attn_gain = weighed((query_weight, g_q), (key_weight, g_k), (value_weight, g_v)) / attn_gain.astype(f32)
    g_mlp_gain = weighed((up_weight, g_up)) / mlp_gain.astype(f32)
    sums = (g_q, g_k, g_v, g_o, g_up, g_down, g_attn_gain, g_mlp_gain, g_up_bias, g_down_bias)
    return (out_f, input_grad, *sums, scale_grad)


def solution(mesh):
    split = P(("replica", "fsdp"), None)
    rows = P("fsdp", None)
    part = P("fsdp")
    return jax.shard_map(
        functools.partial(shards, Grid(mesh.shape)),
        mesh=mesh,
        in_specs=(split, P(("replica", "fsdp")), split, *[rows] * 6, *[part] * 4, P()),
        out_specs=(split, split, *[rows] * 6, *[part] * 4, P()),
        check_vma=False,
    )
```

```python
import functools
import math

import jax
import jax.numpy as jnp
from jax import lax
from jax.experimental import pallas as pl
from jax.experimental.pallas import tpu as pltpu
from jax.sharding import PartitionSpec as P

D = 1280
HEADS = 16
HD = 80
FF = 1280
SEQ = 1024
EPS = 1e-06
LOG2E = math.log2(math.e)
NEG = -1e30
LANES = 128
BLOCK = 256
GROUP = 8
HALF = GROUP * HD
TRIPLE = 3 * HALF
VMEM_LIMIT = 58 << 20
SHORT = 40

bf16 = jnp.bfloat16
f32 = jnp.float32


def rms_parts(v):
    inverse = lax.rsqrt(jnp.mean(v * v, axis=-1, keepdims=True) + EPS)
    return (v * inverse, inverse)


def rms_back(grad_n, normed, inverse):
    return inverse * (grad_n - normed * jnp.mean(grad_n * normed, axis=-1, keepdims=True))


def nt(a, b):
    return lax.dot_general(a, b, (((1,), (1,)), ((), ())), preferred_element_type=f32)


def nn(a, b):
    return lax.dot_general(a, b, (((1,), (0,)), ((), ())), preferred_element_type=f32)


def tn(a, b):
    return lax.dot_general(a, b, (((0,), (0,)), ((), ())), preferred_element_type=f32)


def widen(v):
    return jnp.pad(v, ((0, 0), (0, LANES - HD)))


def split3(v):
    a = v.astype(bf16).astype(f32)
    b = (v - a).astype(bf16).astype(f32)
    c = (v - a - b).astype(bf16).astype(f32)
    return a, b, c


def extra_lanes(lane, base, extra):
    out = jnp.zeros_like(base)
    for place, value in reversed(list(enumerate(extra))):
        out = jnp.where(lane == HD + place, value, out)
    return jnp.where(lane < HD, base, out)


def forward_kernel(heads, len_ref, qkv_ref, o_ref, qa_ref, ka_ref, va_ref):
    length = len_ref[0]
    lane = lax.broadcasted_iota(jnp.int32, (SEQ, LANES), 1)
    row = lax.broadcasted_iota(jnp.int32, (SEQ, LANES), 0)
    mask = jnp.where(row < length, 0.0, NEG)
    k_pad = jnp.where(lane == HD, mask, jnp.where((lane > HD) & (lane < HD + 4), 1.0, 0.0)).astype(bf16)
    v_pad = jnp.where((lane >= HD) & (lane < HD + 3), 1.0, 0.0).astype(bf16)
    q_pad = jnp.where(lane == HD, 1.0, 0.0).astype(bf16)
    in_head = lane < HD
    block_lane = lane[:BLOCK]
    block_row = lax.broadcasted_iota(jnp.int32, (LANES, BLOCK), 0)
    causal = lax.broadcasted_iota(jnp.int32, (BLOCK, BLOCK), 0) <= lax.broadcasted_iota(
        jnp.int32, (BLOCK, BLOCK), 1
    )
    blocks = SEQ // BLOCK

    def prepare(h):
        for n, (ref, pad) in enumerate(((qa_ref, q_pad), (ka_ref, k_pad), (va_ref, v_pad))):
            at = n * HALF + h * HD
            ref[h] = jnp.where(in_head, widen(qkv_ref[:, at : at + HD]), pad)

    def scores(h, i):
        return nt(ka_ref[h, : (i + 1) * BLOCK, :], qa_ref[h, i * BLOCK : (i + 1) * BLOCK, :])

    def attend(h, i, st):
        before = i * BLOCK
        diagonal = jnp.where(causal, st[before:], NEG)
        top = jnp.max(diagonal, axis=0, keepdims=True)
        if i:
            top = jnp.maximum(top, jnp.max(st[:before], axis=0, keepdims=True))
        p = jnp.exp2(diagonal - top).astype(bf16)
        if i:
            p = jnp.concatenate([jnp.exp2(st[:before] - top).astype(bf16), p], axis=0)
        return tn(va_ref[h, : before + BLOCK, :], p), top

    def finish(h, i, ot, top):
        rows = slice(i * BLOCK, (i + 1) * BLOCK)
        total = ot[HD : HD + 1]
        a, b, c = split3(-(top + jnp.log2(total)))
        scaled = jnp.where(block_row < HD, ot / total, 0.0)
        for place, value in ((1, a), (2, b), (3, c)):
            scaled = jnp.where(block_row == HD + place, value, scaled)
        o = scaled.T
        o_ref[rows, h * HD : (h + 1) * HD] = o[:, :HD].astype(bf16)
        qa_ref[h, rows, :] = jnp.where(block_lane <= HD, qa_ref[h, rows, :].astype(f32), o).astype(bf16)

    for h in range(heads):
        prepare(h)
    scored, done = [], []
    for h, i in [(h, i) for h in range(heads) for i in range(blocks)] + [(None, None)] * 2:
        if h is not None:
            scored.append((h, i, scores(h, i)))
        if len(scored) > 1 or (h is None and scored):
            hh, ii, st = scored.pop(0)
            done.append((hh, ii, *attend(hh, ii, st)))
        if len(done) > 1 or (h is None and not scored and done):
            finish(*done.pop(0))
    while done:
        finish(*done.pop(0))


def attend_forward(half, lengths, qkv, before=None):
    wide = pl.BlockSpec((GROUP, SEQ, LANES), lambda g: (0, 0, 0))
    kept = [] if before is None else [before]

    def kernel(len_ref, qkv_ref, *refs):
        forward_kernel(GROUP, len_ref, qkv_ref, *refs[len(kept) :])

    return pl.pallas_call(
        kernel,
        grid=(1,),
        in_specs=[pl.BlockSpec(memory_space=pltpu.SMEM), pl.BlockSpec((SEQ, TRIPLE), lambda g: (0, 0))]
        + [pl.BlockSpec(memory_space=pl.ANY)] * len(kept),
        out_specs=[pl.BlockSpec((SEQ, HALF), lambda g: (0, half)), wide, wide, wide],
        out_shape=[jax.ShapeDtypeStruct((SEQ, D), bf16)]
        + [jax.ShapeDtypeStruct((GROUP, SEQ, LANES), bf16)] * 3,
        input_output_aliases={2: 0} if kept else {},
        compiler_params=pltpu.CompilerParams(vmem_limit_bytes=VMEM_LIMIT),
        cost_estimate=pl.CostEstimate(
            flops=GROUP * SEQ * SEQ * 1200 // SHORT, bytes_accessed=0, transcendentals=0
        ),
        name="attend_forward",
    )(lengths, qkv, *kept)


def backward_kernel(
    heads, fac_ref, qa_ref, ka_ref, va_ref, o_ref, g_ref, d_ref, sg_ref, dqs, gs
):
    lane = lax.broadcasted_iota(jnp.int32, (SEQ, LANES), 1)
    causal = lax.broadcasted_iota(jnp.int32, (BLOCK, BLOCK), 0) <= lax.broadcasted_iota(
        jnp.int32, (BLOCK, BLOCK), 1
    )
    fac = fac_ref[0:1, :]
    blocks = SEQ // BLOCK

    @pl.when(pl.program_id(0) == 0)
    def _():
        sg_ref[...] = jnp.zeros_like(sg_ref)

    sums = []

    def prepare(h):
        own = slice(h * HD, (h + 1) * HD)
        g = widen(g_ref[:, own]).astype(f32)
        o = widen(o_ref[:, own]).astype(f32)
        delta = jnp.sum(g * o, axis=1, keepdims=True)
        gs[h] = extra_lanes(lane, g, split3(-delta)).astype(bf16)

    def products(h, j):
        js = slice(j * BLOCK, (j + 1) * BLOCK)
        return nt(ka_ref[h, js, :], qa_ref[h, j * BLOCK :, :]), nt(va_ref[h, js, :], gs[h, j * BLOCK :, :])

    def middle(j, st, dpt):
        p = jnp.exp2(st)
        diagonal = jnp.where(causal, p[:, :BLOCK], 0.0)
        p = jnp.concatenate([diagonal, p[:, BLOCK:]], axis=1) if j < blocks - 1 else diagonal
        return (p * dpt).astype(bf16), p.astype(bf16)

    def finish(h, j, ds, p):
        own, dk, dv = (slice(n * HALF + h * HD, n * HALF + (h + 1) * HD) for n in range(3))
        js = slice(j * BLOCK, (j + 1) * BLOCK)
        d_ref[js, dv] = nn(p, gs[h, j * BLOCK :, :])[:, :HD].astype(bf16)
        d_ref[js, dk] = (nn(ds, qa_ref[h, j * BLOCK :, :])[:, :HD] * (1.0 / LOG2E)).astype(bf16)
        dqt = tn(ka_ref[h, js, :], ds)
        if j == 0:
            dqs[h % 2] = dqt
        else:
            dqs[h % 2, :, j * BLOCK :] += dqt
        if j == blocks - 1:
            dq = dqs[h % 2].T.astype(bf16).astype(f32)
            sums.append(jnp.sum(dq * qa_ref[h].astype(f32), axis=0, keepdims=True))
            d_ref[:, own] = (dq * fac)[:, :HD].astype(bf16)

    for h in range(heads):
        prepare(h)
    waiting = []
    for h, j in [(h, j) for h in range(heads) for j in range(blocks)]:
        waiting.append((h, j, *products(h, j)))
        if len(waiting) > 1:
            hh, jj, st, dpt = waiting.pop(0)
            finish(hh, jj, *middle(jj, st, dpt))
    hh, jj, st, dpt = waiting.pop(0)
    finish(hh, jj, *middle(jj, st, dpt))
    sg_ref[0:1, :] += sum(sums)


def attend_backward(half, fac, qa, ka, va, o, g):
    part = pl.BlockSpec((SEQ, HALF), lambda g: (0, half))
    wide = pl.BlockSpec((GROUP, SEQ, LANES), lambda g: (0, 0, 0))
    full = pl.BlockSpec((8, LANES), lambda g: (0, 0))
    return pl.pallas_call(
        functools.partial(backward_kernel, GROUP),
        grid=(1,),
        in_specs=[full, wide, wide, wide, part, part],
        out_specs=[pl.BlockSpec((SEQ, TRIPLE), lambda g: (0, 0)), full],
        out_shape=[jax.ShapeDtypeStruct((SEQ, TRIPLE), bf16), jax.ShapeDtypeStruct((8, LANES), f32)],
        scratch_shapes=[pltpu.VMEM((2, LANES, SEQ), f32), pltpu.VMEM((GROUP, SEQ, LANES), bf16)],
        compiler_params=pltpu.CompilerParams(vmem_limit_bytes=VMEM_LIMIT),
        cost_estimate=pl.CostEstimate(
            flops=GROUP * SEQ * SEQ * 2400 // SHORT, bytes_accessed=0, transcendentals=0
        ),
        name="attend_backward",
    )(fac, qa, ka, va, o, g)


class Grid:
    def __init__(self, mesh_shape):
        self.copies, self.owners = mesh_shape["replica"], mesh_shape["fsdp"]
        self.planes = self.owners // 2
        self.rows = D // self.owners

    @property
    def pieced(self):
        return self.copies == 4 and self.owners == 8

    def place(self):
        me, copy = lax.axis_index("fsdp"), lax.axis_index("replica")
        return copy // 2, copy % 2, me // 2, me % 2

    def along_z(self, v, step):
        n = self.planes
        pairs = [(i, (i // 2 + step) % n * 2 + i % 2) for i in range(self.owners)]
        return lax.ppermute(v, "fsdp", pairs)

    def other_core(self, v):
        return lax.ppermute(v, "fsdp", [(i, i ^ 1) for i in range(self.owners)])

    def across(self, v, code):
        return lax.ppermute(v, "replica", [(i, i ^ code) for i in range(self.copies)])


def kernel_call(kernel, name, operands, outs, scratch=(), flops=0, nbytes=0, **more):
    return pl.pallas_call(
        kernel,
        out_shape=outs,
        scratch_shapes=scratch,
        compiler_params=pltpu.CompilerParams(vmem_limit_bytes=VMEM_LIMIT),
        cost_estimate=pl.CostEstimate(flops=flops // SHORT, bytes_accessed=nbytes // SHORT, transcendentals=0),
        name=name,
        **more,
    )(*operands)


def piece_copies(planes, quarter, place_ref, refs, buf, sem):
    y, x, z, core = (place_ref[i] for i in range(4))
    groups = []
    for s, (source, c) in enumerate(((refs[:5], core), (refs[5:10], 1 - core))):
        block, *pieces = source
        home = 2 * z + c
        groups.append((home, [pltpu.make_async_copy(block, buf.at[home], sem.at[s, 0, 0])]))
        for d in range(1, planes):
            owner = 2 * lax.rem(z - d + planes, planes) + c
            copies = []
            for code, piece in enumerate(pieces):
                py = 1 - y if code >= 2 else y
                px = 1 - x if code % 2 else x
                at = pl.multiple_of((2 * py + px) * quarter, 16)
                copies.append(
                    pltpu.make_async_copy(piece.at[d - 1], buf.at[owner, pl.ds(at, quarter), :], sem.at[s, d, code])
                )
            groups.append((owner, copies))
    return groups


def project_kernel(planes, rows, quarter, first, place_ref, scale_ref, x_ref, *refs):
    outs, scratch = refs[10 : 10 + (5 if first else 2)], refs[10 + (5 if first else 2) :]
    qkv_ref, whole_ref = outs[:2]
    buf, sem_in, sem_out = scratch[:3]
    groups = piece_copies(planes, quarter, place_ref, refs, buf, sem_in)
    for _, copies in groups:
        for copy in copies:
            copy.start()
    if first:
        held = scratch[3]
        for at in range(0, SEQ, BLOCK):
            held[at : at + BLOCK, :] = rms_parts(x_ref[at : at + BLOCK, :].astype(f32))[0]
    written = []
    for g, (owner, copies) in enumerate(groups):
        for copy in copies:
            copy.wait()
        at = pl.multiple_of(owner * rows, 16)
        for t in range(3):
            copy = pltpu.make_async_copy(
                buf.at[owner, pl.ds(t * rows, rows), :],
                whole_ref.at[pl.ds(at, rows), pl.ds(t * HALF, HALF)],
                sem_out.at[g, t],
            )
            copy.start()
            written.append(copy)
    if first:
        vec_ref, attn_in, left_ref = outs[2:5]
        vec_ref[...] = buf[:, 3 * rows : 3 * rows + 16, :]
        gain = jnp.concatenate([buf[b, 3 * rows : 3 * rows + 16, :rows][0:1] for b in range(2 * planes)], axis=1)
        gain = gain.astype(f32)
        for at in range(0, SEQ, BLOCK):
            attn_in[at : at + BLOCK, :] = (held[at : at + BLOCK, :] * gain).astype(bf16)
    else:
        attn_in = x_ref
    for t in range(3):
        weight = buf[:, t * rows : (t + 1) * rows, :].reshape(D, HALF)
        result = nn(attn_in[...], weight)
        qkv_ref[:, t * HALF : (t + 1) * HALF] = (result * scale_ref[0:1, :] if t == 0 else result).astype(bf16)
    if first:
        left_ref[...] = attn_in[...].T
    for copy in written:
        copy.wait()


def project(grid, place, scale, x, pieces, first):
    total = pieces[0].shape[0]
    vmem, hbm = pl.BlockSpec(memory_space=pltpu.VMEM), pl.BlockSpec(memory_space=pl.ANY)
    outs = [jax.ShapeDtypeStruct((SEQ, TRIPLE), bf16), jax.ShapeDtypeStruct((D, TRIPLE), bf16)]
    scratch = [
        pltpu.VMEM((grid.owners, total, HALF), bf16),
        pltpu.SemaphoreType.DMA((2, grid.planes, 4)),
        pltpu.SemaphoreType.DMA((grid.owners, 3)),
    ]
    if first:
        outs += [
            jax.ShapeDtypeStruct((grid.owners, 16, HALF), bf16),
            jax.ShapeDtypeStruct((SEQ, D), bf16),
            jax.ShapeDtypeStruct((D, SEQ), bf16),
        ]
        scratch.append(pltpu.VMEM((SEQ, D), f32))
    return kernel_call(
        functools.partial(project_kernel, grid.planes, grid.rows, total // 4, first),
        "project",
        (place, scale, x, *pieces),
        outs,
        scratch=scratch,
        flops=2 * SEQ * D * TRIPLE,
        nbytes=4 * D * TRIPLE + 2 * SEQ * (D + TRIPLE),
        in_specs=[pl.BlockSpec(memory_space=pltpu.SMEM), vmem, vmem] + [hbm] * 10,
        out_specs=[vmem, hbm] + [vmem] * 3 * first,
    )


def cut_kernel(rows, place_ref, *refs):
    weights, vec_ref = refs[:6], refs[6]
    chunks, pieces = refs[7:10], refs[10:13]
    for half in range(2):
        for t in range(3):
            chunks[half][t * rows : (t + 1) * rows, :] = weights[t][:, half * HALF : (half + 1) * HALF]
        chunks[half][3 * rows :, :] = vec_ref[...]
    for t in range(6):
        w, half = 3 + t // 2, t % 2
        chunks[2][t * rows : (t + 1) * rows, :] = weights[w][:, half * HALF : (half + 1) * HALF]
    copy = 2 * place_ref[0] + place_ref[1]
    for chunk, piece in zip(chunks, pieces, strict=True):
        quarter = piece.shape[0]
        piece[...] = chunk[pl.ds(pl.multiple_of(copy * quarter, 16), quarter), :]


def cut(grid, place, weights, vectors):
    rows = [512, 512, 6 * grid.rows]
    vec = jnp.pad(vectors.reshape(1, HALF), ((0, 512 - 3 * grid.rows - 1), (0, 0)))
    out = kernel_call(
        functools.partial(cut_kernel, grid.rows),
        "cut",
        (place, *weights, vec),
        [jax.ShapeDtypeStruct((n, HALF), bf16) for n in rows]
        + [jax.ShapeDtypeStruct((n // 4, HALF), bf16) for n in rows],
        nbytes=12 * grid.rows * D * 2,
        in_specs=[pl.BlockSpec(memory_space=pltpu.SMEM)] + [pl.BlockSpec(memory_space=pltpu.VMEM)] * 7,
    )
    return out[:3], out[3:]


def chunk_across(grid, along):
    return [along] + [grid.across(along, code) for code in (1, 2, 3)]


def both_cores(grid, own):
    return own + [grid.other_core(v) for v in own]


def in_blocks():
    return [slice(at, at + BLOCK) for at in range(0, SEQ, BLOCK)]


def mlp_forward_kernel(planes, rows, quarter, place_ref, gain_ref, bias_ref, *refs):
    attended_ref, token_ref, grad_ref = refs[10:13]
    weights, (hidden_ref, mlp_in_ref, pre_ref, act_ref, down_grad_ref) = refs[13:16], refs[16:21]
    buf, attended, token, grad, hidden, mlp_in, pre, act, down_grad, sem_in, sem_out, sem = refs[21:]
    loads = [
        pltpu.make_async_copy(source, target, sem.at[n])
        for n, (source, target) in enumerate(((attended_ref, attended), (token_ref, token), (grad_ref, grad)))
    ]
    groups = piece_copies(planes, quarter, place_ref, refs, buf, sem_in)
    for _, copies in groups:
        for copy in copies:
            copy.start()
    for load in loads:
        load.start()
    written = []

    def keep(source, target, n):
        copy = pltpu.make_async_copy(source, target, sem.at[n])
        copy.start()
        written.append(copy)

    for g, (owner, copies) in enumerate(groups):
        for copy in copies:
            copy.wait()
        at = pl.multiple_of(owner * rows, 16)
        for t in range(6):
            copy = pltpu.make_async_copy(
                buf.at[owner, pl.ds(t * rows, rows), :],
                weights[t // 2].at[pl.ds(at, rows), pl.ds(t % 2 * HALF, HALF)],
                sem_out.at[g, t],
            )
            copy.start()
            written.append(copy)
    for load in loads:
        load.wait()

    def tile(t):
        return buf[:, t * rows : (t + 1) * rows, :].reshape(D, HALF)

    halves = (slice(0, HALF), slice(HALF, D))
    for h, across in enumerate(halves):
        hidden[:, across] = token[:, across].astype(f32) + nn(attended[...], tile(h))
    keep(hidden, hidden_ref, 3)
    for at in in_blocks():
        mlp_in[at, :] = (rms_parts(hidden[at, :])[0] * gain_ref[0:1, :]).astype(bf16)
    keep(mlp_in, mlp_in_ref, 4)
    for h, across in enumerate(halves):
        value = nn(mlp_in[...], tile(2 + h)) + bias_ref[0:1, across]
        pre[:, across] = value
        act[:, across] = (value * jax.nn.sigmoid(value)).astype(bf16)
    keep(pre, pre_ref, 5)
    keep(act, act_ref, 6)
    down_grad[...] = tn(act[...], grad[...]).astype(bf16)
    keep(down_grad, down_grad_ref, 7)
    for copy in written:
        copy.wait()


def mlp_forward(grid, place, gain, bias, pieces, attended, tokens, grad_out_low):
    total = pieces[0].shape[0]
    vmem, hbm = pl.BlockSpec(memory_space=pltpu.VMEM), pl.BlockSpec(memory_space=pl.ANY)
    low, high, square = ((SEQ, D), bf16), ((SEQ, D), f32), ((D, D), bf16)
    outs = [square] * 3 + [high, low, high, low, square]
    return kernel_call(
        functools.partial(mlp_forward_kernel, grid.planes, grid.rows, total // 4),
        "mlp_forward",
        (place, row_of(gain), row_of(bias), *pieces, attended, tokens, grad_out_low),
        [jax.ShapeDtypeStruct(*o) for o in outs],
        scratch=[
            pltpu.VMEM((grid.owners, total, HALF), bf16),
            *[pltpu.VMEM(*v) for v in (low, low, low, high, low, high, low, square)],
            pltpu.SemaphoreType.DMA((2, grid.planes, 4)),
            pltpu.SemaphoreType.DMA((grid.owners, 6)),
            pltpu.SemaphoreType.DMA((8,)),
        ],
        flops=6 * SEQ * D * D,
        nbytes=16 * D * D + 22 * SEQ * D,
        in_specs=[pl.BlockSpec(memory_space=pltpu.SMEM), vmem, vmem] + [hbm] * 13,
        out_specs=[hbm] * 8,
    )


def row_of(v):
    return jnp.broadcast_to(v[None], (8, v.shape[0]))


def mlp_backward_kernel(gain_ref, *refs):
    grad_ref, down_ref, pre_ref, mlp_in_ref, up_ref, hidden_ref, output_ref, attended_ref = refs[:8]
    up_grad_ref, grad_hidden_ref, grad_att_ref, output_grad_ref, sums_ref = refs[8:13]
    grad, down, wide, mlp_in, up, hidden, output, attended, grad_pre, grad_proj, first, second, sem = refs[13:]
    loads = {}
    for n, (name, source, target) in enumerate(
        (
            ("grad", grad_ref, grad),
            ("down", down_ref, down),
            ("pre", pre_ref, wide),
            ("mlp_in", mlp_in_ref, mlp_in),
            ("up", up_ref, up),
            ("hidden", hidden_ref, hidden),
            ("output", output_ref, output),
            ("attended", attended_ref, attended),
        )
    ):
        loads[name] = pltpu.make_async_copy(source, target, sem.at[n])
        loads[name].start()
    written = []

    def keep(source, target):
        copy = pltpu.make_async_copy(source, target, sem.at[8 + len(written)])
        copy.start()
        written.append(copy)

    for name in ("grad", "down", "pre"):
        loads[name].wait()
    sums = jnp.zeros((1, D), f32)
    for at in in_blocks():
        pre = wide[at, :]
        sigma = jax.nn.sigmoid(pre)
        value = (nt(grad[at, :], down[...]) * (sigma * (1.0 + pre * (1.0 - sigma)))).astype(bf16)
        grad_pre[at, :] = value
        sums = sums + jnp.sum(value.astype(f32), axis=0, keepdims=True)
    sums_ref[...] = jnp.zeros_like(sums_ref)
    sums_ref[0:1, :] = sums
    sums_ref[1:2, :] = jnp.sum(grad[...].astype(f32), axis=0, keepdims=True)
    for name in ("mlp_in", "up", "hidden"):
        loads[name].wait()
    first[...] = tn(mlp_in[...], grad_pre[...]).astype(bf16)
    keep(first, up_grad_ref)
    for at in in_blocks():
        normed, inverse = rms_parts(hidden[at, :])
        back = rms_back(nt(grad_pre[at, :], up[...]) * gain_ref[0:1, :], normed, inverse)
        value = grad[at, :].astype(f32) + back
        wide[at, :] = value
        grad_proj[at, :] = value.astype(bf16)
    keep(wide, grad_hidden_ref)
    for name in ("output", "attended"):
        loads[name].wait()
    for at in in_blocks():
        mlp_in[at, :] = nt(grad_proj[at, :], output[...]).astype(bf16)
    keep(mlp_in, grad_att_ref)
    second[...] = tn(attended[...], grad_proj[...]).astype(bf16)
    keep(second, output_grad_ref)
    for copy in written:
        copy.wait()


def mlp_backward(gain, grad_out_low, w_down, pre, mlp_in, w_up, hidden1, w_out, attended):
    hbm = pl.BlockSpec(memory_space=pl.ANY)
    low, high, square = ((SEQ, D), bf16), ((SEQ, D), f32), ((D, D), bf16)
    up_grad, grad_hidden, grad_att, output_grad, sums = kernel_call(
        mlp_backward_kernel,
        "mlp_backward",
        (row_of(gain), grad_out_low, w_down, pre, mlp_in, w_up, hidden1, w_out, attended),
        [jax.ShapeDtypeStruct(*o) for o in (square, high, low, square, ((8, D), f32))],
        scratch=[
            *[pltpu.VMEM(*v) for v in (low, square, high, low, square, high, square, low, low, low, square, square)],
            pltpu.SemaphoreType.DMA((12,)),
        ],
        flops=10 * SEQ * D * D,
        nbytes=10 * D * D + 26 * SEQ * D,
        in_specs=[pl.BlockSpec(memory_space=pltpu.VMEM)] + [hbm] * 8,
        out_specs=[hbm] * 4 + [pl.BlockSpec(memory_space=pltpu.VMEM)],
    )
    return up_grad, output_grad, grad_hidden, grad_att, sums[0], sums[1]


def weight_grad_kernel(planes, rows, place_ref, left_ref, right_ref, vec_ref, mine, theirs, left, right, stage, sem_in, sem_out):
    core = place_ref[3]
    loads = [pltpu.make_async_copy(left_ref, left, sem_in.at[3])]
    for w in range(3):
        part = pl.ds(w * HALF, HALF)
        loads.append(pltpu.make_async_copy(right_ref.at[:, part], right.at[:, part], sem_in.at[w]))
    for load in loads:
        load.start()
    written = []

    def send(w, source, size, c, whole, z):
        copy = pltpu.make_async_copy(source, whole.at[z, pl.ds(w * rows, size), :], sem_out.at[w, c, z])
        copy.start()
        written.append(copy)

    sides = ((1, theirs), (0, mine))
    owner = {(c, z): 2 * z + (1 - core if c else core) for c in range(2) for z in range(planes)}
    for c, whole in sides:
        for z in range(planes):
            send(3, vec_ref.at[owner[c, z]], 32, c, whole, z)
    loads[0].wait()
    for w in range(3):
        loads[1 + w].wait()
        stage[w] = nn(left[...], right[:, w * HALF : (w + 1) * HALF]).astype(bf16)
        for c, whole in sides:
            for z in range(planes):
                at = pl.multiple_of(owner[c, z] * rows, 16)
                send(w, stage.at[w, pl.ds(at, rows), :], rows, c, whole, z)
    for copy in written:
        copy.wait()


def weight_grads(grid, place, left, right, vectors):
    rows = jnp.stack(vectors, axis=1).astype(bf16)
    rows = jnp.pad(rows, ((0, 0), (0, 32 - len(vectors)), (0, HALF - grid.rows)))
    shape = jax.ShapeDtypeStruct((grid.planes, 512, HALF), bf16)
    hbm = pl.BlockSpec(memory_space=pl.ANY)
    return kernel_call(
        functools.partial(weight_grad_kernel, grid.planes, grid.rows),
        "weight_grads",
        (place, left, right, rows),
        [shape, shape],
        scratch=[
            pltpu.VMEM((D, SEQ), bf16),
            pltpu.VMEM((SEQ, TRIPLE), bf16),
            pltpu.VMEM((3, D, HALF), bf16),
            pltpu.SemaphoreType.DMA((4,)),
            pltpu.SemaphoreType.DMA((4, 2, grid.planes)),
        ],
        flops=2 * SEQ * D * TRIPLE,
        nbytes=(SEQ * D + (SEQ + D) * TRIPLE) * 2,
        in_specs=[pl.BlockSpec(memory_space=pltpu.SMEM), hbm, hbm, pl.BlockSpec(memory_space=pltpu.VMEM)],
        out_specs=[hbm, hbm],
    )


def added(a, b):
    return (a.astype(f32) + b.astype(f32)).astype(bf16)


def fold_cores_kernel(place_ref, a_ref, b_ref, send_low, keep_low, send_high, keep_high):
    y, x = place_ref[0], place_ref[1]
    for p in range(2):
        send_low[0, p] = added(a_ref[0, p, 1 - x, 0], b_ref[0, p, 1 - x, 0])
        keep_low[0, p] = added(a_ref[0, p, x, 0], b_ref[0, p, x, 0])
        send_high[0, p] = added(a_ref[0, 1 - y, p, 1], b_ref[0, 1 - y, p, 1])
        keep_high[0, p] = added(a_ref[0, y, p, 1], b_ref[0, y, p, 1])


def fold_cores(grid, place, a, b):
    n, columns = grid.planes, a.shape[2]
    split = (n, 2, 2, 2, 64, columns)
    block = pl.BlockSpec((1, *split[1:]), lambda i: (i, 0, 0, 0, 0, 0))
    out = pl.BlockSpec((1, 2, 64, columns), lambda i: (i, 0, 0, 0))
    return kernel_call(
        fold_cores_kernel,
        "fold_cores",
        (place, a.reshape(split), b.reshape(split)),
        [jax.ShapeDtypeStruct((n, 2, 64, columns), bf16)] * 4,
        nbytes=a.size * 6,
        grid=(n,),
        in_specs=[pl.BlockSpec(memory_space=pltpu.SMEM), block, block],
        out_specs=[out] * 4,
    )


def fold_first_kernel(place_ref, low_a, low_b, high_a, high_b, send_low, keep_low, send_high, keep_high):
    y, x = place_ref[0], place_ref[1]
    send_low[0] = added(low_a[0, 1 - y], low_b[0, 1 - y])
    keep_low[0] = added(low_a[0, y], low_b[0, y])
    send_high[0] = added(high_a[0, 1 - x], high_b[0, 1 - x])
    keep_high[0] = added(high_a[0, x], high_b[0, x])


def fold_first(grid, place, *parts):
    n, columns = grid.planes, parts[0].shape[3]
    block = pl.BlockSpec((1, 2, 64, columns), lambda i: (i, 0, 0, 0))
    out = pl.BlockSpec((1, 64, columns), lambda i: (i, 0, 0))
    return kernel_call(
        fold_first_kernel,
        "fold_first",
        (place, *parts),
        [jax.ShapeDtypeStruct((n, 64, columns), bf16)] * 4,
        nbytes=parts[0].size * 12,
        grid=(n,),
        in_specs=[pl.BlockSpec(memory_space=pltpu.SMEM)] + [block] * 4,
        out_specs=[out] * 4,
    )


def fold_second_kernel(planes, place_ref, low_a, low_b, high_a, high_b, *outs):
    z = place_ref[2]
    for s in range(planes):
        at = lax.rem(z + s, planes)
        outs[s][0] = added(low_a[at], low_b[at])
        outs[s][1] = added(high_a[at], high_b[at])


def fold_second(grid, place, *parts):
    n, columns = grid.planes, parts[0].shape[2]
    return kernel_call(
        functools.partial(fold_second_kernel, n),
        "fold_second",
        (place, *parts),
        [jax.ShapeDtypeStruct((2, 64, columns), bf16)] * n,
        nbytes=parts[0].size * 12,
        in_specs=[pl.BlockSpec(memory_space=pltpu.SMEM)] + [pl.BlockSpec(memory_space=pltpu.VMEM)] * 4,
    )


def fold_planes_kernel(*refs):
    *parts, out = refs
    total = parts[0][...].astype(f32)
    for part in parts[1:]:
        total = total + part[...].astype(f32)
    out[...] = total.astype(bf16)


def fold_planes(grid, *parts):
    return kernel_call(
        fold_planes_kernel,
        "fold_planes",
        parts,
        jax.ShapeDtypeStruct(parts[0].shape, bf16),
        nbytes=parts[0].size * 10,
    )


def finish_kernel(units, rows, place_ref, *refs):
    me = 2 * place_ref[0] + place_ref[1]
    parts, outs, stage = refs[: 4 * units], refs[4 * units : -1], refs[-1]
    columns = parts[0].shape[2]
    for u in range(units):
        across = slice(u * columns, (u + 1) * columns)
        for r in range(4):
            for code in range(4):

                @pl.when(me == r ^ code)
                def _(r=r, code=code, u=u, across=across):
                    for h in range(2):
                        at = 128 * r + 64 * h
                        stage[at : at + 64, across] = parts[4 * u + code][h].astype(f32)

    for w in range(3):
        outs[w][...] = stage[w * rows : (w + 1) * rows, :]
    outs[3][...] = stage[3 * rows :, :]


def finish(grid, place, units):
    columns = units[0][0].shape[2] * len(units)
    parts = [part for unit in units for part in unit]
    return kernel_call(
        functools.partial(finish_kernel, len(units), grid.rows),
        "finish",
        (place, *parts),
        [jax.ShapeDtypeStruct((grid.rows, columns), f32)] * 3
        + [jax.ShapeDtypeStruct((512 - 3 * grid.rows, columns), f32)],
        scratch=[pltpu.VMEM((512, columns), f32)],
        nbytes=512 * columns * 6,
        in_specs=[pl.BlockSpec(memory_space=pltpu.SMEM)]
        + [pl.BlockSpec(memory_space=pltpu.VMEM)] * len(parts),
    )


def input_grad_kernel(x_ref, gain_ref, hidden_ref, grad_a, grad_b, weight_a, weight_b, out):
    total = nt(grad_a[...], weight_a[...]) + nt(grad_b[...], weight_b[...])
    normed, inverse = rms_parts(x_ref[...].astype(f32))
    out[...] = (hidden_ref[...] + rms_back(total * gain_ref[0:1, :], normed, inverse)).astype(bf16)


def input_grad_of(tokens, gain, grad_hidden, grads, weights):
    count, block = tokens.shape[0], BLOCK
    rows = pl.BlockSpec((block, D), lambda i: (i, 0))
    return kernel_call(
        input_grad_kernel,
        "input_grad",
        (tokens, jnp.broadcast_to(gain[None], (8, D)), grad_hidden, *grads, *weights),
        jax.ShapeDtypeStruct((count, D), bf16),
        flops=6 * count * D * D,
        nbytes=6 * D * D + 14 * count * D,
        grid=(count // block,),
        in_specs=[rows, pl.BlockSpec((8, D), lambda i: (0, 0)), rows]
        + [pl.BlockSpec((block, TRIPLE), lambda i: (i, 0))] * 2
        + [pl.BlockSpec((D, TRIPLE), lambda i: (0, 0))] * 2,
        out_specs=rows,
    )


def after(value, *first):
    return lax.optimization_barrier((value, first))[0]


def shards(
    grid,
    tokens,
    lengths,
    cotangent,
    query_weight,
    key_weight,
    value_weight,
    output_weight,
    up_weight,
    down_weight,
    attn_gain,
    mlp_gain,
    up_bias,
    down_bias,
    query_scale,
):
    assert lengths.shape[0] == 1 and tokens.shape[0] == SEQ
    vectors = jnp.concatenate([attn_gain, mlp_gain, up_bias, down_bias])
    y, x, z, core = grid.place()
    place = jnp.stack([y, x, z, core]).astype(jnp.int32)
    xin = tokens.astype(f32)
    factor = query_scale.astype(f32) * (1.0 / jnp.sqrt(f32(HD)))
    scale_half = row_of(jnp.tile(factor * LOG2E, GROUP))
    valid = (jnp.arange(SEQ, dtype=jnp.int32) < lengths[0]).reshape(-1, 1)
    grad_out_low = jnp.where(valid, cotangent, jnp.zeros_like(cotangent))
    if grid.pieced:
        weights = (query_weight, key_weight, value_weight, output_weight, up_weight, down_weight)
        chunks, cuts = cut(grid, place, weights, vectors)
        planes = range(1, grid.planes)
        z1 = [grid.along_z(cuts[0], d) for d in planes]
        z2 = [grid.along_z(after(cuts[1], *z1), d) for d in planes]
        across1 = chunk_across(grid, jnp.stack(z1))
        across2 = chunk_across(grid, jnp.stack(after(z2, *z1)))
        z3 = [grid.along_z(after(cuts[2], *z2), d) for d in planes]
        qkv_a, wa, vecs, attn_in, left = project(
            grid, place, scale_half, tokens, both_cores(grid, [chunks[0], *across1]), True
        )
        vecs = vecs[:, 0].reshape(grid.owners, 4, grid.rows)
        qkv_a, z3 = after((qkv_a, z3), wa)
        attended, *kept_a = attend_forward(0, lengths, qkv_a)
        across3 = chunk_across(grid, jnp.stack(z3))
        pieces2 = both_cores(grid, [chunks[1], *after(across2, qkv_a)])
        qkv_b, wb = project(grid, place, scale_half, after(attn_in, attended), pieces2, False)
        attended, *kept_b = attend_forward(1, lengths, qkv_b, attended)
        pieces3 = both_cores(grid, [chunks[2], *after(across3, attended)])
        gain_m, bias_up = (vecs[:, i].reshape(D).astype(f32) for i in (1, 2))
        wo, w_up, w_down, hidden1, mlp_in, pre, act, down_grad = mlp_forward(
            grid, place, gain_m, bias_up, pieces3, attended, tokens, grad_out_low
        )
    else:
        wq, wk, wv, wo, w_up, w_down = (
            lax.all_gather(w, "fsdp", axis=0, tiled=True)
            for w in (query_weight, key_weight, value_weight, output_weight, up_weight, down_weight)
        )
        wa = jnp.concatenate([w[:, :HALF] for w in (wq, wk, wv)], axis=1)
        wb = jnp.concatenate([w[:, HALF:] for w in (wq, wk, wv)], axis=1)
        vecs = lax.all_gather(vectors, "fsdp", axis=0).reshape(grid.owners, 4, grid.rows)
        attn_in = (rms_parts(xin)[0] * vecs[:, 0].reshape(D).astype(f32)).astype(bf16)
        left = attn_in.T
        scale_row = jnp.concatenate([scale_half[0], jnp.ones((2 * HALF,), f32)])
        attended, *kept_a = attend_forward(0, lengths, (nn(attn_in, wa) * scale_row).astype(bf16))
        attended, *kept_b = attend_forward(1, lengths, (nn(attn_in, wb) * scale_row).astype(bf16), attended)
        gain_m, bias_up = (vecs[:, i].reshape(D).astype(f32) for i in (1, 2))
        hidden1 = xin + nn(attended, wo)
        mlp_in = (rms_parts(hidden1)[0] * gain_m).astype(bf16)
        pre = nn(mlp_in, w_up) + bias_up
        act = (pre * jax.nn.sigmoid(pre)).astype(bf16)
        down_grad = tn(act, grad_out_low).astype(bf16)
    kept = (kept_a, kept_b)
    gain_a, bias_down = (vecs[:, i].reshape(D).astype(f32) for i in (0, 3))

    fac_row = jnp.broadcast_to(jnp.pad(factor, (0, LANES - HD))[None], (8, LANES))
    owned = (grid.owners, grid.rows)

    def scattered(grad):
        return lax.psum_scatter(grad, "fsdp", scatter_dimension=0, tiled=True)

    part_down = scattered(down_grad)
    up_grad, output_grad, grad_hidden, grad_att, up_bias_grad, down_bias_grad = mlp_backward(
        gain_m, grad_out_low, w_down, pre, mlp_in, w_up, hidden1, wo, attended
    )
    part_up, part_o = scattered(up_grad), scattered(output_grad)

    back_a, scale_a = attend_backward(0, fac_row, *kept[0], attended, grad_att)
    if grid.pieced:
        mine_a, theirs_a = weight_grads(
            grid, place, left, back_a, [up_bias_grad.reshape(owned), down_bias_grad.reshape(owned)]
        )
        recv_a = grid.other_core(theirs_a)
        a1 = fold_cores(grid, place, mine_a, recv_a)
        ra1 = (grid.across(a1[0], 1), grid.across(a1[2], 2))
        grad_att = after(grad_att, a1[0])
    back_b, scale_b = attend_backward(1, fac_row, *kept[1], attended, grad_att)
    scale_part = (scale_a + scale_b)[0, :HD] / (query_scale.astype(f32) * LOG2E)

    if grid.pieced:
        scale_rows = jnp.broadcast_to(jnp.pad(scale_part, (0, grid.rows - HD))[None], owned)
        mine_b, theirs_b = weight_grads(grid, place, left, after(back_b, *ra1), [scale_rows])
        recv_b = grid.other_core(theirs_b)
        a2 = fold_first(grid, place, a1[1], after(ra1[0], mine_b), a1[3], ra1[1])
        ra2 = (grid.across(a2[0], 2), grid.across(a2[2], 1))
        b1 = fold_cores(grid, place, mine_b, after(recv_b, a2[0]))
        rb1 = (grid.across(b1[0], 1), grid.across(b1[2], 2))
        late = jnp.concatenate(after([part_o, part_up, part_down], b1[0]))
        summed = lax.psum(late, "replica").astype(f32)
        input_grad = input_grad_of(tokens, gain_a, after(grad_hidden, b1[0], late), (back_a, back_b), (wa, wb))
        a3 = fold_second(grid, place, a2[1], after(ra2[0], input_grad), a2[3], ra2[1])
        ra3 = [grid.along_z(a3[s], s) for s in range(1, grid.planes)]
        b2 = fold_first(grid, place, b1[1], after(rb1[0], a3[0]), b1[3], rb1[1])
        rb2 = (grid.across(b2[0], 2), grid.across(b2[2], 1))
        act = after(act, b2[0])
        out_f = (hidden1 + nn(act, w_down) + bias_down).astype(bf16)
        a4 = fold_planes(grid, a3[0], *after(ra3, out_f))
        a5 = [a4] + [grid.across(a4, code) for code in (1, 2, 3)]
        b3 = fold_second(grid, place, b2[1], after(rb2[0], a4), b2[3], rb2[1])
        rb3 = [grid.along_z(b3[s], s) for s in range(1, grid.planes)]
        b4 = fold_planes(grid, b3[0], *after(rb3, summed))
        b5 = [b4] + [grid.across(b4, code) for code in (1, 2, 3)]
        g_q, g_k, g_v, tail = finish(grid, place, [a5, b5])
        g_o, g_up, g_down = (summed[i * grid.rows : (i + 1) * grid.rows] for i in range(3))
        g_up_bias, g_down_bias = tail[0, : grid.rows], tail[1, : grid.rows]
        scale_grad = tail[0, HALF : HALF + HD]
    else:
        out_f = (hidden1 + nn(act, w_down) + bias_down).astype(bf16)
        input_grad = input_grad_of(tokens, gain_a, grad_hidden, (back_a, back_b), (wa, wb))
        joined = [
            jnp.concatenate([g[:, w * HALF : (w + 1) * HALF] for g in (back_a, back_b)], axis=1) for w in range(3)
        ]
        g_o, g_up, g_down, g_q, g_k, g_v, g_up_bias, g_down_bias = (
            lax.psum(g.astype(f32), "replica")
            for g in (
                part_o,
                part_up,
                part_down,
                *[scattered(tn(attn_in, g).astype(bf16)) for g in joined],
                scattered(up_bias_grad),
                scattered(down_bias_grad),
            )
        )
        scale_grad = lax.psum(scale_part, ("replica", "fsdp"))

    def weighed(*pairs):
        return sum(jnp.sum(w.astype(f32) * g, axis=1) for w, g in pairs)

    g_attn_gain = weighed((query_weight, g_q), (key_weight, g_k), (value_weight, g_v)) / attn_gain.astype(f32)
    g_mlp_gain = weighed((up_weight, g_up)) / mlp_gain.astype(f32)
    sums = (g_q, g_k, g_v, g_o, g_up, g_down, g_attn_gain, g_mlp_gain, g_up_bias, g_down_bias)
    return (out_f, input_grad, *sums, scale_grad)


def solution(mesh):
    split = P(("replica", "fsdp"), None)
    rows = P("fsdp", None)
    part = P("fsdp")
    return jax.shard_map(
        functools.partial(shards, Grid(mesh.shape)),
        mesh=mesh,
        in_specs=(split, P(("replica", "fsdp")), split, *[rows] * 6, *[part] * 4, P()),
        out_specs=(split, split, *[rows] * 6, *[part] * 4, P()),
        check_vma=False,
    )
```

```python
import functools
import math

import jax
import jax.numpy as jnp
from jax import lax
from jax.experimental import pallas as pl
from jax.experimental.pallas import tpu as pltpu
from jax.sharding import PartitionSpec as P

D = 1280
HEADS = 16
HD = 80
FF = 1280
SEQ = 1024
EPS = 1e-06
LOG2E = math.log2(math.e)
NEG = -1e30
LANES = 128
BLOCK = 256
GROUP = 8
HALF = GROUP * HD
TRIPLE = 3 * HALF
VMEM_LIMIT = 58 << 20
SHORT = 40

bf16 = jnp.bfloat16
f32 = jnp.float32


def rms_parts(v):
    inverse = lax.rsqrt(jnp.mean(v * v, axis=-1, keepdims=True) + EPS)
    return (v * inverse, inverse)


def rms_back(grad_n, normed, inverse):
    return inverse * (grad_n - normed * jnp.mean(grad_n * normed, axis=-1, keepdims=True))


def nt(a, b):
    return lax.dot_general(a, b, (((1,), (1,)), ((), ())), preferred_element_type=f32)


def nn(a, b):
    return lax.dot_general(a, b, (((1,), (0,)), ((), ())), preferred_element_type=f32)


def tn(a, b):
    return lax.dot_general(a, b, (((0,), (0,)), ((), ())), preferred_element_type=f32)


def widen(v):
    return jnp.pad(v, ((0, 0), (0, LANES - HD)))


def split3(v):
    a = v.astype(bf16).astype(f32)
    b = (v - a).astype(bf16).astype(f32)
    c = (v - a - b).astype(bf16).astype(f32)
    return a, b, c


def extra_lanes(lane, base, extra):
    out = jnp.zeros_like(base)
    for place, value in reversed(list(enumerate(extra))):
        out = jnp.where(lane == HD + place, value, out)
    return jnp.where(lane < HD, base, out)


def forward_kernel(heads, len_ref, qkv_ref, o_ref, qa_ref, ka_ref, va_ref):
    length = len_ref[0]
    lane = lax.broadcasted_iota(jnp.int32, (SEQ, LANES), 1)
    row = lax.broadcasted_iota(jnp.int32, (SEQ, LANES), 0)
    mask = jnp.where(row < length, 0.0, NEG)
    k_pad = jnp.where(lane == HD, mask, jnp.where((lane > HD) & (lane < HD + 4), 1.0, 0.0)).astype(bf16)
    v_pad = jnp.where((lane >= HD) & (lane < HD + 3), 1.0, 0.0).astype(bf16)
    q_pad = jnp.where(lane == HD, 1.0, 0.0).astype(bf16)
    in_head = lane < HD
    block_lane = lane[:BLOCK]
    block_row = lax.broadcasted_iota(jnp.int32, (LANES, BLOCK), 0)
    causal = lax.broadcasted_iota(jnp.int32, (BLOCK, BLOCK), 0) <= lax.broadcasted_iota(
        jnp.int32, (BLOCK, BLOCK), 1
    )
    blocks = SEQ // BLOCK

    def prepare(h):
        for n, (ref, pad) in enumerate(((qa_ref, q_pad), (ka_ref, k_pad), (va_ref, v_pad))):
            at = n * HALF + h * HD
            ref[h] = jnp.where(in_head, widen(qkv_ref[:, at : at + HD]), pad)

    def scores(h, i):
        return nt(ka_ref[h, : (i + 1) * BLOCK, :], qa_ref[h, i * BLOCK : (i + 1) * BLOCK, :])

    def attend(h, i, st):
        before = i * BLOCK
        diagonal = jnp.where(causal, st[before:], NEG)
        top = jnp.max(diagonal, axis=0, keepdims=True)
        if i:
            top = jnp.maximum(top, jnp.max(st[:before], axis=0, keepdims=True))
        p = jnp.exp2(diagonal - top).astype(bf16)
        if i:
            p = jnp.concatenate([jnp.exp2(st[:before] - top).astype(bf16), p], axis=0)
        return tn(va_ref[h, : before + BLOCK, :], p), top

    def finish(h, i, ot, top):
        rows = slice(i * BLOCK, (i + 1) * BLOCK)
        total = ot[HD : HD + 1]
        a, b, c = split3(-(top + jnp.log2(total)))
        scaled = jnp.where(block_row < HD, ot / total, 0.0)
        for place, value in ((1, a), (2, b), (3, c)):
            scaled = jnp.where(block_row == HD + place, value, scaled)
        o = scaled.T
        o_ref[rows, h * HD : (h + 1) * HD] = o[:, :HD].astype(bf16)
        qa_ref[h, rows, :] = jnp.where(block_lane <= HD, qa_ref[h, rows, :].astype(f32), o).astype(bf16)

    for h in range(heads):
        prepare(h)
    scored, done = [], []
    for h, i in [(h, i) for h in range(heads) for i in range(blocks)] + [(None, None)] * 2:
        if h is not None:
            scored.append((h, i, scores(h, i)))
        if len(scored) > 1 or (h is None and scored):
            hh, ii, st = scored.pop(0)
            done.append((hh, ii, *attend(hh, ii, st)))
        if len(done) > 1 or (h is None and not scored and done):
            finish(*done.pop(0))
    while done:
        finish(*done.pop(0))


def attend_forward(half, lengths, qkv, before=None):
    wide = pl.BlockSpec((GROUP, SEQ, LANES), lambda g: (0, 0, 0))
    kept = [] if before is None else [before]

    def kernel(len_ref, qkv_ref, *refs):
        forward_kernel(GROUP, len_ref, qkv_ref, *refs[len(kept) :])

    return pl.pallas_call(
        kernel,
        grid=(1,),
        in_specs=[pl.BlockSpec(memory_space=pltpu.SMEM), pl.BlockSpec((SEQ, TRIPLE), lambda g: (0, 0))]
        + [pl.BlockSpec(memory_space=pl.ANY)] * len(kept),
        out_specs=[pl.BlockSpec((SEQ, HALF), lambda g: (0, half)), wide, wide, wide],
        out_shape=[jax.ShapeDtypeStruct((SEQ, D), bf16)]
        + [jax.ShapeDtypeStruct((GROUP, SEQ, LANES), bf16)] * 3,
        input_output_aliases={2: 0} if kept else {},
        compiler_params=pltpu.CompilerParams(vmem_limit_bytes=VMEM_LIMIT),
        cost_estimate=pl.CostEstimate(
            flops=GROUP * SEQ * SEQ * 1200 // SHORT, bytes_accessed=0, transcendentals=0
        ),
        name="attend_forward",
    )(lengths, qkv, *kept)


def backward_kernel(
    heads, fac_ref, qa_ref, ka_ref, va_ref, o_ref, g_ref, d_ref, sg_ref, dqs, gs
):
    lane = lax.broadcasted_iota(jnp.int32, (SEQ, LANES), 1)
    causal = lax.broadcasted_iota(jnp.int32, (BLOCK, BLOCK), 0) <= lax.broadcasted_iota(
        jnp.int32, (BLOCK, BLOCK), 1
    )
    fac = fac_ref[0:1, :]
    blocks = SEQ // BLOCK

    @pl.when(pl.program_id(0) == 0)
    def _():
        sg_ref[...] = jnp.zeros_like(sg_ref)

    sums = []

    def prepare(h):
        own = slice(h * HD, (h + 1) * HD)
        g = widen(g_ref[:, own]).astype(f32)
        o = widen(o_ref[:, own]).astype(f32)
        delta = jnp.sum(g * o, axis=1, keepdims=True)
        gs[h] = extra_lanes(lane, g, split3(-delta)).astype(bf16)

    def products(h, j):
        js = slice(j * BLOCK, (j + 1) * BLOCK)
        return nt(ka_ref[h, js, :], qa_ref[h, j * BLOCK :, :]), nt(va_ref[h, js, :], gs[h, j * BLOCK :, :])

    def middle(j, st, dpt):
        p = jnp.exp2(st)
        diagonal = jnp.where(causal, p[:, :BLOCK], 0.0)
        p = jnp.concatenate([diagonal, p[:, BLOCK:]], axis=1) if j < blocks - 1 else diagonal
        return (p * dpt).astype(bf16), p.astype(bf16)

    def finish(h, j, ds, p):
        own, dk, dv = (slice(n * HALF + h * HD, n * HALF + (h + 1) * HD) for n in range(3))
        js = slice(j * BLOCK, (j + 1) * BLOCK)
        d_ref[js, dv] = nn(p, gs[h, j * BLOCK :, :])[:, :HD].astype(bf16)
        d_ref[js, dk] = (nn(ds, qa_ref[h, j * BLOCK :, :])[:, :HD] * (1.0 / LOG2E)).astype(bf16)
        dqt = tn(ka_ref[h, js, :], ds)
        if j == 0:
            dqs[h % 2] = dqt
        else:
            dqs[h % 2, :, j * BLOCK :] += dqt
        if j == blocks - 1:
            dq = dqs[h % 2].T.astype(bf16).astype(f32)
            sums.append(jnp.sum(dq * qa_ref[h].astype(f32), axis=0, keepdims=True))
            d_ref[:, own] = (dq * fac)[:, :HD].astype(bf16)

    for h in range(heads):
        prepare(h)
    waiting = []
    for h, j in [(h, j) for h in range(heads) for j in range(blocks)]:
        waiting.append((h, j, *products(h, j)))
        if len(waiting) > 1:
            hh, jj, st, dpt = waiting.pop(0)
            finish(hh, jj, *middle(jj, st, dpt))
    hh, jj, st, dpt = waiting.pop(0)
    finish(hh, jj, *middle(jj, st, dpt))
    sg_ref[0:1, :] += sum(sums)


def attend_backward(half, fac, qa, ka, va, o, g):
    part = pl.BlockSpec((SEQ, HALF), lambda g: (0, half))
    wide = pl.BlockSpec((GROUP, SEQ, LANES), lambda g: (0, 0, 0))
    full = pl.BlockSpec((8, LANES), lambda g: (0, 0))
    return pl.pallas_call(
        functools.partial(backward_kernel, GROUP),
        grid=(1,),
        in_specs=[full, wide, wide, wide, part, part],
        out_specs=[pl.BlockSpec((SEQ, TRIPLE), lambda g: (0, 0)), full],
        out_shape=[jax.ShapeDtypeStruct((SEQ, TRIPLE), bf16), jax.ShapeDtypeStruct((8, LANES), f32)],
        scratch_shapes=[pltpu.VMEM((2, LANES, SEQ), f32), pltpu.VMEM((GROUP, SEQ, LANES), bf16)],
        compiler_params=pltpu.CompilerParams(vmem_limit_bytes=VMEM_LIMIT),
        cost_estimate=pl.CostEstimate(
            flops=GROUP * SEQ * SEQ * 2400 // SHORT, bytes_accessed=0, transcendentals=0
        ),
        name="attend_backward",
    )(fac, qa, ka, va, o, g)


class Grid:
    def __init__(self, mesh_shape):
        self.copies, self.owners = mesh_shape["replica"], mesh_shape["fsdp"]
        self.planes = self.owners // 2
        self.rows = D // self.owners

    @property
    def pieced(self):
        return self.copies == 4 and self.owners == 8

    def place(self):
        me, copy = lax.axis_index("fsdp"), lax.axis_index("replica")
        return copy // 2, copy % 2, me // 2, me % 2

    def along_z(self, v, step):
        n = self.planes
        pairs = [(i, (i // 2 + step) % n * 2 + i % 2) for i in range(self.owners)]
        return lax.ppermute(v, "fsdp", pairs)

    def other_core(self, v):
        return lax.ppermute(v, "fsdp", [(i, i ^ 1) for i in range(self.owners)])

    def across(self, v, code):
        return lax.ppermute(v, "replica", [(i, i ^ code) for i in range(self.copies)])


def kernel_call(kernel, name, operands, outs, scratch=(), flops=0, nbytes=0, **more):
    return pl.pallas_call(
        kernel,
        out_shape=outs,
        scratch_shapes=scratch,
        compiler_params=pltpu.CompilerParams(vmem_limit_bytes=VMEM_LIMIT),
        cost_estimate=pl.CostEstimate(flops=flops // SHORT, bytes_accessed=nbytes // SHORT, transcendentals=0),
        name=name,
        **more,
    )(*operands)


def piece_copies(planes, quarter, place_ref, refs, buf, sem):
    y, x, z, core = (place_ref[i] for i in range(4))
    groups = []
    for s, (source, c) in enumerate(((refs[:5], core), (refs[5:10], 1 - core))):
        block, *pieces = source
        home = 2 * z + c
        groups.append((home, [pltpu.make_async_copy(block, buf.at[home], sem.at[s, 0, 0])]))
        for d in range(1, planes):
            owner = 2 * lax.rem(z - d + planes, planes) + c
            copies = []
            for code, piece in enumerate(pieces):
                py = 1 - y if code >= 2 else y
                px = 1 - x if code % 2 else x
                at = pl.multiple_of((2 * py + px) * quarter, 16)
                copies.append(
                    pltpu.make_async_copy(piece.at[d - 1], buf.at[owner, pl.ds(at, quarter), :], sem.at[s, d, code])
                )
            groups.append((owner, copies))
    return groups


def project_kernel(planes, rows, quarter, first, place_ref, scale_ref, x_ref, *refs):
    outs, scratch = refs[10 : 10 + (5 if first else 2)], refs[10 + (5 if first else 2) :]
    qkv_ref, whole_ref = outs[:2]
    buf, sem_in, sem_out = scratch[:3]
    groups = piece_copies(planes, quarter, place_ref, refs, buf, sem_in)
    for _, copies in groups:
        for copy in copies:
            copy.start()
    if first:
        held = scratch[3]
        for at in range(0, SEQ, BLOCK):
            held[at : at + BLOCK, :] = rms_parts(x_ref[at : at + BLOCK, :].astype(f32))[0]
    written = []
    for g, (owner, copies) in enumerate(groups):
        for copy in copies:
            copy.wait()
        at = pl.multiple_of(owner * rows, 16)
        for t in range(3):
            copy = pltpu.make_async_copy(
                buf.at[owner, pl.ds(t * rows, rows), :],
                whole_ref.at[pl.ds(at, rows), pl.ds(t * HALF, HALF)],
                sem_out.at[g, t],
            )
            copy.start()
            written.append(copy)
    if first:
        vec_ref, attn_in, left_ref = outs[2:5]
        vec_ref[...] = buf[:, 3 * rows : 3 * rows + 16, :]
        gain = jnp.concatenate([buf[b, 3 * rows : 3 * rows + 16, :rows][0:1] for b in range(2 * planes)], axis=1)
        gain = gain.astype(f32)
        for at in range(0, SEQ, BLOCK):
            attn_in[at : at + BLOCK, :] = (held[at : at + BLOCK, :] * gain).astype(bf16)
    else:
        attn_in = x_ref
    for t in range(3):
        weight = buf[:, t * rows : (t + 1) * rows, :].reshape(D, HALF)
        result = nn(attn_in[...], weight)
        qkv_ref[:, t * HALF : (t + 1) * HALF] = (result * scale_ref[0:1, :] if t == 0 else result).astype(bf16)
    if first:
        left_ref[...] = attn_in[...].T
    for copy in written:
        copy.wait()


def project(grid, place, scale, x, pieces, first):
    total = pieces[0].shape[0]
    vmem, hbm = pl.BlockSpec(memory_space=pltpu.VMEM), pl.BlockSpec(memory_space=pl.ANY)
    outs = [jax.ShapeDtypeStruct((SEQ, TRIPLE), bf16), jax.ShapeDtypeStruct((D, TRIPLE), bf16)]
    scratch = [
        pltpu.VMEM((grid.owners, total, HALF), bf16),
        pltpu.SemaphoreType.DMA((2, grid.planes, 4)),
        pltpu.SemaphoreType.DMA((grid.owners, 3)),
    ]
    if first:
        outs += [
            jax.ShapeDtypeStruct((grid.owners, 16, HALF), bf16),
            jax.ShapeDtypeStruct((SEQ, D), bf16),
            jax.ShapeDtypeStruct((D, SEQ), bf16),
        ]
        scratch.append(pltpu.VMEM((SEQ, D), f32))
    return kernel_call(
        functools.partial(project_kernel, grid.planes, grid.rows, total // 4, first),
        "project",
        (place, scale, x, *pieces),
        outs,
        scratch=scratch,
        flops=2 * SEQ * D * TRIPLE,
        nbytes=4 * D * TRIPLE + 2 * SEQ * (D + TRIPLE),
        in_specs=[pl.BlockSpec(memory_space=pltpu.SMEM), vmem, vmem] + [hbm] * 10,
        out_specs=[vmem, hbm] + [vmem] * 3 * first,
    )


def cut_kernel(rows, place_ref, *refs):
    weights, vec_ref = refs[:6], refs[6]
    chunks, pieces = refs[7:10], refs[10:13]
    for half in range(2):
        for t in range(3):
            chunks[half][t * rows : (t + 1) * rows, :] = weights[t][:, half * HALF : (half + 1) * HALF]
        chunks[half][3 * rows :, :] = vec_ref[...]
    for t in range(6):
        w, half = 3 + t // 2, t % 2
        chunks[2][t * rows : (t + 1) * rows, :] = weights[w][:, half * HALF : (half + 1) * HALF]
    copy = 2 * place_ref[0] + place_ref[1]
    for chunk, piece in zip(chunks, pieces, strict=True):
        quarter = piece.shape[0]
        piece[...] = chunk[pl.ds(pl.multiple_of(copy * quarter, 16), quarter), :]


def cut(grid, place, weights, vectors):
    rows = [512, 512, 6 * grid.rows]
    vec = jnp.pad(vectors.reshape(1, HALF), ((0, 512 - 3 * grid.rows - 1), (0, 0)))
    out = kernel_call(
        functools.partial(cut_kernel, grid.rows),
        "cut",
        (place, *weights, vec),
        [jax.ShapeDtypeStruct((n, HALF), bf16) for n in rows]
        + [jax.ShapeDtypeStruct((n // 4, HALF), bf16) for n in rows],
        nbytes=12 * grid.rows * D * 2,
        in_specs=[pl.BlockSpec(memory_space=pltpu.SMEM)] + [pl.BlockSpec(memory_space=pltpu.VMEM)] * 7,
    )
    return out[:3], out[3:]


def chunk_across(grid, along):
    return [along] + [grid.across(along, code) for code in (1, 2, 3)]


def both_cores(grid, own):
    return own + [grid.other_core(v) for v in own]


def in_blocks():
    return [slice(at, at + BLOCK) for at in range(0, SEQ, BLOCK)]


def mlp_forward_kernel(planes, rows, quarter, place_ref, gain_ref, bias_ref, *refs):
    attended_ref, token_ref, grad_ref = refs[10:13]
    weights, (hidden_ref, mlp_in_ref, pre_ref, act_ref, down_grad_ref) = refs[13:16], refs[16:21]
    buf, attended, token, grad, hidden, mlp_in, pre, act, down_grad, sem_in, sem_out, sem = refs[21:]
    loads = [
        pltpu.make_async_copy(source, target, sem.at[n])
        for n, (source, target) in enumerate(((attended_ref, attended), (token_ref, token), (grad_ref, grad)))
    ]
    groups = piece_copies(planes, quarter, place_ref, refs, buf, sem_in)
    for _, copies in groups:
        for copy in copies:
            copy.start()
    for load in loads:
        load.start()
    written = []

    def keep(source, target, n):
        copy = pltpu.make_async_copy(source, target, sem.at[n])
        copy.start()
        written.append(copy)

    for g, (owner, copies) in enumerate(groups):
        for copy in copies:
            copy.wait()
        at = pl.multiple_of(owner * rows, 16)
        for t in range(6):
            copy = pltpu.make_async_copy(
                buf.at[owner, pl.ds(t * rows, rows), :],
                weights[t // 2].at[pl.ds(at, rows), pl.ds(t % 2 * HALF, HALF)],
                sem_out.at[g, t],
            )
            copy.start()
            written.append(copy)
    for load in loads:
        load.wait()

    def tile(t):
        return buf[:, t * rows : (t + 1) * rows, :].reshape(D, HALF)

    halves = (slice(0, HALF), slice(HALF, D))
    for h, across in enumerate(halves):
        hidden[:, across] = token[:, across].astype(f32) + nn(attended[...], tile(h))
    keep(hidden, hidden_ref, 3)
    for at in in_blocks():
        mlp_in[at, :] = (rms_parts(hidden[at, :])[0] * gain_ref[0:1, :]).astype(bf16)
    keep(mlp_in, mlp_in_ref, 4)
    for h, across in enumerate(halves):
        value = nn(mlp_in[...], tile(2 + h)) + bias_ref[0:1, across]
        pre[:, across] = value
        act[:, across] = (value * jax.nn.sigmoid(value)).astype(bf16)
    keep(pre, pre_ref, 5)
    keep(act, act_ref, 6)
    down_grad[...] = tn(act[...], grad[...]).astype(bf16)
    keep(down_grad, down_grad_ref, 7)
    for copy in written:
        copy.wait()


def mlp_forward(grid, place, gain, bias, pieces, attended, tokens, grad_out_low):
    total = pieces[0].shape[0]
    vmem, hbm = pl.BlockSpec(memory_space=pltpu.VMEM), pl.BlockSpec(memory_space=pl.ANY)
    low, high, square = ((SEQ, D), bf16), ((SEQ, D), f32), ((D, D), bf16)
    outs = [square] * 3 + [high, low, high, low, square]
    return kernel_call(
        functools.partial(mlp_forward_kernel, grid.planes, grid.rows, total // 4),
        "mlp_forward",
        (place, row_of(gain), row_of(bias), *pieces, attended, tokens, grad_out_low),
        [jax.ShapeDtypeStruct(*o) for o in outs],
        scratch=[
            pltpu.VMEM((grid.owners, total, HALF), bf16),
            *[pltpu.VMEM(*v) for v in (low, low, low, high, low, high, low, square)],
            pltpu.SemaphoreType.DMA((2, grid.planes, 4)),
            pltpu.SemaphoreType.DMA((grid.owners, 6)),
            pltpu.SemaphoreType.DMA((8,)),
        ],
        flops=6 * SEQ * D * D,
        nbytes=16 * D * D + 22 * SEQ * D,
        in_specs=[pl.BlockSpec(memory_space=pltpu.SMEM), vmem, vmem] + [hbm] * 13,
        out_specs=[hbm] * 8,
    )


def row_of(v):
    return jnp.broadcast_to(v[None], (8, v.shape[0]))


def mlp_backward_kernel(gain_ref, *refs):
    grad_ref, down_ref, pre_ref, mlp_in_ref, up_ref, hidden_ref, output_ref, attended_ref = refs[:8]
    both_ref, grad_hidden_ref, grad_att_ref, sums_ref = refs[8:12]
    grad, down, wide, mlp_in, up, hidden, output, attended, grad_pre, grad_proj, first, second, sem = refs[12:]
    loads = {}
    for n, (name, source, target) in enumerate(
        (
            ("grad", grad_ref, grad),
            ("down", down_ref, down),
            ("pre", pre_ref, wide),
            ("mlp_in", mlp_in_ref, mlp_in),
            ("up", up_ref, up),
            ("hidden", hidden_ref, hidden),
            ("output", output_ref, output),
            ("attended", attended_ref, attended),
        )
    ):
        loads[name] = pltpu.make_async_copy(source, target, sem.at[n])
        loads[name].start()
    written = []

    def keep(source, target):
        copy = pltpu.make_async_copy(source, target, sem.at[8 + len(written)])
        copy.start()
        written.append(copy)

    for name in ("down", "grad", "pre"):
        loads[name].wait()
    sums = jnp.zeros((1, D), f32)
    for at in in_blocks():
        pre = wide[at, :]
        sigma = jax.nn.sigmoid(pre)
        value = (nt(grad[at, :], down[...]) * (sigma * (1.0 + pre * (1.0 - sigma)))).astype(bf16)
        grad_pre[at, :] = value
        sums = sums + jnp.sum(value.astype(f32), axis=0, keepdims=True)
    sums_ref[...] = jnp.zeros_like(sums_ref)
    sums_ref[0:1, :] = sums
    sums_ref[1:2, :] = jnp.sum(grad[...].astype(f32), axis=0, keepdims=True)
    for name in ("mlp_in", "up", "hidden"):
        loads[name].wait()
    first[...] = tn(mlp_in[...], grad_pre[...]).astype(bf16)
    keep(first, both_ref.at[:, pl.ds(0, D)])
    for at in in_blocks():
        normed, inverse = rms_parts(hidden[at, :])
        back = rms_back(nt(grad_pre[at, :], up[...]) * gain_ref[0:1, :], normed, inverse)
        value = grad[at, :].astype(f32) + back
        wide[at, :] = value
        grad_proj[at, :] = value.astype(bf16)
    keep(wide, grad_hidden_ref)
    for name in ("output", "attended"):
        loads[name].wait()
    for at in in_blocks():
        mlp_in[at, :] = nt(grad_proj[at, :], output[...]).astype(bf16)
    keep(mlp_in, grad_att_ref)
    second[...] = tn(attended[...], grad_proj[...]).astype(bf16)
    keep(second, both_ref.at[:, pl.ds(D, D)])
    for copy in written:
        copy.wait()


def mlp_backward(gain, grad_out_low, w_down, pre, mlp_in, w_up, hidden1, w_out, attended):
    hbm = pl.BlockSpec(memory_space=pl.ANY)
    low, high, square = ((SEQ, D), bf16), ((SEQ, D), f32), ((D, D), bf16)
    both, grad_hidden, grad_att, sums = kernel_call(
        mlp_backward_kernel,
        "mlp_backward",
        (row_of(gain), grad_out_low, w_down, pre, mlp_in, w_up, hidden1, w_out, attended),
        [jax.ShapeDtypeStruct(*o) for o in (((D, 2 * D), bf16), high, low, ((8, D), f32))],
        scratch=[
            *[pltpu.VMEM(*v) for v in (low, square, high, low, square, high, square, low, low, low, square, square)],
            pltpu.SemaphoreType.DMA((12,)),
        ],
        flops=10 * SEQ * D * D,
        nbytes=10 * D * D + 26 * SEQ * D,
        in_specs=[pl.BlockSpec(memory_space=pltpu.VMEM)] + [hbm] * 8,
        out_specs=[hbm] * 3 + [pl.BlockSpec(memory_space=pltpu.VMEM)],
    )
    return both, grad_hidden, grad_att, sums[0], sums[1]


def weight_grad_kernel(planes, rows, place_ref, left_ref, right_ref, vec_ref, mine, theirs, left, right, stage, sem_in, sem_out):
    core = place_ref[3]
    loads = [pltpu.make_async_copy(left_ref, left, sem_in.at[3])]
    for w in range(3):
        part = pl.ds(w * HALF, HALF)
        loads.append(pltpu.make_async_copy(right_ref.at[:, part], right.at[:, part], sem_in.at[w]))
    for load in loads:
        load.start()
    written = []

    def send(w, source, size, c, whole, z):
        copy = pltpu.make_async_copy(source, whole.at[z, pl.ds(w * rows, size), :], sem_out.at[w, c, z])
        copy.start()
        written.append(copy)

    sides = ((1, theirs), (0, mine))
    owner = {(c, z): 2 * z + (1 - core if c else core) for c in range(2) for z in range(planes)}
    for c, whole in sides:
        for z in range(planes):
            send(3, vec_ref.at[owner[c, z]], 32, c, whole, z)
    loads[0].wait()
    for w in range(3):
        loads[1 + w].wait()
        stage[w] = nn(left[...], right[:, w * HALF : (w + 1) * HALF]).astype(bf16)
        for c, whole in sides:
            for z in range(planes):
                at = pl.multiple_of(owner[c, z] * rows, 16)
                send(w, stage.at[w, pl.ds(at, rows), :], rows, c, whole, z)
    for copy in written:
        copy.wait()


def weight_grads(grid, place, left, right, vectors):
    rows = jnp.stack(vectors, axis=1).astype(bf16)
    rows = jnp.pad(rows, ((0, 0), (0, 32 - len(vectors)), (0, HALF - grid.rows)))
    shape = jax.ShapeDtypeStruct((grid.planes, 512, HALF), bf16)
    hbm = pl.BlockSpec(memory_space=pl.ANY)
    return kernel_call(
        functools.partial(weight_grad_kernel, grid.planes, grid.rows),
        "weight_grads",
        (place, left, right, rows),
        [shape, shape],
        scratch=[
            pltpu.VMEM((D, SEQ), bf16),
            pltpu.VMEM((SEQ, TRIPLE), bf16),
            pltpu.VMEM((3, D, HALF), bf16),
            pltpu.SemaphoreType.DMA((4,)),
            pltpu.SemaphoreType.DMA((4, 2, grid.planes)),
        ],
        flops=2 * SEQ * D * TRIPLE,
        nbytes=(SEQ * D + (SEQ + D) * TRIPLE) * 2,
        in_specs=[pl.BlockSpec(memory_space=pltpu.SMEM), hbm, hbm, pl.BlockSpec(memory_space=pltpu.VMEM)],
        out_specs=[hbm, hbm],
    )


def added(a, b):
    return (a.astype(f32) + b.astype(f32)).astype(bf16)


def fold_cores_kernel(place_ref, a_ref, b_ref, send_low, keep_low, send_high, keep_high):
    y, x = place_ref[0], place_ref[1]
    for p in range(2):
        send_low[0, p] = added(a_ref[0, p, 1 - x, 0], b_ref[0, p, 1 - x, 0])
        keep_low[0, p] = added(a_ref[0, p, x, 0], b_ref[0, p, x, 0])
        send_high[0, p] = added(a_ref[0, 1 - y, p, 1], b_ref[0, 1 - y, p, 1])
        keep_high[0, p] = added(a_ref[0, y, p, 1], b_ref[0, y, p, 1])


def fold_cores(grid, place, a, b):
    n, columns = grid.planes, a.shape[2]
    split = (n, 2, 2, 2, 64, columns)
    block = pl.BlockSpec((1, *split[1:]), lambda i: (i, 0, 0, 0, 0, 0))
    out = pl.BlockSpec((1, 2, 64, columns), lambda i: (i, 0, 0, 0))
    return kernel_call(
        fold_cores_kernel,
        "fold_cores",
        (place, a.reshape(split), b.reshape(split)),
        [jax.ShapeDtypeStruct((n, 2, 64, columns), bf16)] * 4,
        nbytes=a.size * 6,
        grid=(n,),
        in_specs=[pl.BlockSpec(memory_space=pltpu.SMEM), block, block],
        out_specs=[out] * 4,
    )


def fold_first_kernel(place_ref, low_a, low_b, high_a, high_b, send_low, keep_low, send_high, keep_high):
    y, x = place_ref[0], place_ref[1]
    send_low[0] = added(low_a[0, 1 - y], low_b[0, 1 - y])
    keep_low[0] = added(low_a[0, y], low_b[0, y])
    send_high[0] = added(high_a[0, 1 - x], high_b[0, 1 - x])
    keep_high[0] = added(high_a[0, x], high_b[0, x])


def fold_first(grid, place, *parts):
    n, columns = grid.planes, parts[0].shape[3]
    block = pl.BlockSpec((1, 2, 64, columns), lambda i: (i, 0, 0, 0))
    out = pl.BlockSpec((1, 64, columns), lambda i: (i, 0, 0))
    return kernel_call(
        fold_first_kernel,
        "fold_first",
        (place, *parts),
        [jax.ShapeDtypeStruct((n, 64, columns), bf16)] * 4,
        nbytes=parts[0].size * 12,
        grid=(n,),
        in_specs=[pl.BlockSpec(memory_space=pltpu.SMEM)] + [block] * 4,
        out_specs=[out] * 4,
    )


def fold_second_kernel(planes, place_ref, low_a, low_b, high_a, high_b, *outs):
    z = place_ref[2]
    for s in range(planes):
        at = lax.rem(z + s, planes)
        outs[s][0] = added(low_a[at], low_b[at])
        outs[s][1] = added(high_a[at], high_b[at])


def fold_second(grid, place, *parts):
    n, columns = grid.planes, parts[0].shape[2]
    return kernel_call(
        functools.partial(fold_second_kernel, n),
        "fold_second",
        (place, *parts),
        [jax.ShapeDtypeStruct((2, 64, columns), bf16)] * n,
        nbytes=parts[0].size * 12,
        in_specs=[pl.BlockSpec(memory_space=pltpu.SMEM)] + [pl.BlockSpec(memory_space=pltpu.VMEM)] * 4,
    )


def fold_planes_kernel(*refs):
    *parts, out = refs
    total = parts[0][...].astype(f32)
    for part in parts[1:]:
        total = total + part[...].astype(f32)
    out[...] = total.astype(bf16)


def fold_planes(grid, *parts):
    return kernel_call(
        fold_planes_kernel,
        "fold_planes",
        parts,
        jax.ShapeDtypeStruct(parts[0].shape, bf16),
        nbytes=parts[0].size * 10,
    )


def finish_kernel(units, rows, place_ref, *refs):
    me = 2 * place_ref[0] + place_ref[1]
    parts, outs, stage = refs[: 4 * units], refs[4 * units : -1], refs[-1]
    columns = parts[0].shape[2]
    for u in range(units):
        across = slice(u * columns, (u + 1) * columns)
        for r in range(4):
            for code in range(4):

                @pl.when(me == r ^ code)
                def _(r=r, code=code, u=u, across=across):
                    for h in range(2):
                        at = 128 * r + 64 * h
                        stage[at : at + 64, across] = parts[4 * u + code][h].astype(f32)

    for w in range(3):
        outs[w][...] = stage[w * rows : (w + 1) * rows, :]
    outs[3][...] = stage[3 * rows :, :]


def finish(grid, place, units):
    columns = units[0][0].shape[2] * len(units)
    parts = [part for unit in units for part in unit]
    return kernel_call(
        functools.partial(finish_kernel, len(units), grid.rows),
        "finish",
        (place, *parts),
        [jax.ShapeDtypeStruct((grid.rows, columns), f32)] * 3
        + [jax.ShapeDtypeStruct((512 - 3 * grid.rows, columns), f32)],
        scratch=[pltpu.VMEM((512, columns), f32)],
        nbytes=512 * columns * 6,
        in_specs=[pl.BlockSpec(memory_space=pltpu.SMEM)]
        + [pl.BlockSpec(memory_space=pltpu.VMEM)] * len(parts),
    )


def input_grad_kernel(x_ref, gain_ref, hidden_ref, grad_a, grad_b, weight_a, weight_b, out):
    total = nt(grad_a[...], weight_a[...]) + nt(grad_b[...], weight_b[...])
    normed, inverse = rms_parts(x_ref[...].astype(f32))
    out[...] = (hidden_ref[...] + rms_back(total * gain_ref[0:1, :], normed, inverse)).astype(bf16)


def input_grad_of(tokens, gain, grad_hidden, grads, weights):
    count, block = tokens.shape[0], BLOCK
    rows = pl.BlockSpec((block, D), lambda i: (i, 0))
    return kernel_call(
        input_grad_kernel,
        "input_grad",
        (tokens, jnp.broadcast_to(gain[None], (8, D)), grad_hidden, *grads, *weights),
        jax.ShapeDtypeStruct((count, D), bf16),
        flops=6 * count * D * D,
        nbytes=6 * D * D + 14 * count * D,
        grid=(count // block,),
        in_specs=[rows, pl.BlockSpec((8, D), lambda i: (0, 0)), rows]
        + [pl.BlockSpec((block, TRIPLE), lambda i: (i, 0))] * 2
        + [pl.BlockSpec((D, TRIPLE), lambda i: (0, 0))] * 2,
        out_specs=rows,
    )


def after(value, *first):
    return lax.optimization_barrier((value, first))[0]


def shards(
    grid,
    tokens,
    lengths,
    cotangent,
    query_weight,
    key_weight,
    value_weight,
    output_weight,
    up_weight,
    down_weight,
    attn_gain,
    mlp_gain,
    up_bias,
    down_bias,
    query_scale,
):
    assert lengths.shape[0] == 1 and tokens.shape[0] == SEQ
    vectors = jnp.concatenate([attn_gain, mlp_gain, up_bias, down_bias])
    y, x, z, core = grid.place()
    place = jnp.stack([y, x, z, core]).astype(jnp.int32)
    xin = tokens.astype(f32)
    factor = query_scale.astype(f32) * (1.0 / jnp.sqrt(f32(HD)))
    scale_half = row_of(jnp.tile(factor * LOG2E, GROUP))
    valid = (jnp.arange(SEQ, dtype=jnp.int32) < lengths[0]).reshape(-1, 1)
    grad_out_low = jnp.where(valid, cotangent, jnp.zeros_like(cotangent))
    if grid.pieced:
        weights = (query_weight, key_weight, value_weight, output_weight, up_weight, down_weight)
        chunks, cuts = cut(grid, place, weights, vectors)
        planes = range(1, grid.planes)
        z1 = [grid.along_z(cuts[0], d) for d in planes]
        z2 = [grid.along_z(after(cuts[1], *z1), d) for d in planes]
        across1 = chunk_across(grid, jnp.stack(z1))
        across2 = chunk_across(grid, jnp.stack(after(z2, *z1)))
        z3 = [grid.along_z(after(cuts[2], *z2), d) for d in planes]
        qkv_a, wa, vecs, attn_in, left = project(
            grid, place, scale_half, tokens, both_cores(grid, [chunks[0], *across1]), True
        )
        vecs = vecs[:, 0].reshape(grid.owners, 4, grid.rows)
        qkv_a, z3 = after((qkv_a, z3), wa)
        attended, *kept_a = attend_forward(0, lengths, qkv_a)
        across3 = chunk_across(grid, jnp.stack(z3))
        pieces2 = both_cores(grid, [chunks[1], *after(across2, qkv_a)])
        qkv_b, wb = project(grid, place, scale_half, after(attn_in, attended), pieces2, False)
        attended, *kept_b = attend_forward(1, lengths, qkv_b, attended)
        pieces3 = both_cores(grid, [chunks[2], *after(across3, attended)])
        gain_m, bias_up = (vecs[:, i].reshape(D).astype(f32) for i in (1, 2))
        wo, w_up, w_down, hidden1, mlp_in, pre, act, down_grad = mlp_forward(
            grid, place, gain_m, bias_up, pieces3, attended, tokens, grad_out_low
        )
    else:
        wq, wk, wv, wo, w_up, w_down = (
            lax.all_gather(w, "fsdp", axis=0, tiled=True)
            for w in (query_weight, key_weight, value_weight, output_weight, up_weight, down_weight)
        )
        wa = jnp.concatenate([w[:, :HALF] for w in (wq, wk, wv)], axis=1)
        wb = jnp.concatenate([w[:, HALF:] for w in (wq, wk, wv)], axis=1)
        vecs = lax.all_gather(vectors, "fsdp", axis=0).reshape(grid.owners, 4, grid.rows)
        attn_in = (rms_parts(xin)[0] * vecs[:, 0].reshape(D).astype(f32)).astype(bf16)
        left = attn_in.T
        scale_row = jnp.concatenate([scale_half[0], jnp.ones((2 * HALF,), f32)])
        attended, *kept_a = attend_forward(0, lengths, (nn(attn_in, wa) * scale_row).astype(bf16))
        attended, *kept_b = attend_forward(1, lengths, (nn(attn_in, wb) * scale_row).astype(bf16), attended)
        gain_m, bias_up = (vecs[:, i].reshape(D).astype(f32) for i in (1, 2))
        hidden1 = xin + nn(attended, wo)
        mlp_in = (rms_parts(hidden1)[0] * gain_m).astype(bf16)
        pre = nn(mlp_in, w_up) + bias_up
        act = (pre * jax.nn.sigmoid(pre)).astype(bf16)
        down_grad = tn(act, grad_out_low).astype(bf16)
    kept = (kept_a, kept_b)
    gain_a, bias_down = (vecs[:, i].reshape(D).astype(f32) for i in (0, 3))

    fac_row = jnp.broadcast_to(jnp.pad(factor, (0, LANES - HD))[None], (8, LANES))
    owned = (grid.owners, grid.rows)

    def scattered(grad):
        return lax.psum_scatter(grad, "fsdp", scatter_dimension=0, tiled=True)

    part_down = scattered(down_grad)
    both, grad_hidden, grad_att, up_bias_grad, down_bias_grad = mlp_backward(
        gain_m, grad_out_low, w_down, pre, mlp_in, w_up, hidden1, wo, attended
    )
    part_both = scattered(both)

    back_a, scale_a = attend_backward(0, fac_row, *kept[0], attended, grad_att)
    if grid.pieced:
        mine_a, theirs_a = weight_grads(
            grid, place, left, back_a, [up_bias_grad.reshape(owned), down_bias_grad.reshape(owned)]
        )
        recv_a = grid.other_core(theirs_a)
        a1 = fold_cores(grid, place, mine_a, recv_a)
        ra1 = (grid.across(a1[0], 1), grid.across(a1[2], 2))
        grad_att = after(grad_att, a1[0])
    back_b, scale_b = attend_backward(1, fac_row, *kept[1], attended, grad_att)
    scale_part = (scale_a + scale_b)[0, :HD] / (query_scale.astype(f32) * LOG2E)

    if grid.pieced:
        scale_rows = jnp.broadcast_to(jnp.pad(scale_part, (0, grid.rows - HD))[None], owned)
        mine_b, theirs_b = weight_grads(grid, place, left, after(back_b, *ra1), [scale_rows])
        recv_b = grid.other_core(theirs_b)
        late = jnp.concatenate(after([part_both, part_down], mine_b), axis=1)
        summed = lax.psum(late, "replica").astype(f32)
        a2 = fold_first(grid, place, a1[1], after(ra1[0], mine_b, late), a1[3], ra1[1])
        ra2 = (grid.across(a2[0], 2), grid.across(a2[2], 1))
        b1 = fold_cores(grid, place, mine_b, after(recv_b, a2[0]))
        rb1 = (grid.across(b1[0], 1), grid.across(b1[2], 2))
        input_grad = input_grad_of(tokens, gain_a, after(grad_hidden, b1[0]), (back_a, back_b), (wa, wb))
        a3 = fold_second(grid, place, a2[1], after(ra2[0], input_grad), a2[3], ra2[1])
        ra3 = [grid.along_z(a3[s], s) for s in range(1, grid.planes)]
        b2 = fold_first(grid, place, b1[1], after(rb1[0], a3[0]), b1[3], rb1[1])
        rb2 = (grid.across(b2[0], 2), grid.across(b2[2], 1))
        act = after(act, b2[0])
        out_f = (hidden1 + nn(act, w_down) + bias_down).astype(bf16)
        a4 = fold_planes(grid, a3[0], *after(ra3, out_f))
        a5 = [a4] + [grid.across(a4, code) for code in (1, 2, 3)]
        b3 = fold_second(grid, place, b2[1], after(rb2[0], a4, summed), b2[3], rb2[1])
        rb3 = [grid.along_z(b3[s], s) for s in range(1, grid.planes)]
        b4 = fold_planes(grid, b3[0], *rb3)
        b5 = [b4] + [grid.across(b4, code) for code in (1, 2, 3)]
        g_q, g_k, g_v, tail = finish(grid, place, [a5, b5])
        g_up, g_o, g_down = (summed[:, i * D : (i + 1) * D] for i in range(3))
        g_up_bias, g_down_bias = tail[0, : grid.rows], tail[1, : grid.rows]
        scale_grad = tail[0, HALF : HALF + HD]
    else:
        out_f = (hidden1 + nn(act, w_down) + bias_down).astype(bf16)
        input_grad = input_grad_of(tokens, gain_a, grad_hidden, (back_a, back_b), (wa, wb))
        joined = [
            jnp.concatenate([g[:, w * HALF : (w + 1) * HALF] for g in (back_a, back_b)], axis=1) for w in range(3)
        ]
        g_o, g_up, g_down, g_q, g_k, g_v, g_up_bias, g_down_bias = (
            lax.psum(g.astype(f32), "replica")
            for g in (
                part_both[:, D:],
                part_both[:, :D],
                part_down,
                *[scattered(tn(attn_in, g).astype(bf16)) for g in joined],
                scattered(up_bias_grad),
                scattered(down_bias_grad),
            )
        )
        scale_grad = lax.psum(scale_part, ("replica", "fsdp"))

    def weighed(*pairs):
        return sum(jnp.sum(w.astype(f32) * g, axis=1) for w, g in pairs)

    g_attn_gain = weighed((query_weight, g_q), (key_weight, g_k), (value_weight, g_v)) / attn_gain.astype(f32)
    g_mlp_gain = weighed((up_weight, g_up)) / mlp_gain.astype(f32)
    sums = (g_q, g_k, g_v, g_o, g_up, g_down, g_attn_gain, g_mlp_gain, g_up_bias, g_down_bias)
    return (out_f, input_grad, *sums, scale_grad)


def solution(mesh):
    split = P(("replica", "fsdp"), None)
    rows = P("fsdp", None)
    part = P("fsdp")
    return jax.shard_map(
        functools.partial(shards, Grid(mesh.shape)),
        mesh=mesh,
        in_specs=(split, P(("replica", "fsdp")), split, *[rows] * 6, *[part] * 4, P()),
        out_specs=(split, split, *[rows] * 6, *[part] * 4, P()),
        check_vma=False,
    )
```

```python
import functools
import math

import jax
import jax.numpy as jnp
from jax import lax
from jax.experimental import pallas as pl
from jax.experimental.pallas import tpu as pltpu
from jax.sharding import PartitionSpec as P

D = 1280
HEADS = 16
HD = 80
FF = 1280
SEQ = 1024
EPS = 1e-06
LOG2E = math.log2(math.e)
NEG = -1e30
LANES = 128
BLOCK = 256
GROUP = 8
HALF = GROUP * HD
TRIPLE = 3 * HALF
VMEM_LIMIT = 58 << 20
SHORT = 40

bf16 = jnp.bfloat16
f32 = jnp.float32


def rms_parts(v):
    inverse = lax.rsqrt(jnp.mean(v * v, axis=-1, keepdims=True) + EPS)
    return (v * inverse, inverse)


def rms_back(grad_n, normed, inverse):
    return inverse * (grad_n - normed * jnp.mean(grad_n * normed, axis=-1, keepdims=True))


def nt(a, b):
    return lax.dot_general(a, b, (((1,), (1,)), ((), ())), preferred_element_type=f32)


def nn(a, b):
    return lax.dot_general(a, b, (((1,), (0,)), ((), ())), preferred_element_type=f32)


def tn(a, b):
    return lax.dot_general(a, b, (((0,), (0,)), ((), ())), preferred_element_type=f32)


def widen(v):
    return jnp.pad(v, ((0, 0), (0, LANES - HD)))


def split3(v):
    a = v.astype(bf16).astype(f32)
    b = (v - a).astype(bf16).astype(f32)
    c = (v - a - b).astype(bf16).astype(f32)
    return a, b, c


def extra_lanes(lane, base, extra):
    out = jnp.zeros_like(base)
    for place, value in reversed(list(enumerate(extra))):
        out = jnp.where(lane == HD + place, value, out)
    return jnp.where(lane < HD, base, out)


def forward_kernel(heads, len_ref, qkv_ref, o_ref, qa_ref, ka_ref, va_ref):
    length = len_ref[0]
    lane = lax.broadcasted_iota(jnp.int32, (SEQ, LANES), 1)
    row = lax.broadcasted_iota(jnp.int32, (SEQ, LANES), 0)
    mask = jnp.where(row < length, 0.0, NEG)
    k_pad = jnp.where(lane == HD, mask, jnp.where((lane > HD) & (lane < HD + 4), 1.0, 0.0)).astype(bf16)
    v_pad = jnp.where((lane >= HD) & (lane < HD + 3), 1.0, 0.0).astype(bf16)
    q_pad = jnp.where(lane == HD, 1.0, 0.0).astype(bf16)
    in_head = lane < HD
    block_lane = lane[:BLOCK]
    block_row = lax.broadcasted_iota(jnp.int32, (LANES, BLOCK), 0)
    causal = lax.broadcasted_iota(jnp.int32, (BLOCK, BLOCK), 0) <= lax.broadcasted_iota(
        jnp.int32, (BLOCK, BLOCK), 1
    )
    blocks = SEQ // BLOCK

    def prepare(h):
        for n, (ref, pad) in enumerate(((qa_ref, q_pad), (ka_ref, k_pad), (va_ref, v_pad))):
            at = n * HALF + h * HD
            ref[h] = jnp.where(in_head, widen(qkv_ref[:, at : at + HD]), pad)

    def scores(h, i):
        return nt(ka_ref[h, : (i + 1) * BLOCK, :], qa_ref[h, i * BLOCK : (i + 1) * BLOCK, :])

    def attend(h, i, st):
        before = i * BLOCK
        diagonal = jnp.where(causal, st[before:], NEG)
        top = jnp.max(diagonal, axis=0, keepdims=True)
        if i:
            top = jnp.maximum(top, jnp.max(st[:before], axis=0, keepdims=True))
        p = jnp.exp2(diagonal - top).astype(bf16)
        if i:
            p = jnp.concatenate([jnp.exp2(st[:before] - top).astype(bf16), p], axis=0)
        return tn(va_ref[h, : before + BLOCK, :], p), top

    def finish(h, i, ot, top):
        rows = slice(i * BLOCK, (i + 1) * BLOCK)
        total = ot[HD : HD + 1]
        a, b, c = split3(-(top + jnp.log2(total)))
        scaled = jnp.where(block_row < HD, ot / total, 0.0)
        for place, value in ((1, a), (2, b), (3, c)):
            scaled = jnp.where(block_row == HD + place, value, scaled)
        o = scaled.T
        o_ref[rows, h * HD : (h + 1) * HD] = o[:, :HD].astype(bf16)
        qa_ref[h, rows, :] = jnp.where(block_lane <= HD, qa_ref[h, rows, :].astype(f32), o).astype(bf16)

    for h in range(heads):
        prepare(h)
    scored, done = [], []
    for h, i in [(h, i) for h in range(heads) for i in range(blocks)] + [(None, None)] * 2:
        if h is not None:
            scored.append((h, i, scores(h, i)))
        if len(scored) > 1 or (h is None and scored):
            hh, ii, st = scored.pop(0)
            done.append((hh, ii, *attend(hh, ii, st)))
        if len(done) > 1 or (h is None and not scored and done):
            finish(*done.pop(0))
    while done:
        finish(*done.pop(0))


def attend_forward(half, lengths, qkv, before=None):
    wide = pl.BlockSpec((GROUP, SEQ, LANES), lambda g: (0, 0, 0))
    kept = [] if before is None else [before]

    def kernel(len_ref, qkv_ref, *refs):
        forward_kernel(GROUP, len_ref, qkv_ref, *refs[len(kept) :])

    return pl.pallas_call(
        kernel,
        grid=(1,),
        in_specs=[pl.BlockSpec(memory_space=pltpu.SMEM), pl.BlockSpec((SEQ, TRIPLE), lambda g: (0, 0))]
        + [pl.BlockSpec(memory_space=pl.ANY)] * len(kept),
        out_specs=[pl.BlockSpec((SEQ, HALF), lambda g: (0, half)), wide, wide, wide],
        out_shape=[jax.ShapeDtypeStruct((SEQ, D), bf16)]
        + [jax.ShapeDtypeStruct((GROUP, SEQ, LANES), bf16)] * 3,
        input_output_aliases={2: 0} if kept else {},
        compiler_params=pltpu.CompilerParams(vmem_limit_bytes=VMEM_LIMIT),
        cost_estimate=pl.CostEstimate(
            flops=GROUP * SEQ * SEQ * 1200 // SHORT, bytes_accessed=0, transcendentals=0
        ),
        name="attend_forward",
    )(lengths, qkv, *kept)


def backward_kernel(
    heads, fac_ref, qa_ref, ka_ref, va_ref, o_ref, g_ref, d_ref, sg_ref, dqs, gs
):
    lane = lax.broadcasted_iota(jnp.int32, (SEQ, LANES), 1)
    causal = lax.broadcasted_iota(jnp.int32, (BLOCK, BLOCK), 0) <= lax.broadcasted_iota(
        jnp.int32, (BLOCK, BLOCK), 1
    )
    fac = fac_ref[0:1, :]
    blocks = SEQ // BLOCK

    @pl.when(pl.program_id(0) == 0)
    def _():
        sg_ref[...] = jnp.zeros_like(sg_ref)

    sums = []

    def prepare(h):
        own = slice(h * HD, (h + 1) * HD)
        g = widen(g_ref[:, own]).astype(f32)
        o = widen(o_ref[:, own]).astype(f32)
        delta = jnp.sum(g * o, axis=1, keepdims=True)
        gs[h] = extra_lanes(lane, g, split3(-delta)).astype(bf16)

    def products(h, j):
        js = slice(j * BLOCK, (j + 1) * BLOCK)
        return nt(ka_ref[h, js, :], qa_ref[h, j * BLOCK :, :]), nt(va_ref[h, js, :], gs[h, j * BLOCK :, :])

    def middle(j, st, dpt):
        p = jnp.exp2(st)
        diagonal = jnp.where(causal, p[:, :BLOCK], 0.0)
        p = jnp.concatenate([diagonal, p[:, BLOCK:]], axis=1) if j < blocks - 1 else diagonal
        return (p * dpt).astype(bf16), p.astype(bf16)

    def finish(h, j, ds, p):
        own, dk, dv = (slice(n * HALF + h * HD, n * HALF + (h + 1) * HD) for n in range(3))
        js = slice(j * BLOCK, (j + 1) * BLOCK)
        d_ref[js, dv] = nn(p, gs[h, j * BLOCK :, :])[:, :HD].astype(bf16)
        d_ref[js, dk] = (nn(ds, qa_ref[h, j * BLOCK :, :])[:, :HD] * (1.0 / LOG2E)).astype(bf16)
        dqt = tn(ka_ref[h, js, :], ds)
        if j == 0:
            dqs[h % 2] = dqt
        else:
            dqs[h % 2, :, j * BLOCK :] += dqt
        if j == blocks - 1:
            dq = dqs[h % 2].T.astype(bf16).astype(f32)
            sums.append(jnp.sum(dq * qa_ref[h].astype(f32), axis=0, keepdims=True))
            d_ref[:, own] = (dq * fac)[:, :HD].astype(bf16)

    for h in range(heads):
        prepare(h)
    waiting = []
    for h, j in [(h, j) for h in range(heads) for j in range(blocks)]:
        waiting.append((h, j, *products(h, j)))
        if len(waiting) > 1:
            hh, jj, st, dpt = waiting.pop(0)
            finish(hh, jj, *middle(jj, st, dpt))
    hh, jj, st, dpt = waiting.pop(0)
    finish(hh, jj, *middle(jj, st, dpt))
    sg_ref[0:1, :] += sum(sums)


def attend_backward(half, fac, qa, ka, va, o, g):
    part = pl.BlockSpec((SEQ, HALF), lambda g: (0, half))
    wide = pl.BlockSpec((GROUP, SEQ, LANES), lambda g: (0, 0, 0))
    full = pl.BlockSpec((8, LANES), lambda g: (0, 0))
    return pl.pallas_call(
        functools.partial(backward_kernel, GROUP),
        grid=(1,),
        in_specs=[full, wide, wide, wide, part, part],
        out_specs=[pl.BlockSpec((SEQ, TRIPLE), lambda g: (0, 0)), full],
        out_shape=[jax.ShapeDtypeStruct((SEQ, TRIPLE), bf16), jax.ShapeDtypeStruct((8, LANES), f32)],
        scratch_shapes=[pltpu.VMEM((2, LANES, SEQ), f32), pltpu.VMEM((GROUP, SEQ, LANES), bf16)],
        compiler_params=pltpu.CompilerParams(vmem_limit_bytes=VMEM_LIMIT),
        cost_estimate=pl.CostEstimate(
            flops=GROUP * SEQ * SEQ * 2400 // SHORT, bytes_accessed=0, transcendentals=0
        ),
        name="attend_backward",
    )(fac, qa, ka, va, o, g)


class Grid:
    def __init__(self, mesh_shape):
        self.copies, self.owners = mesh_shape["replica"], mesh_shape["fsdp"]
        self.planes = self.owners // 2
        self.rows = D // self.owners

    @property
    def pieced(self):
        return self.copies == 4 and self.owners == 8

    def place(self):
        me, copy = lax.axis_index("fsdp"), lax.axis_index("replica")
        return copy // 2, copy % 2, me // 2, me % 2

    def along_z(self, v, step):
        n = self.planes
        pairs = [(i, (i // 2 + step) % n * 2 + i % 2) for i in range(self.owners)]
        return lax.ppermute(v, "fsdp", pairs)

    def other_core(self, v):
        return lax.ppermute(v, "fsdp", [(i, i ^ 1) for i in range(self.owners)])

    def across(self, v, code):
        return lax.ppermute(v, "replica", [(i, i ^ code) for i in range(self.copies)])


def kernel_call(kernel, name, operands, outs, scratch=(), flops=0, nbytes=0, **more):
    return pl.pallas_call(
        kernel,
        out_shape=outs,
        scratch_shapes=scratch,
        compiler_params=pltpu.CompilerParams(vmem_limit_bytes=VMEM_LIMIT),
        cost_estimate=pl.CostEstimate(flops=flops // SHORT, bytes_accessed=nbytes // SHORT, transcendentals=0),
        name=name,
        **more,
    )(*operands)


def piece_copies(planes, quarter, place_ref, refs, buf, sem):
    y, x, z, core = (place_ref[i] for i in range(4))
    groups = []
    for s, (source, c) in enumerate(((refs[:5], core), (refs[5:10], 1 - core))):
        block, *pieces = source
        home = 2 * z + c
        groups.append((home, [pltpu.make_async_copy(block, buf.at[home], sem.at[s, 0, 0])]))
        for d in range(1, planes):
            owner = 2 * lax.rem(z - d + planes, planes) + c
            copies = []
            for code, piece in enumerate(pieces):
                py = 1 - y if code >= 2 else y
                px = 1 - x if code % 2 else x
                at = pl.multiple_of((2 * py + px) * quarter, 16)
                copies.append(
                    pltpu.make_async_copy(piece.at[d - 1], buf.at[owner, pl.ds(at, quarter), :], sem.at[s, d, code])
                )
            groups.append((owner, copies))
    return groups


def project_kernel(planes, rows, quarter, first, place_ref, scale_ref, x_ref, *refs):
    outs, scratch = refs[10 : 10 + (5 if first else 2)], refs[10 + (5 if first else 2) :]
    qkv_ref, whole_ref = outs[:2]
    buf, sem_in, sem_out = scratch[:3]
    groups = piece_copies(planes, quarter, place_ref, refs, buf, sem_in)
    for _, copies in groups:
        for copy in copies:
            copy.start()
    if first:
        held = scratch[3]
        for at in range(0, SEQ, BLOCK):
            held[at : at + BLOCK, :] = rms_parts(x_ref[at : at + BLOCK, :].astype(f32))[0]
    written = []
    for g, (owner, copies) in enumerate(groups):
        for copy in copies:
            copy.wait()
        at = pl.multiple_of(owner * rows, 16)
        for t in range(3):
            copy = pltpu.make_async_copy(
                buf.at[owner, pl.ds(t * rows, rows), :],
                whole_ref.at[pl.ds(at, rows), pl.ds(t * HALF, HALF)],
                sem_out.at[g, t],
            )
            copy.start()
            written.append(copy)
    if first:
        vec_ref, attn_in, left_ref = outs[2:5]
        vec_ref[...] = buf[:, 3 * rows : 3 * rows + 16, :]
        gain = jnp.concatenate([buf[b, 3 * rows : 3 * rows + 16, :rows][0:1] for b in range(2 * planes)], axis=1)
        gain = gain.astype(f32)
        for at in range(0, SEQ, BLOCK):
            attn_in[at : at + BLOCK, :] = (held[at : at + BLOCK, :] * gain).astype(bf16)
    else:
        attn_in = x_ref
    for t in range(3):
        weight = buf[:, t * rows : (t + 1) * rows, :].reshape(D, HALF)
        result = nn(attn_in[...], weight)
        qkv_ref[:, t * HALF : (t + 1) * HALF] = (result * scale_ref[0:1, :] if t == 0 else result).astype(bf16)
    if first:
        left_ref[...] = attn_in[...].T
    for copy in written:
        copy.wait()


def project(grid, place, scale, x, pieces, first):
    total = pieces[0].shape[0]
    vmem, hbm = pl.BlockSpec(memory_space=pltpu.VMEM), pl.BlockSpec(memory_space=pl.ANY)
    outs = [jax.ShapeDtypeStruct((SEQ, TRIPLE), bf16), jax.ShapeDtypeStruct((D, TRIPLE), bf16)]
    scratch = [
        pltpu.VMEM((grid.owners, total, HALF), bf16),
        pltpu.SemaphoreType.DMA((2, grid.planes, 4)),
        pltpu.SemaphoreType.DMA((grid.owners, 3)),
    ]
    if first:
        outs += [
            jax.ShapeDtypeStruct((grid.owners, 16, HALF), bf16),
            jax.ShapeDtypeStruct((SEQ, D), bf16),
            jax.ShapeDtypeStruct((D, SEQ), bf16),
        ]
        scratch.append(pltpu.VMEM((SEQ, D), f32))
    return kernel_call(
        functools.partial(project_kernel, grid.planes, grid.rows, total // 4, first),
        "project",
        (place, scale, x, *pieces),
        outs,
        scratch=scratch,
        flops=2 * SEQ * D * TRIPLE,
        nbytes=4 * D * TRIPLE + 2 * SEQ * (D + TRIPLE),
        in_specs=[pl.BlockSpec(memory_space=pltpu.SMEM), vmem, vmem] + [hbm] * 10,
        out_specs=[vmem, hbm] + [vmem] * 3 * first,
    )


def cut_kernel(rows, place_ref, *refs):
    weights, vec_ref = refs[:6], refs[6]
    chunks, pieces = refs[7:10], refs[10:13]
    for half in range(2):
        for t in range(3):
            chunks[half][t * rows : (t + 1) * rows, :] = weights[t][:, half * HALF : (half + 1) * HALF]
        chunks[half][3 * rows :, :] = vec_ref[...]
    for t in range(6):
        w, half = 3 + t // 2, t % 2
        chunks[2][t * rows : (t + 1) * rows, :] = weights[w][:, half * HALF : (half + 1) * HALF]
    copy = 2 * place_ref[0] + place_ref[1]
    for chunk, piece in zip(chunks, pieces, strict=True):
        quarter = piece.shape[0]
        piece[...] = chunk[pl.ds(pl.multiple_of(copy * quarter, 16), quarter), :]


def cut(grid, place, weights, vectors):
    rows = [512, 512, 6 * grid.rows]
    vec = jnp.pad(vectors.reshape(1, HALF), ((0, 512 - 3 * grid.rows - 1), (0, 0)))
    out = kernel_call(
        functools.partial(cut_kernel, grid.rows),
        "cut",
        (place, *weights, vec),
        [jax.ShapeDtypeStruct((n, HALF), bf16) for n in rows]
        + [jax.ShapeDtypeStruct((n // 4, HALF), bf16) for n in rows],
        nbytes=12 * grid.rows * D * 2,
        in_specs=[pl.BlockSpec(memory_space=pltpu.SMEM)] + [pl.BlockSpec(memory_space=pltpu.VMEM)] * 7,
    )
    return out[:3], out[3:]


def chunk_across(grid, along):
    return [along] + [grid.across(along, code) for code in (1, 2, 3)]


def both_cores(grid, own):
    return own + [grid.other_core(v) for v in own]


def in_blocks():
    return [slice(at, at + BLOCK) for at in range(0, SEQ, BLOCK)]


def mlp_forward_kernel(planes, rows, quarter, place_ref, gain_ref, bias_ref, *refs):
    attended_ref, token_ref, grad_ref = refs[10:13]
    weights, (hidden_ref, mlp_in_ref, pre_ref, act_ref, down_grad_ref) = refs[13:16], refs[16:21]
    buf, attended, token, grad, hidden, mlp_in, pre, act, down_grad, sem_in, sem_out, sem = refs[21:]
    loads = [
        pltpu.make_async_copy(source, target, sem.at[n])
        for n, (source, target) in enumerate(((attended_ref, attended), (token_ref, token), (grad_ref, grad)))
    ]
    groups = piece_copies(planes, quarter, place_ref, refs, buf, sem_in)
    for _, copies in groups:
        for copy in copies:
            copy.start()
    for load in loads:
        load.start()
    written = []

    def keep(source, target, n):
        copy = pltpu.make_async_copy(source, target, sem.at[n])
        copy.start()
        written.append(copy)

    for g, (owner, copies) in enumerate(groups):
        for copy in copies:
            copy.wait()
        at = pl.multiple_of(owner * rows, 16)
        for t in range(6):
            copy = pltpu.make_async_copy(
                buf.at[owner, pl.ds(t * rows, rows), :],
                weights[t // 2].at[pl.ds(at, rows), pl.ds(t % 2 * HALF, HALF)],
                sem_out.at[g, t],
            )
            copy.start()
            written.append(copy)
    for load in loads[:2]:
        load.wait()

    def tile(t):
        return buf[:, t * rows : (t + 1) * rows, :].reshape(D, HALF)

    halves = (slice(0, HALF), slice(HALF, D))
    for h, across in enumerate(halves):
        hidden[:, across] = token[:, across].astype(f32) + nn(attended[...], tile(h))
    keep(hidden, hidden_ref, 3)
    for at in in_blocks():
        mlp_in[at, :] = (rms_parts(hidden[at, :])[0] * gain_ref[0:1, :]).astype(bf16)
    keep(mlp_in, mlp_in_ref, 4)
    for h, across in enumerate(halves):
        value = nn(mlp_in[...], tile(2 + h)) + bias_ref[0:1, across]
        pre[:, across] = value
        act[:, across] = (value * jax.nn.sigmoid(value)).astype(bf16)
    keep(pre, pre_ref, 5)
    keep(act, act_ref, 6)
    loads[2].wait()
    down_grad[...] = tn(act[...], grad[...]).astype(bf16)
    keep(down_grad, down_grad_ref, 7)
    for copy in written:
        copy.wait()


def mlp_forward(grid, place, gain, bias, pieces, attended, tokens, grad_out_low):
    total = pieces[0].shape[0]
    vmem, hbm = pl.BlockSpec(memory_space=pltpu.VMEM), pl.BlockSpec(memory_space=pl.ANY)
    low, high, square = ((SEQ, D), bf16), ((SEQ, D), f32), ((D, D), bf16)
    outs = [square] * 3 + [high, low, high, low, square]
    return kernel_call(
        functools.partial(mlp_forward_kernel, grid.planes, grid.rows, total // 4),
        "mlp_forward",
        (place, row_of(gain), row_of(bias), *pieces, attended, tokens, grad_out_low),
        [jax.ShapeDtypeStruct(*o) for o in outs],
        scratch=[
            pltpu.VMEM((grid.owners, total, HALF), bf16),
            *[pltpu.VMEM(*v) for v in (low, low, low, high, low, high, low, square)],
            pltpu.SemaphoreType.DMA((2, grid.planes, 4)),
            pltpu.SemaphoreType.DMA((grid.owners, 6)),
            pltpu.SemaphoreType.DMA((8,)),
        ],
        flops=6 * SEQ * D * D,
        nbytes=16 * D * D + 22 * SEQ * D,
        in_specs=[pl.BlockSpec(memory_space=pltpu.SMEM), vmem, vmem] + [hbm] * 13,
        out_specs=[hbm] * 8,
    )


def row_of(v):
    return jnp.broadcast_to(v[None], (8, v.shape[0]))


def mlp_backward_kernel(gain_ref, *refs):
    grad_ref, down_ref, pre_ref, mlp_in_ref, up_ref, hidden_ref, output_ref, attended_ref = refs[:8]
    up_grad_ref, grad_hidden_ref, grad_att_ref, output_grad_ref, sums_ref = refs[8:13]
    grad, down, wide, mlp_in, up, hidden, output, attended, grad_pre, grad_proj, first, second, sem = refs[13:]
    loads = {}
    for n, (name, source, target) in enumerate(
        (
            ("grad", grad_ref, grad),
            ("down", down_ref, down),
            *[(f"pre{at.start}", pre_ref.at[at, :], wide.at[at, :]) for at in in_blocks()],
            ("mlp_in", mlp_in_ref, mlp_in),
            ("up", up_ref, up),
            ("hidden", hidden_ref, hidden),
            ("output", output_ref, output),
            ("attended", attended_ref, attended),
        )
    ):
        loads[name] = pltpu.make_async_copy(source, target, sem.at[n])
        loads[name].start()
    written = []

    def keep(source, target):
        copy = pltpu.make_async_copy(source, target, sem.at[7 + SEQ // BLOCK + len(written)])
        copy.start()
        written.append(copy)

    for name in ("grad", "down"):
        loads[name].wait()
    sums = jnp.zeros((1, D), f32)
    for at in in_blocks():
        loads[f"pre{at.start}"].wait()
        pre = wide[at, :]
        sigma = jax.nn.sigmoid(pre)
        value = (nt(grad[at, :], down[...]) * (sigma * (1.0 + pre * (1.0 - sigma)))).astype(bf16)
        grad_pre[at, :] = value
        sums = sums + jnp.sum(value.astype(f32), axis=0, keepdims=True)
    sums_ref[...] = jnp.zeros_like(sums_ref)
    sums_ref[0:1, :] = sums
    sums_ref[1:2, :] = jnp.sum(grad[...].astype(f32), axis=0, keepdims=True)
    for name in ("mlp_in", "up", "hidden"):
        loads[name].wait()
    first[...] = tn(mlp_in[...], grad_pre[...]).astype(bf16)
    keep(first, up_grad_ref)
    for at in in_blocks():
        normed, inverse = rms_parts(hidden[at, :])
        back = rms_back(nt(grad_pre[at, :], up[...]) * gain_ref[0:1, :], normed, inverse)
        value = grad[at, :].astype(f32) + back
        wide[at, :] = value
        grad_proj[at, :] = value.astype(bf16)
    keep(wide, grad_hidden_ref)
    for name in ("output", "attended"):
        loads[name].wait()
    for at in in_blocks():
        mlp_in[at, :] = nt(grad_proj[at, :], output[...]).astype(bf16)
    keep(mlp_in, grad_att_ref)
    second[...] = tn(attended[...], grad_proj[...]).astype(bf16)
    keep(second, output_grad_ref)
    for copy in written:
        copy.wait()


def mlp_backward(gain, grad_out_low, w_down, pre, mlp_in, w_up, hidden1, w_out, attended):
    hbm = pl.BlockSpec(memory_space=pl.ANY)
    low, high, square = ((SEQ, D), bf16), ((SEQ, D), f32), ((D, D), bf16)
    up_grad, grad_hidden, grad_att, output_grad, sums = kernel_call(
        mlp_backward_kernel,
        "mlp_backward",
        (row_of(gain), grad_out_low, w_down, pre, mlp_in, w_up, hidden1, w_out, attended),
        [jax.ShapeDtypeStruct(*o) for o in (square, high, low, square, ((8, D), f32))],
        scratch=[
            *[pltpu.VMEM(*v) for v in (low, square, high, low, square, high, square, low, low, low, square, square)],
            pltpu.SemaphoreType.DMA((11 + SEQ // BLOCK,)),
        ],
        flops=10 * SEQ * D * D,
        nbytes=10 * D * D + 26 * SEQ * D,
        in_specs=[pl.BlockSpec(memory_space=pltpu.VMEM)] + [hbm] * 8,
        out_specs=[hbm] * 4 + [pl.BlockSpec(memory_space=pltpu.VMEM)],
    )
    return up_grad, output_grad, grad_hidden, grad_att, sums[0], sums[1]


def weight_grad_kernel(planes, rows, place_ref, left_ref, right_ref, vec_ref, mine, theirs, left, right, stage, sem_in, sem_out):
    core = place_ref[3]
    loads = [pltpu.make_async_copy(left_ref, left, sem_in.at[3])]
    for w in range(3):
        part = pl.ds(w * HALF, HALF)
        loads.append(pltpu.make_async_copy(right_ref.at[:, part], right.at[:, part], sem_in.at[w]))
    for load in loads:
        load.start()
    written = []

    def send(w, source, size, c, whole, z):
        copy = pltpu.make_async_copy(source, whole.at[z, pl.ds(w * rows, size), :], sem_out.at[w, c, z])
        copy.start()
        written.append(copy)

    sides = ((1, theirs), (0, mine))
    owner = {(c, z): 2 * z + (1 - core if c else core) for c in range(2) for z in range(planes)}
    for c, whole in sides:
        for z in range(planes):
            send(3, vec_ref.at[owner[c, z]], 32, c, whole, z)
    loads[0].wait()
    for w in range(3):
        loads[1 + w].wait()
        stage[w] = nn(left[...], right[:, w * HALF : (w + 1) * HALF]).astype(bf16)
        for c, whole in sides:
            for z in range(planes):
                at = pl.multiple_of(owner[c, z] * rows, 16)
                send(w, stage.at[w, pl.ds(at, rows), :], rows, c, whole, z)
    for copy in written:
        copy.wait()


def weight_grads(grid, place, left, right, vectors):
    rows = jnp.stack(vectors, axis=1).astype(bf16)
    rows = jnp.pad(rows, ((0, 0), (0, 32 - len(vectors)), (0, HALF - grid.rows)))
    shape = jax.ShapeDtypeStruct((grid.planes, 512, HALF), bf16)
    hbm = pl.BlockSpec(memory_space=pl.ANY)
    return kernel_call(
        functools.partial(weight_grad_kernel, grid.planes, grid.rows),
        "weight_grads",
        (place, left, right, rows),
        [shape, shape],
        scratch=[
            pltpu.VMEM((D, SEQ), bf16),
            pltpu.VMEM((SEQ, TRIPLE), bf16),
            pltpu.VMEM((3, D, HALF), bf16),
            pltpu.SemaphoreType.DMA((4,)),
            pltpu.SemaphoreType.DMA((4, 2, grid.planes)),
        ],
        flops=2 * SEQ * D * TRIPLE,
        nbytes=(SEQ * D + (SEQ + D) * TRIPLE) * 2,
        in_specs=[pl.BlockSpec(memory_space=pltpu.SMEM), hbm, hbm, pl.BlockSpec(memory_space=pltpu.VMEM)],
        out_specs=[hbm, hbm],
    )


def added(a, b):
    return (a.astype(f32) + b.astype(f32)).astype(bf16)


def fold_cores_kernel(place_ref, a_ref, b_ref, send_low, keep_low, send_high, keep_high):
    y, x = place_ref[0], place_ref[1]
    for p in range(2):
        send_low[0, p] = added(a_ref[0, p, 1 - x, 0], b_ref[0, p, 1 - x, 0])
        keep_low[0, p] = added(a_ref[0, p, x, 0], b_ref[0, p, x, 0])
        send_high[0, p] = added(a_ref[0, 1 - y, p, 1], b_ref[0, 1 - y, p, 1])
        keep_high[0, p] = added(a_ref[0, y, p, 1], b_ref[0, y, p, 1])


def fold_cores(grid, place, a, b):
    n, columns = grid.planes, a.shape[2]
    split = (n, 2, 2, 2, 64, columns)
    block = pl.BlockSpec((1, *split[1:]), lambda i: (i, 0, 0, 0, 0, 0))
    out = pl.BlockSpec((1, 2, 64, columns), lambda i: (i, 0, 0, 0))
    return kernel_call(
        fold_cores_kernel,
        "fold_cores",
        (place, a.reshape(split), b.reshape(split)),
        [jax.ShapeDtypeStruct((n, 2, 64, columns), bf16)] * 4,
        nbytes=a.size * 6,
        grid=(n,),
        in_specs=[pl.BlockSpec(memory_space=pltpu.SMEM), block, block],
        out_specs=[out] * 4,
    )


def fold_first_kernel(place_ref, low_a, low_b, high_a, high_b, send_low, keep_low, send_high, keep_high):
    y, x = place_ref[0], place_ref[1]
    send_low[0] = added(low_a[0, 1 - y], low_b[0, 1 - y])
    keep_low[0] = added(low_a[0, y], low_b[0, y])
    send_high[0] = added(high_a[0, 1 - x], high_b[0, 1 - x])
    keep_high[0] = added(high_a[0, x], high_b[0, x])


def fold_first(grid, place, *parts):
    n, columns = grid.planes, parts[0].shape[3]
    block = pl.BlockSpec((1, 2, 64, columns), lambda i: (i, 0, 0, 0))
    out = pl.BlockSpec((1, 64, columns), lambda i: (i, 0, 0))
    return kernel_call(
        fold_first_kernel,
        "fold_first",
        (place, *parts),
        [jax.ShapeDtypeStruct((n, 64, columns), bf16)] * 4,
        nbytes=parts[0].size * 12,
        grid=(n,),
        in_specs=[pl.BlockSpec(memory_space=pltpu.SMEM)] + [block] * 4,
        out_specs=[out] * 4,
    )


def fold_second_kernel(planes, place_ref, low_a, low_b, high_a, high_b, *outs):
    z = place_ref[2]
    for s in range(planes):
        at = lax.rem(z + s, planes)
        outs[s][0] = added(low_a[at], low_b[at])
        outs[s][1] = added(high_a[at], high_b[at])


def fold_second(grid, place, *parts):
    n, columns = grid.planes, parts[0].shape[2]
    return kernel_call(
        functools.partial(fold_second_kernel, n),
        "fold_second",
        (place, *parts),
        [jax.ShapeDtypeStruct((2, 64, columns), bf16)] * n,
        nbytes=parts[0].size * 12,
        in_specs=[pl.BlockSpec(memory_space=pltpu.SMEM)] + [pl.BlockSpec(memory_space=pltpu.VMEM)] * 4,
    )


def fold_planes_kernel(*refs):
    *parts, out = refs
    total = parts[0][...].astype(f32)
    for part in parts[1:]:
        total = total + part[...].astype(f32)
    out[...] = total.astype(bf16)


def fold_planes(grid, *parts):
    return kernel_call(
        fold_planes_kernel,
        "fold_planes",
        parts,
        jax.ShapeDtypeStruct(parts[0].shape, bf16),
        nbytes=parts[0].size * 10,
    )


def finish_kernel(units, rows, place_ref, *refs):
    me = 2 * place_ref[0] + place_ref[1]
    parts, outs, stage = refs[: 4 * units], refs[4 * units : -1], refs[-1]
    columns = parts[0].shape[2]
    for u in range(units):
        across = slice(u * columns, (u + 1) * columns)
        for r in range(4):
            for code in range(4):

                @pl.when(me == r ^ code)
                def _(r=r, code=code, u=u, across=across):
                    for h in range(2):
                        at = 128 * r + 64 * h
                        stage[at : at + 64, across] = parts[4 * u + code][h].astype(f32)

    for w in range(3):
        outs[w][...] = stage[w * rows : (w + 1) * rows, :]
    outs[3][...] = stage[3 * rows :, :]


def finish(grid, place, units):
    columns = units[0][0].shape[2] * len(units)
    parts = [part for unit in units for part in unit]
    return kernel_call(
        functools.partial(finish_kernel, len(units), grid.rows),
        "finish",
        (place, *parts),
        [jax.ShapeDtypeStruct((grid.rows, columns), f32)] * 3
        + [jax.ShapeDtypeStruct((512 - 3 * grid.rows, columns), f32)],
        scratch=[pltpu.VMEM((512, columns), f32)],
        nbytes=512 * columns * 6,
        in_specs=[pl.BlockSpec(memory_space=pltpu.SMEM)]
        + [pl.BlockSpec(memory_space=pltpu.VMEM)] * len(parts),
    )


def input_grad_kernel(x_ref, gain_ref, hidden_ref, grad_a, grad_b, weight_a, weight_b, out):
    total = nt(grad_a[...], weight_a[...]) + nt(grad_b[...], weight_b[...])
    normed, inverse = rms_parts(x_ref[...].astype(f32))
    out[...] = (hidden_ref[...] + rms_back(total * gain_ref[0:1, :], normed, inverse)).astype(bf16)


def input_grad_of(tokens, gain, grad_hidden, grads, weights):
    count, block = tokens.shape[0], BLOCK
    rows = pl.BlockSpec((block, D), lambda i: (i, 0))
    return kernel_call(
        input_grad_kernel,
        "input_grad",
        (tokens, jnp.broadcast_to(gain[None], (8, D)), grad_hidden, *grads, *weights),
        jax.ShapeDtypeStruct((count, D), bf16),
        flops=6 * count * D * D,
        nbytes=6 * D * D + 14 * count * D,
        grid=(count // block,),
        in_specs=[rows, pl.BlockSpec((8, D), lambda i: (0, 0)), rows]
        + [pl.BlockSpec((block, TRIPLE), lambda i: (i, 0))] * 2
        + [pl.BlockSpec((D, TRIPLE), lambda i: (0, 0))] * 2,
        out_specs=rows,
    )


def after(value, *first):
    return lax.optimization_barrier((value, first))[0]


def shards(
    grid,
    tokens,
    lengths,
    cotangent,
    query_weight,
    key_weight,
    value_weight,
    output_weight,
    up_weight,
    down_weight,
    attn_gain,
    mlp_gain,
    up_bias,
    down_bias,
    query_scale,
):
    assert lengths.shape[0] == 1 and tokens.shape[0] == SEQ
    vectors = jnp.concatenate([attn_gain, mlp_gain, up_bias, down_bias])
    y, x, z, core = grid.place()
    place = jnp.stack([y, x, z, core]).astype(jnp.int32)
    xin = tokens.astype(f32)
    factor = query_scale.astype(f32) * (1.0 / jnp.sqrt(f32(HD)))
    scale_half = row_of(jnp.tile(factor * LOG2E, GROUP))
    valid = (jnp.arange(SEQ, dtype=jnp.int32) < lengths[0]).reshape(-1, 1)
    grad_out_low = jnp.where(valid, cotangent, jnp.zeros_like(cotangent))
    if grid.pieced:
        weights = (query_weight, key_weight, value_weight, output_weight, up_weight, down_weight)
        chunks, cuts = cut(grid, place, weights, vectors)
        planes = range(1, grid.planes)
        z1 = [grid.along_z(cuts[0], d) for d in planes]
        z2 = [grid.along_z(after(cuts[1], *z1), d) for d in planes]
        across1 = chunk_across(grid, jnp.stack(z1))
        across2 = chunk_across(grid, jnp.stack(after(z2, *z1)))
        z3 = [grid.along_z(after(cuts[2], *z2), d) for d in planes]
        qkv_a, wa, vecs, attn_in, left = project(
            grid, place, scale_half, tokens, both_cores(grid, [chunks[0], *across1]), True
        )
        vecs = vecs[:, 0].reshape(grid.owners, 4, grid.rows)
        qkv_a, z3 = after((qkv_a, z3), wa)
        attended, *kept_a = attend_forward(0, lengths, qkv_a)
        across3 = chunk_across(grid, jnp.stack(z3))
        pieces2 = both_cores(grid, [chunks[1], *after(across2, qkv_a)])
        qkv_b, wb = project(grid, place, scale_half, after(attn_in, attended), pieces2, False)
        attended, *kept_b = attend_forward(1, lengths, qkv_b, attended)
        pieces3 = both_cores(grid, [chunks[2], *after(across3, attended)])
        gain_m, bias_up = (vecs[:, i].reshape(D).astype(f32) for i in (1, 2))
        wo, w_up, w_down, hidden1, mlp_in, pre, act, down_grad = mlp_forward(
            grid, place, gain_m, bias_up, pieces3, attended, tokens, grad_out_low
        )
    else:
        wq, wk, wv, wo, w_up, w_down = (
            lax.all_gather(w, "fsdp", axis=0, tiled=True)
            for w in (query_weight, key_weight, value_weight, output_weight, up_weight, down_weight)
        )
        wa = jnp.concatenate([w[:, :HALF] for w in (wq, wk, wv)], axis=1)
        wb = jnp.concatenate([w[:, HALF:] for w in (wq, wk, wv)], axis=1)
        vecs = lax.all_gather(vectors, "fsdp", axis=0).reshape(grid.owners, 4, grid.rows)
        attn_in = (rms_parts(xin)[0] * vecs[:, 0].reshape(D).astype(f32)).astype(bf16)
        left = attn_in.T
        scale_row = jnp.concatenate([scale_half[0], jnp.ones((2 * HALF,), f32)])
        attended, *kept_a = attend_forward(0, lengths, (nn(attn_in, wa) * scale_row).astype(bf16))
        attended, *kept_b = attend_forward(1, lengths, (nn(attn_in, wb) * scale_row).astype(bf16), attended)
        gain_m, bias_up = (vecs[:, i].reshape(D).astype(f32) for i in (1, 2))
        hidden1 = xin + nn(attended, wo)
        mlp_in = (rms_parts(hidden1)[0] * gain_m).astype(bf16)
        pre = nn(mlp_in, w_up) + bias_up
        act = (pre * jax.nn.sigmoid(pre)).astype(bf16)
        down_grad = tn(act, grad_out_low).astype(bf16)
    kept = (kept_a, kept_b)
    gain_a, bias_down = (vecs[:, i].reshape(D).astype(f32) for i in (0, 3))

    fac_row = jnp.broadcast_to(jnp.pad(factor, (0, LANES - HD))[None], (8, LANES))
    owned = (grid.owners, grid.rows)

    def scattered(grad):
        return lax.psum_scatter(grad, "fsdp", scatter_dimension=0, tiled=True)

    part_down = scattered(down_grad)
    up_grad, output_grad, grad_hidden, grad_att, up_bias_grad, down_bias_grad = mlp_backward(
        gain_m, grad_out_low, w_down, pre, mlp_in, w_up, hidden1, wo, attended
    )
    part_up, part_o = scattered(up_grad), scattered(output_grad)

    back_a, scale_a = attend_backward(0, fac_row, *kept[0], attended, grad_att)
    if grid.pieced:
        mine_a, theirs_a = weight_grads(
            grid, place, left, back_a, [up_bias_grad.reshape(owned), down_bias_grad.reshape(owned)]
        )
        recv_a = grid.other_core(theirs_a)
        a1 = fold_cores(grid, place, mine_a, recv_a)
        ra1 = (grid.across(a1[0], 1), grid.across(a1[2], 2))
        grad_att = after(grad_att, a1[0])
    back_b, scale_b = attend_backward(1, fac_row, *kept[1], attended, grad_att)
    scale_part = (scale_a + scale_b)[0, :HD] / (query_scale.astype(f32) * LOG2E)

    if grid.pieced:
        scale_rows = jnp.broadcast_to(jnp.pad(scale_part, (0, grid.rows - HD))[None], owned)
        mine_b, theirs_b = weight_grads(grid, place, left, after(back_b, *ra1), [scale_rows])
        recv_b = grid.other_core(theirs_b)
        a2 = fold_first(grid, place, a1[1], after(ra1[0], mine_b), a1[3], ra1[1])
        ra2 = (grid.across(a2[0], 2), grid.across(a2[2], 1))
        b1 = fold_cores(grid, place, mine_b, after(recv_b, a2[0]))
        rb1 = (grid.across(b1[0], 1), grid.across(b1[2], 2))
        late = jnp.concatenate(after([part_o, part_up, part_down], b1[0]))
        summed = lax.psum(late, "replica").astype(f32)
        input_grad = input_grad_of(tokens, gain_a, after(grad_hidden, b1[0], late), (back_a, back_b), (wa, wb))
        a3 = fold_second(grid, place, a2[1], after(ra2[0], input_grad), a2[3], ra2[1])
        ra3 = [grid.along_z(a3[s], s) for s in range(1, grid.planes)]
        b2 = fold_first(grid, place, b1[1], after(rb1[0], a3[0]), b1[3], rb1[1])
        rb2 = (grid.across(b2[0], 2), grid.across(b2[2], 1))
        act = after(act, b2[0])
        out_f = (hidden1 + nn(act, w_down) + bias_down).astype(bf16)
        a4 = fold_planes(grid, a3[0], *after(ra3, out_f))
        a5 = [a4] + [grid.across(a4, code) for code in (1, 2, 3)]
        b3 = fold_second(grid, place, b2[1], after(rb2[0], a4), b2[3], rb2[1])
        rb3 = [grid.along_z(b3[s], s) for s in range(1, grid.planes)]
        b4 = fold_planes(grid, b3[0], *after(rb3, summed))
        b5 = [b4] + [grid.across(b4, code) for code in (1, 2, 3)]
        g_q, g_k, g_v, tail = finish(grid, place, [a5, b5])
        g_o, g_up, g_down = (summed[i * grid.rows : (i + 1) * grid.rows] for i in range(3))
        g_up_bias, g_down_bias = tail[0, : grid.rows], tail[1, : grid.rows]
        scale_grad = tail[0, HALF : HALF + HD]
    else:
        out_f = (hidden1 + nn(act, w_down) + bias_down).astype(bf16)
        input_grad = input_grad_of(tokens, gain_a, grad_hidden, (back_a, back_b), (wa, wb))
        joined = [
            jnp.concatenate([g[:, w * HALF : (w + 1) * HALF] for g in (back_a, back_b)], axis=1) for w in range(3)
        ]
        g_o, g_up, g_down, g_q, g_k, g_v, g_up_bias, g_down_bias = (
            lax.psum(g.astype(f32), "replica")
            for g in (
                part_o,
                part_up,
                part_down,
                *[scattered(tn(attn_in, g).astype(bf16)) for g in joined],
                scattered(up_bias_grad),
                scattered(down_bias_grad),
            )
        )
        scale_grad = lax.psum(scale_part, ("replica", "fsdp"))

    def weighed(*pairs):
        return sum(jnp.sum(w.astype(f32) * g, axis=1) for w, g in pairs)

    g_attn_gain = weighed((query_weight, g_q), (key_weight, g_k), (value_weight, g_v)) / attn_gain.astype(f32)
    g_mlp_gain = weighed((up_weight, g_up)) / mlp_gain.astype(f32)
    sums = (g_q, g_k, g_v, g_o, g_up, g_down, g_attn_gain, g_mlp_gain, g_up_bias, g_down_bias)
    return (out_f, input_grad, *sums, scale_grad)


def solution(mesh):
    split = P(("replica", "fsdp"), None)
    rows = P("fsdp", None)
    part = P("fsdp")
    return jax.shard_map(
        functools.partial(shards, Grid(mesh.shape)),
        mesh=mesh,
        in_specs=(split, P(("replica", "fsdp")), split, *[rows] * 6, *[part] * 4, P()),
        out_specs=(split, split, *[rows] * 6, *[part] * 4, P()),
        check_vma=False,
    )
```
